512 devices in a mesh: depth: 2 (over x_hi), row: 16 (over x_lo, y, core), col: 16 (over z).
Axes of the slice: x: 4 (x_hi: 2, x_lo: 2; x = x_hi * 2 + x_lo), y: 4, z: 16, core: 2. Of those that a mesh axis runs over, the one named last changes fastest.
Arguments:
- latents: bfloat16 [4096, 2432], P(('depth', 'row'), 'col'), may hold values from -6 to 6
- out_grad: bfloat16 [4096, 2432], P(('depth', 'row'), 'col'), may hold values from -2 to 2
- w_query: bfloat16 [2432, 2048], P('row', 'col'), may hold values from -0.10406108557514765 to 0.10406108557514765
- w_key: bfloat16 [2432, 2048], P('row', 'col'), may hold values from -0.10406108557514765 to 0.10406108557514765
- w_value: bfloat16 [2432, 2048], P('row', 'col'), may hold values from -0.125 to 0.125
- w_out: bfloat16 [2432, 2048], P('row', 'col'), may hold values from -1.6171875 to 1.6171875
- gain: bfloat16 [2432], P('col'), may hold values from 0.25 to 1.75
Outputs:
- latent_grad: bfloat16 [4096, 2432], P(('depth', 'row'), 'col')
The draws below stay inside these ranges and needn't reach their ends.
All inputs are finite; a program needn't handle non-finite values.
Results may differ from the reference program's by a relative error of at most 0.024.
Values may be sent and summed in bfloat16 or wider, within the bound.
A program may use at most 64 MiB of HBM per device.

```python
import math
import jax
import jax.numpy as jnp
from jax import lax

D = 2432
HEADS = 32
HDIM = 64
TOK_ROW = 128
SEQ = 2048
INNER = 2048
TOKENS = 4096
N_DEPTH = 2
N_ROW = 16
N_COL = 16


def projection_draw(key, own_key):
    base = jnp.clip(jax.random.normal(own_key, (D, INNER), jnp.float32), -5.0, 5.0) * D ** (-0.5)
    return base.astype(jnp.bfloat16)


def draw_w_query(key, part):
    own_key = jax.random.fold_in(key, 11)
    return projection_draw(key, own_key)


def draw_w_key(key, part):
    own_key = jax.random.fold_in(key, 12)
    return projection_draw(key, own_key)


def column_profile(ratio):
    position = jnp.arange(D, dtype=jnp.float32) / (D - 1.0)
    return jnp.exp(math.log(ratio) * (position - 0.5))[None, :]


def token_profile(ratio):
    position = jnp.arange(TOKENS, dtype=jnp.float32) / (TOKENS - 1.0)
    return jnp.exp(math.log(ratio) * (position - 0.5))[:, None]


def draw_latents(key, part):
    own_key = jax.random.fold_in(key, 13)
    values = jax.random.normal(own_key, (TOKENS, D), jnp.float32) * column_profile(3.0)
    return jnp.clip(values, -6.0, 6.0).astype(jnp.bfloat16)


def draw_out_grad(key, part):
    own_key = jax.random.fold_in(key, 14)
    values = jax.random.normal(own_key, (TOKENS, D), jnp.float32) * 0.25 * token_profile(3.0)
    return jnp.clip(values, -2.0, 2.0).astype(jnp.bfloat16)


def steps_of(key, dims, shards, low, high):
    loudness, own = 1.0, jax.random.fold_in(key, 6)
    for axis_at, blocks in shards:
        heights = jnp.exp(jax.random.uniform(jax.random.fold_in(own, axis_at), (blocks,), jnp.float32, low / len(shards), high / len(shards)))
        loudness = loudness * jnp.repeat(heights, dims[axis_at] // blocks).reshape([-1 if axis == axis_at else 1 for axis in range(len(dims))])
    return loudness


def gaussian(key, extent, scale, most, cuts=(), kind=jnp.bfloat16):
    loudness = steps_of(key, extent, cuts, -0.22, 0.18) if cuts else 1.0
    drawn = jax.random.normal(key, extent, jnp.float32) * scale * loudness
    return jnp.minimum(jnp.maximum(drawn, -most), most).astype(kind)


def setup_inputs(seed: int = 0) -> dict:
    streams_of = jax.random.split(jax.random.key(seed), 8)
    return {
        "latents": draw_latents(jax.random.fold_in(streams_of[7], 71), 0),
        "out_grad": draw_out_grad(jax.random.fold_in(streams_of[7], 71), 0),
        "w_query": draw_w_query(jax.random.fold_in(streams_of[7], 71), 0),
        "w_key": draw_w_key(jax.random.fold_in(streams_of[7], 71), 0),
        "w_value": gaussian(streams_of[4], (D, INNER), D ** -0.5, 0.125, ((0, 16), (1, 16))),
        "w_out": gaussian(streams_of[5], (D, INNER), (16 * D ** -0.5), 1.6171875, ((0, 16), (1, 16))),
        "gain": jnp.clip(1.0 + 0.15 * jax.random.normal(streams_of[6], (D,), jnp.float32), 0.25, 1.75).astype(jnp.bfloat16),
    }


epsilon = 1e-06

def rounded(array):
    return lax.optimization_barrier(array.astype(jnp.bfloat16)).astype(jnp.float32)

def head_grads(stacked):
    queries, keys_all, values_all, out_dir = stacked
    scores = jnp.dot(queries, keys_all.T, preferred_element_type=jnp.float32) * 0.125
    maxima = lax.optimization_barrier(jnp.max(scores, axis=1, keepdims=True))
    expo = jnp.exp(scores - maxima)
    totals = lax.optimization_barrier(jnp.sum(expo, axis=1, keepdims=True))
    attended = jnp.dot(expo.astype(jnp.bfloat16), values_all, preferred_element_type=jnp.float32) / totals
    probs = expo / totals
    delta = lax.optimization_barrier(jnp.sum(out_dir.astype(jnp.float32) * attended, axis=1, keepdims=True))
    prob_grad = jnp.dot(out_dir, values_all.T, preferred_element_type=jnp.float32)
    score_grad = (probs * (prob_grad - delta)).astype(jnp.bfloat16)
    query_grad = (0.125 * jnp.dot(score_grad, keys_all, preferred_element_type=jnp.float32)).astype(jnp.bfloat16)
    score_blocks = score_grad.astype(jnp.float32).reshape(N_ROW, TOK_ROW, SEQ)
    prob_blocks = probs.astype(jnp.bfloat16).astype(jnp.float32).reshape(N_ROW, TOK_ROW, SEQ)
    query_blocks = queries.astype(jnp.float32).reshape(N_ROW, TOK_ROW, HDIM)
    dir_blocks = out_dir.astype(jnp.float32).reshape(N_ROW, TOK_ROW, HDIM)
    key_terms = 0.125 * jnp.einsum('jqk,jqd->jkd', score_blocks, query_blocks)
    value_terms = jnp.einsum('jqk,jqd->jkd', prob_blocks, dir_blocks)
    key_grad = lax.optimization_barrier(jnp.sum(rounded(key_terms), axis=0)).astype(jnp.bfloat16)
    value_grad = lax.optimization_barrier(jnp.sum(rounded(value_terms), axis=0)).astype(jnp.bfloat16)
    return (query_grad, key_grad, value_grad)

def heads_first(array):
    return array.reshape(N_DEPTH, SEQ, HEADS, HDIM).transpose(0, 2, 1, 3).reshape(N_DEPTH * HEADS, SEQ, HDIM)

def heads_back(array):
    return array.reshape(N_DEPTH, HEADS, SEQ, HDIM).transpose(0, 2, 1, 3).reshape(N_DEPTH * SEQ, HEADS * HDIM)

def col_blocks(array):
    return array.reshape(array.shape[0], N_COL, -1).transpose(1, 0, 2)

def add_block(total, parts):
    query_part, key_part, value_part, wq_part, wk_part, wv_part = parts
    term = jnp.dot(query_part, wq_part.T, preferred_element_type=jnp.float32)
    term = term + jnp.dot(key_part, wk_part.T, preferred_element_type=jnp.float32)
    term = term + jnp.dot(value_part, wv_part.T, preferred_element_type=jnp.float32)
    return (total + rounded(term), None)

def reference(latents, out_grad, w_query, w_key, w_value, w_out, gain):
    x_wide = latents.astype(jnp.float32)
    gain_wide = gain.astype(jnp.float32)
    norm_scale = lax.rsqrt(lax.optimization_barrier(jnp.mean(x_wide * x_wide, axis=1, keepdims=True)) + epsilon)
    normalized = x_wide * norm_scale
    normed = (normalized * gain_wide).astype(jnp.bfloat16)
    queries = jnp.dot(normed, w_query, preferred_element_type=jnp.float32).astype(jnp.bfloat16)
    keys_all = jnp.dot(normed, w_key, preferred_element_type=jnp.float32).astype(jnp.bfloat16)
    values_all = jnp.dot(normed, w_value, preferred_element_type=jnp.float32).astype(jnp.bfloat16)
    out_dir = jnp.dot(out_grad, w_out, preferred_element_type=jnp.float32).astype(jnp.bfloat16)
    query_h, key_h, value_h = lax.map(head_grads, (heads_first(queries), heads_first(keys_all), heads_first(values_all), heads_first(out_dir)))
    query_grad = heads_back(query_h)
    key_grad = heads_back(key_h)
    value_grad = heads_back(value_h)
    start_sum = jnp.zeros((TOKENS, D), jnp.float32)
    normed_grad, unused = lax.scan(add_block, start_sum, (col_blocks(query_grad), col_blocks(key_grad), col_blocks(value_grad), col_blocks(w_query), col_blocks(w_key), col_blocks(w_value)))
    scaled = normed_grad * gain_wide
    inner_sum = lax.optimization_barrier(jnp.mean(scaled * normalized, axis=1, keepdims=True))
    raw = out_grad.astype(jnp.float32) + norm_scale * (scaled - normalized * inner_sum)
    return (raw * lax.rsqrt(jnp.mean(raw * raw) + epsilon)).astype(jnp.bfloat16)
```

```python
import functools

import jax
import jax.numpy as jnp
from jax import lax
from jax.experimental import pallas as pl
from jax.experimental.pallas import tpu as pltpu
from jax.sharding import PartitionSpec as P

MESH = pl.DeviceIdType.MESH
F32 = jnp.float32
BF16 = jnp.bfloat16
FEAT = 152
PAD = 160
HALF = 80
TOK = 128
WIDE = 128
HDIM = 64
SLOT = 256
epsilon = 1e-06


def dot_nt(a, b):
    return lax.dot_general(a, b, (((1,), (1,)), ((), ())), preferred_element_type=F32)


def dot_tn(a, b):
    return lax.dot_general(a, b, (((0,), (0,)), ((), ())), preferred_element_type=F32)


def dot_nn(a, b):
    return jnp.dot(a, b, preferred_element_type=F32)


def eye(rows, columns):
    at = lax.broadcasted_iota(jnp.int32, (rows, columns), 0)
    to = lax.broadcasted_iota(jnp.int32, (rows, columns), 1)
    return jnp.where(at == to, 1.0, 0.0).astype(BF16)


def kernel(
    sizes,
    lat_ref, og_ref, wq_ref, wk_ref, wv_ref, wo_ref, gain_ref,
    out_ref,
    xt_all, og_all, wkv_all, wqo_all, kv_all,
    xt_own, og_own, gain_own,
    s_ref, dp_ref, terms, sib_rx, pair_sum, rx,
    rs_tx, rs_right, rs_left,
    pw_tx, pw0, pw1, pw2,
    z_send, z_recv,
    w_send, w_recv, wsib_send, wsib_recv,
    kv_send, kv_recv, kvsib_send, kvsib_recv,
    t_send, t_recv, r_send, r_recv,
    rs_send, rs_recv,
    p_send, p_recv,
):
    depths, los, ys, zs = sizes
    xs = depths * los
    chips = los * ys
    planes = xs * ys
    rows = chips * 2
    seq = rows * TOK
    right_steps = zs // 2
    left_steps = zs - 1 - right_steps

    d = lax.axis_index("depth")
    r = lax.axis_index("row")
    c = lax.axis_index("col")
    core = lax.rem(r, 2)
    other = 1 - core
    chip = r // 2
    lo = chip // ys
    y = lax.rem(chip, ys)
    x = d * los + lo
    here = x * ys + y

    sibling = (d, chip * 2 + other, c)
    z_right = (d, r, lax.rem(c + 1, zs))
    z_left = (d, r, lax.rem(c + zs - 1, zs))

    def plane_device(at):
        to_x, to_y = at // ys, lax.rem(at, ys)
        return (to_x // los, (lax.rem(to_x, los) * ys + to_y) * 2 + core, c)

    def chip_device(to_chip):
        return (d, to_chip * 2 + core, c)

    def remote(src, dst, send, recv, device):
        return pltpu.make_async_remote_copy(
            src_ref=src, dst_ref=dst, send_sem=send, recv_sem=recv, device_id=device, device_id_type=MESH
        )

    barrier = pltpu.get_barrier_semaphore()

    def greet(device):
        pl.semaphore_signal(barrier, inc=1, device_id=device, device_id_type=MESH)

    greet(sibling)

    @pl.loop(1, zs)
    def _(i):
        greet((d, r, lax.rem(c + i, zs)))

    @pl.loop(1, planes)
    def _(i):
        greet(plane_device(lax.rem(here + i, planes)))

    row_at = lax.broadcasted_iota(jnp.int32, (PAD, TOK), 0)
    turn = eye(PAD, FEAT)
    xt = dot_nt(turn, lat_ref[...])
    ogt = dot_nt(turn, og_ref[...])
    gain_diag = turn * gain_ref[...]
    gain_wide = dot_nt(gain_diag, jnp.ones((TOK, FEAT), BF16))
    squares = jnp.sum(xt * xt, axis=0, keepdims=True)
    square_hi = squares.astype(BF16).astype(F32)
    rest = squares - square_hi
    square_mid = rest.astype(BF16).astype(F32)
    square_lo = rest - square_mid
    sent = xt * gain_wide
    sent = jnp.where(row_at == FEAT, square_hi, sent)
    sent = jnp.where(row_at == FEAT + 1, square_mid, sent)
    sent = jnp.where(row_at == FEAT + 2, square_lo, sent)
    xt_all[c] = sent.astype(BF16)
    og_all[c] = ogt.astype(BF16)
    xt_own[...] = xt
    og_own[...] = ogt
    gain_own[...] = gain_wide
    nothing = jnp.zeros((PAD - FEAT, WIDE), BF16)

    def padded(w_ref):
        return jnp.concatenate([w_ref[...], nothing], axis=0)

    wkv_all[r] = jnp.concatenate([padded(wk_ref), padded(wv_ref)], axis=1)
    wqo_all[r] = jnp.concatenate([padded(wq_ref), padded(wo_ref)], axis=1)

    pl.semaphore_wait(barrier, 1 + (zs - 1) + (planes - 1))

    gathers = (xt_all, og_all)

    def ring_right(array, step):
        slot = gathers[array].at[lax.rem(c + zs - step, zs)]
        return remote(slot, slot, z_send.at[array, 0, step], z_recv.at[array, 0, step], z_right)

    def ring_right_came(array, step):
        slot = gathers[array].at[lax.rem(c + 2 * zs - 1 - step, zs)]
        remote(slot, slot, z_send.at[array, 0, step], z_recv.at[array, 0, step], z_right).wait_recv()

    def ring_left(array, step):
        slot = gathers[array].at[lax.rem(c + step, zs)]
        return remote(slot, slot, z_send.at[array, 1, step], z_recv.at[array, 1, step], z_left)

    def ring_left_came(array, step):
        slot = gathers[array].at[lax.rem(c + 1 + step, zs)]
        remote(slot, slot, z_send.at[array, 1, step], z_recv.at[array, 1, step], z_left).wait_recv()

    weights = (wkv_all, wqo_all)

    def weight_column(array, i):
        slot = weights[array].at[r]
        to = x * ys + lax.rem(y + i, ys)
        return remote(slot, slot, w_send.at[array, i], w_recv.at[array, chip], plane_device(to))

    def weight_across(array, i, side):
        slot = weights[array].at[r, pl.ds(side * HALF, HALF)]
        to = lax.rem(x + (1 if side == 0 else xs - 1), xs) * ys + lax.rem(y + i, ys)
        return remote(
            slot, slot, w_send.at[array, ys * (1 + side) + i], w_recv.at[array, chip], plane_device(to)
        )

    def weight_sibling(array, of_chip):
        slot = weights[array].at[of_chip * 2 + core]
        return remote(slot, slot, wsib_send.at[array, of_chip], wsib_recv.at[array, of_chip], sibling)

    def weight_sibling_came(array, of_chip):
        slot = weights[array].at[of_chip * 2 + other]
        remote(slot, slot, wsib_send.at[array, of_chip], wsib_recv.at[array, of_chip], sibling).wait_recv()

    def weight_came(array, of_chip):
        slot = weights[array].at[of_chip * 2 + core]
        remote(slot, slot, w_send.at[array, 0], w_recv.at[array, of_chip], sibling).wait_recv()

    def weight_start(array):
        weight_sibling(array, chip).start()

        @pl.loop(1, ys)
        def _(i):
            weight_column(array, i).start()

        if los > 1:

            @pl.loop(0, ys)
            def _(i):
                weight_across(array, i, 0).start()
                weight_across(array, i, 1).start()

    def nth_chip(t):
        same = t < ys - 1
        of_lo = jnp.where(same, lo, los - 1 - lo)
        of_y = lax.rem(y + jnp.where(same, 1 + t, t - (ys - 1)), ys)
        return of_lo * ys + of_y

    for array in range(2):
        ring_right(array, 0).start()
        ring_left(array, 0).start()
    weight_start(0)
    weight_start(1)

    @pl.loop(1, right_steps)
    def _(step):
        for array in range(2):
            ring_right_came(array, step - 1)
            ring_right(array, step).start()
            ring_left_came(array, step - 1)

            @pl.when(step < left_steps)
            def _():
                ring_left(array, step).start()

        of_chip = nth_chip(step - 1)
        weight_came(0, of_chip)
        weight_sibling(0, of_chip).start()

    ring_right_came(0, right_steps - 1)

    @pl.loop(0, chips)
    def _(i):
        weight_sibling_came(0, i)

    tails = jnp.zeros((16, TOK), F32)
    for j in range(zs):
        tails = tails + xt_all[j, PAD - 16 : PAD, :].astype(F32)
    square_sum = jnp.sum(tails[8:16], axis=0, keepdims=True)
    scale_row = lax.rsqrt(square_sum * (1.0 / (zs * FEAT)) + epsilon)
    scale_wide = jnp.transpose(jnp.broadcast_to(scale_row, (TOK, TOK)))
    scale_two = jnp.concatenate([scale_wide, scale_wide], axis=1)
    group = 4

    def project(source, weight, lanes):
        def body(i, total):
            a = source[pl.ds(i * group, group)].reshape(group * PAD, TOK)
            b = weight[pl.ds(i * group, group), :, lanes]
            return total + dot_tn(a, b.reshape(group * PAD, b.shape[-1]))

        width = lanes.stop - lanes.start
        return lax.fori_loop(0, zs // group, body, jnp.zeros((TOK, width), F32))

    kv = (project(xt_all, wkv_all, slice(0, SLOT)) * scale_two).astype(BF16)
    kv_all[r] = kv

    def kv_copy(i):
        slot = kv_all.at[r]
        return remote(
            slot, slot, kv_send.at[i], kv_recv.at[chip], chip_device(lax.rem(chip + i, chips))
        )

    def kv_came(of_chip):
        slot = kv_all.at[of_chip * 2 + core]
        remote(slot, slot, kv_send.at[0], kv_recv.at[of_chip], sibling).wait_recv()

    def kv_sibling(of_chip):
        slot = kv_all.at[of_chip * 2 + core]
        return remote(slot, slot, kvsib_send.at[of_chip], kvsib_recv.at[of_chip], sibling)

    def kv_sibling_came(of_chip):
        slot = kv_all.at[of_chip * 2 + other]
        remote(slot, slot, kvsib_send.at[of_chip], kvsib_recv.at[of_chip], sibling).wait_recv()

    @pl.loop(1, chips)
    def _(i):
        kv_copy(i).start()

    kv_sibling(chip).start()

    @pl.loop(0, chips - 1)
    def _(t):
        of_chip = nth_chip(t)
        weight_came(1, of_chip)
        weight_sibling(1, of_chip).start()

    ring_right_came(1, right_steps - 1)

    @pl.loop(0, chips)
    def _(i):
        weight_sibling_came(1, i)

    queries = (project(xt_all, wqo_all, slice(0, WIDE)) * scale_wide).astype(BF16)
    out_dir = project(og_all, wqo_all, slice(WIDE, SLOT)).astype(BF16)
    low = lax.broadcasted_iota(jnp.int32, (TOK, WIDE), 1) < HDIM

    def stacked(a):
        wide = a.astype(F32)
        parts = [jnp.where(low, wide, 0.0), jnp.where(low, 0.0, wide)]
        return jnp.concatenate(parts, axis=0).astype(BF16)

    query_stack = stacked(queries.astype(F32) * 0.125)
    dir_stack = stacked(out_dir)

    @pl.loop(1, chips)
    def _(i):
        of_chip = lax.rem(chip + chips - i, chips)
        kv_came(of_chip)
        kv_sibling(of_chip).start()

    @pl.loop(0, chips)
    def _(i):
        kv_sibling_came(i)

    block = 2 * TOK

    def keys_of(i):
        return kv_all[pl.ds(i * 2, 2), :, 0:WIDE].reshape(block, WIDE)

    def values_of(i):
        return kv_all[pl.ds(i * 2, 2), :, WIDE:SLOT].reshape(block, WIDE)

    def folded(a):
        return a.reshape(block // 8, 8, SLOT)

    def scores_body(i, most):
        scores = dot_nt(keys_of(i), query_stack)
        s_ref[i] = scores
        return jnp.maximum(most, jnp.max(folded(scores), axis=0))

    most = lax.fori_loop(0, chips, scores_body, jnp.full((8, SLOT), -jnp.inf, F32))
    most = jnp.max(most, axis=0, keepdims=True)

    def expo_body(i, sums):
        expo = jnp.exp(s_ref[i] - most)
        s_ref[i] = expo
        prob_grad = dot_nt(values_of(i), dir_stack)
        dp_ref[i] = prob_grad
        return sums[0] + jnp.sum(folded(expo), axis=0), sums[1] + jnp.sum(folded(expo * prob_grad), axis=0)

    zero = jnp.zeros((8, SLOT), F32)
    totals, delta = lax.fori_loop(0, chips, expo_body, (zero, zero))
    inverse = 1.0 / jnp.sum(totals, axis=0, keepdims=True)
    delta = jnp.sum(delta, axis=0, keepdims=True) * inverse

    def term_sibling(of_chip):
        return remote(
            terms.at[of_chip * 2 + other], sib_rx.at[of_chip], t_send.at[of_chip], t_recv.at[of_chip], sibling
        )

    def term_copy(of_chip):
        return remote(
            pair_sum.at[of_chip], rx.at[chip], r_send.at[of_chip], r_recv.at[chip], chip_device(of_chip)
        )

    def term_came(of_chip):
        remote(
            pair_sum.at[of_chip], rx.at[of_chip], r_send.at[of_chip], r_recv.at[of_chip], sibling
        ).wait_recv()

    def pair(of_chip):
        term_sibling(of_chip).wait_recv()
        own = terms[of_chip * 2 + core].astype(F32)
        pair_sum[of_chip] = (own + sib_rx[of_chip].astype(F32)).astype(BF16)

    def grads_body(n, query_grad):
        i = lax.rem(chip + 1 + n, chips)
        probs = s_ref[i] * inverse
        score_grad = (probs * (dp_ref[i] - delta)).astype(BF16)
        key_term = dot_nn(score_grad, query_stack)
        value_term = dot_nn(probs.astype(BF16), dir_stack)
        both = jnp.concatenate([key_term, value_term], axis=1).astype(BF16)
        terms[pl.ds(i * 2, 2)] = both.reshape(2, TOK, SLOT)
        term_sibling(i).start()

        @pl.when(n > 0)
        def _():
            before = lax.rem(chip + n, chips)
            pair(before)
            term_copy(before).start()

        return query_grad + dot_tn(keys_of(i), score_grad)

    query_grad = lax.fori_loop(0, chips, grads_body, jnp.zeros((WIDE, SLOT), F32))
    query_grad = jnp.concatenate([query_grad[0:HDIM, 0:TOK], query_grad[HDIM:WIDE, TOK:SLOT]], axis=0)
    query_grad = (query_grad * 0.125).astype(BF16)
    pair(chip)
    total = pair_sum[chip].astype(F32)

    def sum_body(i, total):
        of_chip = lax.rem(chip + chips - i, chips)
        term_came(of_chip)
        return total + rx[of_chip].astype(F32)

    kv_grad = lax.fori_loop(1, chips, sum_body, total).astype(BF16)

    queries_turned = dot_nt(eye(WIDE, WIDE), queries)
    inner = jnp.sum(query_grad.astype(F32) * queries_turned, axis=0, keepdims=True)
    kv_inner = kv_grad.astype(F32) * kv.astype(F32)
    kv_hi = kv_inner.astype(BF16)
    kv_lo = (kv_inner - kv_hi.astype(F32)).astype(BF16)
    ones = jnp.ones((8, SLOT), BF16)
    kv_inner = dot_nt(ones, kv_hi) + dot_nt(ones, kv_lo)
    inner = inner + kv_inner[0:1]

    def partial(j):
        value = dot_nt(wkv_all[j], kv_grad) + dot_nn(wqo_all[j, :, 0:WIDE], query_grad)
        return jnp.where(row_at == FEAT, inner, value)

    def rs_copy(src, side, step):
        dst = (rs_right, rs_left)[side].at[step]
        return remote(src, dst, rs_send.at[side, step], rs_recv.at[side, step], (z_right, z_left)[side])

    def rs_came(side, step):
        rs_copy(rs_tx.at[side], side, step).wait_recv()

    rs_tx[0] = partial(lax.rem(c + right_steps, zs)).astype(BF16)
    rs_copy(rs_tx.at[0], 0, 0).start()
    rs_tx[1] = partial(lax.rem(c + zs - left_steps, zs)).astype(BF16)
    rs_copy(rs_tx.at[1], 1, 0).start()

    @pl.loop(1, right_steps)
    def _(step):
        to_right = partial(lax.rem(c + right_steps - step, zs))
        to_left = partial(lax.rem(c + zs - left_steps + step, zs))
        rs_came(0, step - 1)
        rs_right[step - 1] = (rs_right[step - 1].astype(F32) + to_right).astype(BF16)
        rs_copy(rs_right.at[step - 1], 0, step).start()
        rs_came(1, step - 1)

        @pl.when(step < left_steps)
        def _():
            rs_left[step - 1] = (rs_left[step - 1].astype(F32) + to_left).astype(BF16)
            rs_copy(rs_left.at[step - 1], 1, step).start()

    own = partial(c) + rs_left[left_steps - 1].astype(F32)
    rs_came(0, right_steps - 1)
    own = own + rs_right[right_steps - 1].astype(F32)

    inner = own[FEAT : FEAT + 1] * (1.0 / (zs * FEAT))
    scaled = own * gain_own[...]
    normalized = xt_own[...] * scale_row
    raw = og_own[...] + scale_row * (scaled - normalized * inner)
    power = jnp.sum((raw * raw).reshape(PAD // 8, 8, TOK), axis=0)

    def power_sibling():
        return remote(pw_tx.at[0], pw0, p_send.at[0, 0], p_recv.at[0, 0], sibling)

    def power_plane(i):
        to = plane_device(lax.rem(here + i, planes))
        return remote(pw_tx.at[1], pw1.at[here], p_send.at[1, i], p_recv.at[1, here], to)

    def power_plane_came(i):
        of = lax.rem(here + i, planes)
        remote(pw_tx.at[1], pw1.at[of], p_send.at[1, i], p_recv.at[1, of], sibling).wait_recv()

    def power_col(i):
        return remote(pw_tx.at[2], pw2.at[c], p_send.at[2, i], p_recv.at[2, c], (d, r, lax.rem(c + i, zs)))

    def power_col_came(i):
        of = lax.rem(c + i, zs)
        remote(pw_tx.at[2], pw2.at[of], p_send.at[2, i], p_recv.at[2, of], sibling).wait_recv()

    pw_tx[0] = power
    power_sibling().start()
    power_sibling().wait_recv()
    power = power + pw0[...]
    pw_tx[1] = power
    pw1[here] = power

    @pl.loop(1, planes)
    def _(i):
        power_plane(i).start()

    @pl.loop(1, planes)
    def _(i):
        power_plane_came(i)

    power = jnp.sum(pw1[...], axis=0)
    pw_tx[2] = power
    pw2[c] = power

    @pl.loop(1, zs)
    def _(i):
        power_col(i).start()

    @pl.loop(1, zs)
    def _(i):
        power_col_came(i)

    power = jnp.sum(jnp.sum(pw2[...], axis=0), axis=0, keepdims=True)
    power = jnp.sum(power, axis=1, keepdims=True)
    cells = depths * seq * zs * FEAT
    final = (raw * lax.rsqrt(power * (1.0 / cells) + epsilon)).astype(BF16)
    out_ref[...] = dot_nt(eye(TOK, TOK), final)[:, 0:FEAT].astype(BF16)

    for array in range(2):

        @pl.loop(0, right_steps)
        def _(step):
            ring_right(array, step).wait_send()

        @pl.loop(0, left_steps)
        def _(step):
            ring_left(array, step).wait_send()

        @pl.loop(1, ys)
        def _(i):
            weight_column(array, i).wait_send()

        if los > 1:

            @pl.loop(0, ys)
            def _(i):
                weight_across(array, i, 0).wait_send()
                weight_across(array, i, 1).wait_send()

        @pl.loop(0, chips)
        def _(i):
            weight_sibling(array, i).wait_send()

    @pl.loop(1, chips)
    def _(i):
        kv_copy(i).wait_send()
        term_copy(lax.rem(chip + i, chips)).wait_send()

    @pl.loop(0, chips)
    def _(i):
        kv_sibling(i).wait_send()
        term_sibling(i).wait_send()

    @pl.loop(0, right_steps)
    def _(step):
        rs_copy(rs_tx.at[0], 0, step).wait_send()

    @pl.loop(0, left_steps)
    def _(step):
        rs_copy(rs_tx.at[1], 1, step).wait_send()

    power_sibling().wait_send()

    @pl.loop(1, planes)
    def _(i):
        power_plane(i).wait_send()

    @pl.loop(1, zs)
    def _(i):
        power_col(i).wait_send()


def sizes_of(mesh):
    depths, rows, zs = mesh.shape["depth"], mesh.shape["row"], mesh.shape["col"]
    los = 2
    return depths, los, rows // (2 * los), zs


def solution(mesh):
    depths, los, ys, zs = sizes_of(mesh)
    chips, planes = los * ys, depths * los * ys
    rows = chips * 2
    right_steps = zs // 2
    left_steps = zs - 1 - right_steps
    dma = pltpu.SemaphoreType.DMA
    scratch = [
        pltpu.VMEM((zs, PAD, TOK), BF16),
        pltpu.VMEM((zs, PAD, TOK), BF16),
        pltpu.VMEM((rows, PAD, SLOT), BF16),
        pltpu.VMEM((rows, PAD, SLOT), BF16),
        pltpu.VMEM((rows, TOK, SLOT), BF16),
        pltpu.VMEM((PAD, TOK), F32),
        pltpu.VMEM((PAD, TOK), F32),
        pltpu.VMEM((PAD, TOK), F32),
        pltpu.VMEM((chips, 2 * TOK, SLOT), F32),
        pltpu.VMEM((chips, 2 * TOK, SLOT), F32),
        pltpu.VMEM((rows, TOK, SLOT), BF16),
        pltpu.VMEM((chips, TOK, SLOT), BF16),
        pltpu.VMEM((chips, TOK, SLOT), BF16),
        pltpu.VMEM((chips, TOK, SLOT), BF16),
        pltpu.VMEM((2, PAD, TOK), BF16),
        pltpu.VMEM((right_steps, PAD, TOK), BF16),
        pltpu.VMEM((left_steps, PAD, TOK), BF16),
        pltpu.VMEM((3, 8, TOK), F32),
        pltpu.VMEM((8, TOK), F32),
        pltpu.VMEM((planes, 8, TOK), F32),
        pltpu.VMEM((zs, 8, TOK), F32),
        dma((2, 2, right_steps)), dma((2, 2, right_steps)),
        dma((2, 3 * ys)), dma((2, chips)), dma((2, chips)), dma((2, chips)),
        dma((chips,)), dma((chips,)), dma((chips,)), dma((chips,)),
        dma((chips,)), dma((chips,)), dma((chips,)), dma((chips,)),
        dma((2, right_steps)), dma((2, right_steps)),
        dma((3, max(planes, zs))), dma((3, max(planes, zs))),
    ]

    def shards(latents, out_grad, w_query, w_key, w_value, w_out, gain):
        vmem = pl.BlockSpec(memory_space=pltpu.VMEM)
        return pl.pallas_call(
            functools.partial(kernel, (depths, los, ys, zs)),
            out_shape=jax.ShapeDtypeStruct((TOK, FEAT), BF16),
            in_specs=[vmem] * 7,
            out_specs=vmem,
            scratch_shapes=scratch,
            compiler_params=pltpu.CompilerParams(
                collective_id=0, has_side_effects=True, vmem_limit_bytes=40 * 1024 * 1024
            ),
        )(latents, out_grad, w_query, w_key, w_value, w_out, gain.reshape(1, FEAT))

    return jax.shard_map(
        shards,
        mesh=mesh,
        in_specs=(
            P(("depth", "row"), "col"),
            P(("depth", "row"), "col"),
            P("row", "col"),
            P("row", "col"),
            P("row", "col"),
            P("row", "col"),
            P("col"),
        ),
        out_specs=P(("depth", "row"), "col"),
        check_vma=False,
    )
```

```python
import functools

import jax
import jax.numpy as jnp
from jax import lax
from jax.experimental import pallas as pl
from jax.experimental.pallas import tpu as pltpu
from jax.sharding import PartitionSpec as P

MESH = pl.DeviceIdType.MESH
F32 = jnp.float32
BF16 = jnp.bfloat16
FEAT = 152
PAD = 160
HALF = 80
TOK = 128
WIDE = 128
HDIM = 64
SLOT = 256
epsilon = 1e-06


def dot_nt(a, b):
    return lax.dot_general(a, b, (((1,), (1,)), ((), ())), preferred_element_type=F32)


def dot_tn(a, b):
    return lax.dot_general(a, b, (((0,), (0,)), ((), ())), preferred_element_type=F32)


def dot_nn(a, b):
    return jnp.dot(a, b, preferred_element_type=F32)


def eye(rows, columns):
    at = lax.broadcasted_iota(jnp.int32, (rows, columns), 0)
    to = lax.broadcasted_iota(jnp.int32, (rows, columns), 1)
    return jnp.where(at == to, 1.0, 0.0).astype(BF16)


def kernel(
    sizes,
    lat_hbm, og_hbm, wq_hbm, wk_hbm, wv_hbm, wo_hbm, gain_hbm,
    out_ref,
    lat_ref, og_ref, wq_ref, wk_ref, wv_ref, wo_ref, gain_ref,
    xt_all, og_all, wkv_all, wqo_all, kv_all, qd_all, st_all,
    xt_own, og_own, gain_own,
    s_ref, dp_ref, kt_ref, ds_ref, s2_ref, dp2_ref, p2_ref, ds2_ref,
    rs_leaf_tx, rs_hub_tx, rs_leaf, rs_hub,
    pw_tx, pw0, pw1, pw2,
    in_sem,
    z_send, z_recv,
    w_send, w_recv, wsib_recv,
    a_send, a_recv, asib_recv,
    st_send, st_recv,
    rs_send, rs_recv,
    p_send, p_recv,
):
    depths, los, ys, zs = sizes
    xs = depths * los
    chips = los * ys
    planes = xs * ys
    rows = chips * 2
    seq = rows * TOK
    quarter = zs // 4

    d = lax.axis_index("depth")
    r = lax.axis_index("row")
    c = lax.axis_index("col")
    core = lax.rem(r, 2)
    other = 1 - core
    chip = r // 2
    lo = chip // ys
    y = lax.rem(chip, ys)
    x = d * los + lo
    here = x * ys + y

    sibling = (d, chip * 2 + other, c)

    def z_at(by):
        return lax.rem(c + by % zs, zs)

    def z_device(by):
        return (d, r, z_at(by))

    def plane_device(at):
        to_x, to_y = at // ys, lax.rem(at, ys)
        return (to_x // los, (lax.rem(to_x, los) * ys + to_y) * 2 + core, c)

    def remote(src, dst, send, recv, device):
        return pltpu.make_async_remote_copy(
            src_ref=src, dst_ref=dst, send_sem=send, recv_sem=recv, device_id=device, device_id_type=MESH
        )

    inputs = (lat_hbm, og_hbm, gain_hbm, wk_hbm, wv_hbm, wq_hbm, wo_hbm)
    staged = (lat_ref, og_ref, gain_ref, wk_ref, wv_ref, wq_ref, wo_ref)
    fetches = [pltpu.make_async_copy(a, b, in_sem.at[i]) for i, (a, b) in enumerate(zip(inputs, staged))]
    for fetch in fetches:
        fetch.start()

    barrier = pltpu.get_barrier_semaphore()

    def greet(device):
        pl.semaphore_signal(barrier, inc=1, device_id=device, device_id_type=MESH)

    for by in sorted({by % zs for by in (1, -1, 2, -2)}):
        greet(z_device(by))
    greet(sibling)

    @pl.loop(1, planes)
    def _(i):
        greet(plane_device(lax.rem(here + i, planes)))

    for fetch in fetches:
        fetch.wait()

    row_at = lax.broadcasted_iota(jnp.int32, (PAD, TOK), 0)
    nothing = jnp.zeros((PAD - FEAT, WIDE), BF16)

    def padded(ref):
        return jnp.concatenate([ref[...], nothing], axis=0)

    og_all[c] = padded(og_ref)
    xt = padded(lat_ref).astype(F32)
    gain_wide = dot_nt(eye(PAD, FEAT) * gain_ref[...].reshape(1, FEAT), jnp.ones((TOK, FEAT), BF16))
    squares = jnp.sum(xt * xt, axis=0, keepdims=True)
    square_hi = squares.astype(BF16).astype(F32)
    rest = squares - square_hi
    square_mid = rest.astype(BF16).astype(F32)
    square_lo = rest - square_mid
    sent = xt * gain_wide
    sent = jnp.where(row_at == FEAT, square_hi, sent)
    sent = jnp.where(row_at == FEAT + 1, square_mid, sent)
    sent = jnp.where(row_at == FEAT + 2, square_lo, sent)
    xt_all[c] = sent.astype(BF16)
    xt_own[...] = xt
    og_own[...] = padded(og_ref).astype(F32)
    gain_own[...] = gain_wide
    wkv_all[lo, y, core] = jnp.concatenate([padded(wk_ref), padded(wv_ref)], axis=1)
    wqo_all[lo, y, core] = jnp.concatenate([padded(wq_ref), padded(wo_ref)], axis=1)

    pl.semaphore_wait(barrier, len({by % zs for by in (1, -1, 2, -2)}) + planes)

    streams = (xt_all, og_all)

    def tree(stream, side, leaf, k):
        sign = -1 if side else 1
        slot = streams[stream].at[z_at(-2 * k * sign)]
        to = z_device(sign if leaf else 2 * sign)
        return remote(slot, slot, z_send.at[stream], z_recv.at[stream, side, leaf, k], to)

    def tree_came(stream, side, leaf, k):
        sign = -1 if side else 1
        slot = streams[stream].at[z_at(-(2 * k + (1 if leaf else 2)) * sign)]
        remote(slot, slot, z_send.at[stream], z_recv.at[stream, side, leaf, k], sibling).wait_recv()

    def tree_round(stream, k):
        if k:
            tree_came(stream, 0, 0, k - 1)
        tree(stream, 0, 0, k).start()
        if k:
            tree(stream, 0, 1, k).start()
            tree_came(stream, 1, 0, k - 1)
        if k < quarter - 1:
            tree(stream, 1, 0, k).start()
        if not k:
            tree(stream, 0, 1, k).start()
        tree(stream, 1, 1, k).start()

    def tree_end(stream):
        tree_came(stream, 0, 0, quarter - 1)
        for k in range(quarter):
            tree_came(stream, 0, 1, k)
            tree_came(stream, 1, 1, k)

    def column_device(up):
        return (d, (lo * ys + lax.rem(y + up % ys, ys)) * 2 + core, c)

    def x_device(by):
        return plane_device(lax.rem(x + by % xs, xs) * ys + y)

    def y_at(up):
        return lax.rem(y + up % ys, ys)

    weights = (wkv_all, wqo_all)

    def weight_y(array, up, start, size, to):
        slot = weights[array].at[lo, y_at(up), core, pl.ds(start, size)]
        return remote(slot, slot, w_send.at[array, 0], w_recv.at[array, y_at(up)], column_device(to))

    def weight_y_came(array, up):
        weight_y(array, up, 0, PAD, 0).wait_recv()

    def weight_x(array, side):
        slot = weights[array].at[lo, :, core, pl.ds(side * HALF, HALF)]
        return remote(slot, slot, w_send.at[array, 1], w_recv.at[array, ys], x_device(-1 if side else 1))

    def weight_x_one(array, up):
        for side in range(2):
            slot = weights[array].at[lo, y_at(up), core, pl.ds(side * HALF, HALF)]
            to = x_device(-1 if side else 1)
            remote(slot, slot, w_send.at[array, 1], w_recv.at[array, ys], to).start()

    def weight_sibling(array, of_lo):
        slot = weights[array].at[of_lo, :, core]
        return remote(slot, slot, w_send.at[array, 2], wsib_recv.at[array], sibling)

    def weight_first(array):
        if ys == 4:
            weight_y(array, 0, 0, PAD, 1).start()
            weight_y(array, 0, 0, PAD, -1).start()
        elif ys == 2:
            weight_y(array, 0, 0, PAD, 1).start()

    def weight_near(array):
        if ys == 4:
            weight_y_came(array, -1)
            weight_y(array, -1, 0, HALF, 1).start()
            weight_y_came(array, 1)
            weight_y(array, 1, HALF, HALF, -1).start()
            if array == 0:
                weight_x_one(array, -1)
                weight_x_one(array, 1)
        elif ys == 2:
            weight_y_came(array, 1)
            if array == 0:
                weight_x_one(array, 1)

    def weight_column(array):
        if ys == 4:
            weight_y_came(array, 2)
            if array == 0:
                weight_x_one(array, 2)
        if array == 1:
            weight_x(array, 0).start()
            weight_x(array, 1).start()
        weight_sibling(array, lo).start()

    def weight_crossed(array):
        slot = weights[array].at[1 - lo, :, core]
        remote(slot, slot, w_send.at[array, 2], w_recv.at[array, ys], sibling).wait_recv()
        weight_sibling(array, 1 - lo).start()

    def weight_all(array):
        slot = weights[array].at[:, :, other]
        remote(slot, slot, w_send.at[array, 2], wsib_recv.at[array], sibling).wait_recv()

    def sent(ref, sem):
        remote(ref, ref, sem, p_recv.at[0], sibling).wait_send()

    tree_round(0, 0)
    weight_first(0)
    weight_x_one(0, 0)
    weight_first(1)
    for k in range(1, quarter):
        tree_round(0, k)
        if k == 1:
            weight_near(0)
        if k == 2:
            weight_column(0)
            weight_near(1)
    if quarter < 2:
        weight_near(0)
    tree_round(1, 0)
    if quarter < 3:
        weight_column(0)
        weight_near(1)
    weight_column(1)
    weight_crossed(0)
    tree_end(0)
    weight_all(0)
    if quarter > 1:
        tree_round(1, 1)

    tails = jnp.zeros((16, TOK), F32)
    for j in range(zs):
        tails = tails + xt_all[j, PAD - 16 : PAD, :].astype(F32)
    square_sum = jnp.sum(tails[8:16], axis=0, keepdims=True)
    scale_row = lax.rsqrt(square_sum * (1.0 / (zs * FEAT)) + epsilon)
    scale_wide = jnp.transpose(jnp.broadcast_to(scale_row, (TOK, TOK)))
    scale_two = jnp.concatenate([scale_wide, scale_wide], axis=1)
    pair = min(ys, 2)

    def project(source, weight, lanes):
        total = None
        for of_lo in range(los):
            for of_y in range(0, ys, pair):
                first = (of_lo * ys + of_y) * 2
                a = source[first : first + 2 * pair].reshape(2 * pair * PAD, TOK)
                b = weight[of_lo, of_y : of_y + pair, :, :, lanes]
                term = dot_tn(a, b.reshape(2 * pair * PAD, b.shape[-1]))
                total = term if total is None else total + term
        return total

    gathered = (kv_all, qd_all)
    half = TOK // 2

    def column(across):
        return 1 - lo if across else lo

    def slot_x(array):
        slot = gathered[array].at[lo, y, core]
        to = (d, ((1 - lo) * ys + y) * 2 + core, c)
        return remote(slot, slot, a_send.at[array, 1], a_recv.at[array, lo, y], to)

    def slot_y(array, across, up, start, size, to):
        slot = gathered[array].at[column(across), y_at(up), core, pl.ds(start, size)]
        recv = a_recv.at[array, column(across), y_at(up)]
        return remote(slot, slot, a_send.at[array, 0], recv, column_device(to))

    def slot_came(array, across, up):
        slot_y(array, across, up, 0, TOK, 0).wait_recv()

    def slot_out(array, across):
        if across:
            slot_came(array, 1, 0)
        if ys == 4:
            slot_y(array, across, 0, 0, TOK, 1).start()
            slot_y(array, across, 0, 0, TOK, -1).start()
        elif ys == 2:
            slot_y(array, across, 0, 0, TOK, 1).start()

    def slot_start(array):
        slot_x(array).start()
        slot_out(array, 0)

    def slot_near(array, across):
        if ys == 4:
            slot_came(array, across, -1)
            slot_y(array, across, -1, 0, half, 1).start()
            slot_came(array, across, 1)
            slot_y(array, across, 1, half, half, -1).start()
        elif ys == 2:
            slot_came(array, across, 1)

    def slot_far(array, across):
        if ys == 4:
            slot_came(array, across, 2)
        slot = gathered[array].at[column(across), :, core]
        remote(slot, slot, a_send.at[array, 2], asib_recv.at[array], sibling).start()

    def slot_all(array):
        slot = gathered[array].at[:, :, other]
        remote(slot, slot, a_send.at[array, 2], asib_recv.at[array], sibling).wait_recv()

    kv = (project(xt_all, wkv_all, slice(0, SLOT)) * scale_two).astype(BF16)
    kv_all[lo, y, core] = kv
    slot_start(0)
    weight_crossed(1)
    if quarter > 2:
        tree_round(1, 2)
    weight_all(1)
    queries = (project(xt_all, wqo_all, slice(0, WIDE)) * scale_wide).astype(BF16)
    slot_out(0, 1)
    slot_near(0, 0)
    if quarter > 3:
        tree_round(1, 3)
    slot_near(0, 1)
    slot_far(0, 0)
    tree_end(1)
    out_dir = project(og_all, wqo_all, slice(WIDE, SLOT)).astype(BF16)
    scaled_queries = (queries.astype(F32) * 0.125).astype(BF16)
    qd_all[lo, y, core] = jnp.concatenate([scaled_queries, out_dir], axis=1)
    slot_start(1)
    slot_far(0, 1)
    low = lax.broadcasted_iota(jnp.int32, (TOK, WIDE), 1) < HDIM

    def stacked(a):
        wide = a.astype(F32)
        parts = [jnp.where(low, wide, 0.0), jnp.where(low, 0.0, wide)]
        return jnp.concatenate(parts, axis=0).astype(BF16)

    query_stack = stacked(scaled_queries)
    dir_stack = stacked(out_dir)

    def slots_of(ref, parity, lanes):
        return ref[:, :, parity, :, lanes].reshape(chips * TOK, lanes.stop - lanes.start)

    def scores_of(parity):
        keys = slots_of(kv_all, parity, slice(0, WIDE))
        scores = dot_nt(keys, query_stack)
        s_ref[:, :, parity] = scores.reshape(los, ys, TOK, SLOT)
        prob_grad = dot_nt(slots_of(kv_all, parity, slice(WIDE, SLOT)), dir_stack)
        dp_ref[:, :, parity] = prob_grad.reshape(los, ys, TOK, SLOT)
        kt_ref[parity] = jnp.transpose(keys)
        return jnp.max(scores.reshape(chips * TOK // 8, 8, SLOT), axis=0)

    most = scores_of(core)
    slot_out(1, 1)
    slot_near(1, 0)
    slot_all(0)
    most = jnp.max(jnp.maximum(most, scores_of(other)), axis=0, keepdims=True)
    slot_near(1, 1)
    slot_far(1, 0)

    def tile_at(i):
        return i // (2 * ys), lax.rem(i // 2, ys), lax.rem(i, 2)

    def folded(a):
        return jnp.sum(a.reshape(TOK // 8, 8, SLOT), axis=0)

    def expo_body(i, sums):
        at = tile_at(i)
        expo = jnp.exp(s_ref[at] - most)
        s_ref[at] = expo
        return sums[0] + folded(expo), sums[1] + folded(expo * dp_ref[at])

    zero = jnp.zeros((8, SLOT), F32)
    totals, delta = lax.fori_loop(0, rows, expo_body, (zero, zero), unroll=2)
    totals = jnp.sum(totals, axis=0, keepdims=True)
    inverse = 1.0 / totals
    delta = jnp.sum(delta, axis=0, keepdims=True) * inverse
    slot_far(1, 1)

    def stat_copy(i):
        to = lax.rem(r + i, rows)
        return remote(st_all.at[r], st_all.at[r], st_send, st_recv, (d, to, c))

    def small_came(ref, count, sem):
        some = ref.at[pl.ds(0, count)]
        remote(some, some, p_send.at[0], sem, sibling).wait_recv()

    st_all[r] = jnp.concatenate([most + jnp.log(totals), delta, jnp.zeros((6, SLOT), F32)], axis=0)

    @pl.loop(1, rows)
    def _(i):
        stat_copy(i).start()

    def score_grad_body(i, nothing):
        at = tile_at(i)
        ds_ref[at] = (s_ref[at] * (dp_ref[at] - delta)).astype(BF16)
        return nothing

    lax.fori_loop(0, rows, score_grad_body, 0, unroll=2)
    query_grad = jnp.zeros((WIDE, SLOT), F32)
    for parity in range(2):
        query_grad = query_grad + dot_nn(kt_ref[parity], slots_of(ds_ref, parity, slice(0, SLOT)))
    query_grad = query_grad * (inverse * 0.125)
    query_grad = jnp.concatenate([query_grad[0:HDIM, 0:TOK], query_grad[HDIM:WIDE, TOK:SLOT]], axis=0)
    query_grad = query_grad.astype(BF16)

    key_stack = stacked(kv[:, 0:WIDE])
    value_stack = stacked(kv[:, WIDE:SLOT])
    wide = pair * TOK
    blocks = [(of_lo, of_y) for of_lo in range(los) for of_y in range(0, ys, pair)]
    parities = (core, other)

    def own_scores(side):
        for n, (of_lo, of_y) in enumerate(blocks):
            block = qd_all[of_lo, of_y : of_y + pair, parities[side]].reshape(wide, SLOT)
            s2_ref[side * len(blocks) + n] = dot_nt(key_stack, block[:, 0:WIDE])
            dp2_ref[side * len(blocks) + n] = dot_nt(value_stack, block[:, WIDE:SLOT])

    own_scores(0)
    slot_all(1)
    own_scores(1)
    small_came(st_all, rows - 1, st_recv)

    for side in range(2):
        for n, (of_lo, of_y) in enumerate(blocks):
            stats = [st_all[(of_lo * ys + of_y + i) * 2 + parities[side]] for i in range(pair)]
            at = side * len(blocks) + n
            lanes = slice(at * wide, (at + 1) * wide)
            for head in range(2):
                part = slice(head * TOK, (head + 1) * TOK)
                total = jnp.concatenate([stat[0:1, part] for stat in stats], axis=1)
                shift = jnp.concatenate([stat[1:2, part] for stat in stats], axis=1)
                probs = jnp.exp(s2_ref[at, part] - total)
                p2_ref[part, lanes] = probs.astype(BF16)
                ds2_ref[part, lanes] = (probs * (dp2_ref[at, part] - shift)).astype(BF16)

    key_grad = jnp.zeros((SLOT, WIDE), F32)
    value_grad = jnp.zeros((SLOT, WIDE), F32)
    for side in range(2):
        lanes = slice(side * chips * TOK, (side + 1) * chips * TOK)
        key_grad = key_grad + dot_nn(ds2_ref[:, lanes], slots_of(qd_all, parities[side], slice(0, WIDE)))
        value_grad = value_grad + dot_nn(p2_ref[:, lanes], slots_of(qd_all, parities[side], slice(WIDE, SLOT)))
    key_grad = jnp.where(low, key_grad[0:TOK], key_grad[TOK:SLOT])
    value_grad = jnp.where(low, value_grad[0:TOK], value_grad[TOK:SLOT])
    kv_grad = jnp.concatenate([key_grad, value_grad], axis=1)
    turned = jnp.concatenate([jnp.transpose(key_grad), jnp.transpose(value_grad)], axis=0).astype(BF16)
    kv_grad = kv_grad.astype(BF16)
    grads_turned = jnp.concatenate([turned, query_grad], axis=0)

    queries_turned = dot_nt(eye(WIDE, WIDE), queries)
    inner = jnp.sum(query_grad.astype(F32) * queries_turned, axis=0, keepdims=True)
    kv_inner = kv_grad.astype(F32) * kv.astype(F32)
    kv_hi = kv_inner.astype(BF16)
    kv_lo = (kv_inner - kv_hi.astype(F32)).astype(BF16)
    ones = jnp.ones((8, SLOT), BF16)
    kv_inner = dot_nt(ones, kv_hi) + dot_nt(ones, kv_lo)
    inner = inner + kv_inner[0:1]

    def partials(places):
        slots = []
        for by in places:
            j = z_at(by)
            at = (j // (2 * ys), lax.rem(j // 2, ys), lax.rem(j, 2))
            slots.append(jnp.concatenate([wkv_all[at], wqo_all[at + (slice(None), slice(0, WIDE))]], axis=1))
        value = dot_nn(jnp.concatenate(slots, axis=0), grads_turned)
        parts = [value[i * PAD : (i + 1) * PAD] for i in range(len(places))]
        return [jnp.where(row_at == FEAT, inner, part) for part in parts]

    some = pl.ds(0, zs - 1)
    for i in range(2):
        sent(streams[i].at[some], z_send.at[i])
        for group, sems, x_slots in ((weights[i], w_send, slice(0, ys)), (gathered[i], a_send, slice(0, 1))):
            if ys > 1:
                columns = slice(0, 1) if group is weights[i] else slice(0, 2)
                sent(group.at[columns, pl.ds(0, ys - 1), 0], sems.at[i, 0])
            sent(group.at[0, x_slots, 0], sems.at[i, 1])
            sent(group.at[:, :, 0], sems.at[i, 2])

    sent(st_all.at[pl.ds(0, rows - 1)], st_send)

    far = 2 * quarter

    def rs_leaf_copy(side, m):
        to = z_device(-1 if side else 1)
        return remote(rs_leaf_tx.at[side, m], rs_leaf.at[side, m], rs_send.at[side], rs_recv.at[side, 1, m], to)

    def rs_hub_copy(side, k):
        to = z_device(-2 if side else 2)
        return remote(rs_hub_tx.at[side, k], rs_hub.at[side, k], rs_send.at[side], rs_recv.at[side, 0, k], to)

    def leaf(side, m, part):
        rs_leaf_tx[side, m] = part.astype(BF16)
        rs_leaf_copy(side, m).start()

    hub_part, right_part, left_part = partials([far, far - 1, 1 - far])
    rs_hub_tx[0, 0] = hub_part.astype(BF16)
    rs_hub_copy(0, 0).start()
    leaf(0, 0, right_part)
    leaf(1, 0, left_part)
    for k in range(1, quarter):
        by = far - 2 * k
        to_right, to_left, right_part, left_part = partials([by, -by, by - 1, 1 - by])
        rs_hub_copy(0, k - 1).wait_recv()
        rs_leaf_copy(0, k - 1).wait_recv()
        total = to_right + rs_hub[0, k - 1].astype(F32) + rs_leaf[0, k - 1].astype(F32)
        rs_hub_tx[0, k] = total.astype(BF16)
        rs_hub_copy(0, k).start()
        rs_leaf_copy(1, k - 1).wait_recv()
        total = to_left + rs_leaf[1, k - 1].astype(F32)
        if k > 1:
            rs_hub_copy(1, k - 2).wait_recv()
            total = total + rs_hub[1, k - 2].astype(F32)
        rs_hub_tx[1, k - 1] = total.astype(BF16)
        rs_hub_copy(1, k - 1).start()
        leaf(0, k, right_part)
        leaf(1, k, left_part)

    own = partials([0])[0]
    for side in range(2):
        last = quarter - 1 - side
        rs_leaf_copy(side, quarter - 1).wait_recv()
        own = own + rs_leaf[side, quarter - 1].astype(F32)
        if last >= 0:
            rs_hub_copy(side, last).wait_recv()
            own = own + rs_hub[side, last].astype(F32)

    inner = own[FEAT : FEAT + 1] * (1.0 / (zs * FEAT))
    scaled = own * gain_own[...]
    normalized = xt_own[...] * scale_row
    raw = og_own[...] + scale_row * (scaled - normalized * inner)
    power = jnp.sum((raw * raw).reshape(PAD // 8, 8, TOK), axis=0)

    def power_sibling():
        return remote(pw_tx.at[0], pw0, p_send.at[0], p_recv.at[0], sibling)

    def power_plane(i):
        to = plane_device(lax.rem(here + i, planes))
        return remote(pw_tx.at[1], pw1.at[here], p_send.at[1], p_recv.at[1], to)

    def power_col(i):
        return remote(pw_tx.at[2], pw2.at[c], p_send.at[2], p_recv.at[2], (d, r, lax.rem(c + i, zs)))

    pw_tx[0] = power
    power_sibling().start()
    power_sibling().wait_recv()
    power = power + pw0[...]
    pw_tx[1] = power
    pw1[here] = power

    @pl.loop(1, planes)
    def _(i):
        power_plane(i).start()

    small_came(pw1, planes - 1, p_recv.at[1])

    sent(xt_all.at[pl.ds(0, far)], rs_send.at[0])
    sent(xt_all.at[pl.ds(0, far - 1)], rs_send.at[1])
    power = jnp.sum(pw1[...], axis=0)
    pw_tx[2] = power
    pw2[c] = power

    @pl.loop(1, zs)
    def _(i):
        power_col(i).start()

    small_came(pw2, zs - 1, p_recv.at[2])

    power_sibling().wait_send()
    sent(pw1.at[pl.ds(0, planes - 1)], p_send.at[1])
    sent(pw2.at[pl.ds(0, zs - 1)], p_send.at[2])
    power = jnp.sum(jnp.sum(pw2[...], axis=0), axis=0, keepdims=True)
    power = jnp.sum(power, axis=1, keepdims=True)
    cells = depths * seq * zs * FEAT
    final = raw * lax.rsqrt(power * (1.0 / cells) + epsilon)
    out_ref[...] = final[0:FEAT].astype(BF16)


def sizes_of(mesh):
    depths, rows, zs = mesh.shape["depth"], mesh.shape["row"], mesh.shape["col"]
    los = 2
    return depths, los, rows // (2 * los), zs


def solution(mesh):
    depths, los, ys, zs = sizes_of(mesh)
    chips, planes = los * ys, depths * los * ys
    rows = chips * 2
    quarter = zs // 4
    dma = pltpu.SemaphoreType.DMA
    scratch = [
        *([pltpu.VMEM((FEAT, TOK), BF16)] * 6),
        pltpu.VMEM((FEAT,), BF16),
        pltpu.VMEM((zs, PAD, TOK), BF16),
        pltpu.VMEM((zs, PAD, TOK), BF16),
        pltpu.VMEM((los, ys, 2, PAD, SLOT), BF16),
        pltpu.VMEM((los, ys, 2, PAD, SLOT), BF16),
        pltpu.VMEM((los, ys, 2, TOK, SLOT), BF16),
        pltpu.VMEM((los, ys, 2, TOK, SLOT), BF16),
        pltpu.VMEM((rows, 8, SLOT), F32),
        pltpu.VMEM((PAD, TOK), F32),
        pltpu.VMEM((PAD, TOK), F32),
        pltpu.VMEM((PAD, TOK), F32),
        pltpu.VMEM((los, ys, 2, TOK, SLOT), F32),
        pltpu.VMEM((los, ys, 2, TOK, SLOT), F32),
        pltpu.VMEM((2, WIDE, chips * TOK), BF16),
        pltpu.VMEM((los, ys, 2, TOK, SLOT), BF16),
        pltpu.VMEM((rows // min(ys, 2), SLOT, min(ys, 2) * TOK), F32),
        pltpu.VMEM((rows // min(ys, 2), SLOT, min(ys, 2) * TOK), F32),
        pltpu.VMEM((SLOT, rows * TOK), BF16),
        pltpu.VMEM((SLOT, rows * TOK), BF16),
        *([pltpu.VMEM((2, quarter, PAD, TOK), BF16)] * 4),
        pltpu.VMEM((3, 8, TOK), F32),
        pltpu.VMEM((8, TOK), F32),
        pltpu.VMEM((planes, 8, TOK), F32),
        pltpu.VMEM((zs, 8, TOK), F32),
        dma((7,)),
        dma((2,)), dma((2, 2, 2, quarter)),
        dma((2, 3)), dma((2, ys + 1)), dma((2,)),
        dma((2, 3)), dma((2, los, ys)), dma((2,)),
        dma, dma,
        dma((2,)), dma((2, 2, quarter)),
        dma((3,)), dma((3,)),
    ]

    def shards(latents, out_grad, w_query, w_key, w_value, w_out, gain):
        return pl.pallas_call(
            functools.partial(kernel, (depths, los, ys, zs)),
            out_shape=jax.ShapeDtypeStruct((FEAT, TOK), BF16),
            in_specs=[pl.BlockSpec(memory_space=pl.ANY)] * 7,
            out_specs=pl.BlockSpec(memory_space=pltpu.VMEM),
            scratch_shapes=scratch,
            compiler_params=pltpu.CompilerParams(
                collective_id=0, has_side_effects=True, vmem_limit_bytes=56 * 1024 * 1024
            ),
        )(latents.T, out_grad.T, w_query, w_key, w_value, w_out, gain).T

    return jax.shard_map(
        shards,
        mesh=mesh,
        in_specs=(
            P(("depth", "row"), "col"),
            P(("depth", "row"), "col"),
            P("row", "col"),
            P("row", "col"),
            P("row", "col"),
            P("row", "col"),
            P("col"),
        ),
        out_specs=P(("depth", "row"), "col"),
        check_vma=False,
    )
```

```python
import functools

import jax
import jax.numpy as jnp
from jax import lax
from jax.experimental import pallas as pl
from jax.experimental.pallas import tpu as pltpu
from jax.sharding import PartitionSpec as P

MESH = pl.DeviceIdType.MESH
F32 = jnp.float32
BF16 = jnp.bfloat16
FEAT = 152
PAD = 160
HALF = 80
TOK = 128
WIDE = 128
HDIM = 64
SLOT = 256
epsilon = 1e-06


def dot_nt(a, b):
    return lax.dot_general(a, b, (((1,), (1,)), ((), ())), preferred_element_type=F32)


def dot_tn(a, b):
    return lax.dot_general(a, b, (((0,), (0,)), ((), ())), preferred_element_type=F32)


def dot_nn(a, b):
    return jnp.dot(a, b, preferred_element_type=F32)


def eye(rows, columns):
    at = lax.broadcasted_iota(jnp.int32, (rows, columns), 0)
    to = lax.broadcasted_iota(jnp.int32, (rows, columns), 1)
    return jnp.where(at == to, 1.0, 0.0).astype(BF16)


def kernel(
    sizes,
    lat_hbm, og_hbm, wq_hbm, wk_hbm, wv_hbm, wo_hbm, gain_hbm,
    out_ref,
    lat_ref, og_ref, wq_ref, wk_ref, wv_ref, wo_ref, gain_ref,
    xt_all, og_all, wkv_all, wqo_all, kv_all, qd_all, st_all,
    xt_own, og_own, gain_own,
    s_ref, dp_ref, kt_ref, ds_ref, s2_ref, dp2_ref,
    rs_leaf_tx, rs_hub_tx, rs_leaf, rs_hub,
    pw_tx, pw0, pw1, pw2,
    in_sem,
    z_send, z_recv,
    w_send, w_recv, wsib_recv,
    a_send, a_recv, asib_recv,
    st_send, st_recv,
    rs_send, rs_recv,
    p_send, p_recv,
):
    depths, los, ys, zs = sizes
    xs = depths * los
    chips = los * ys
    planes = xs * ys
    rows = chips * 2
    seq = rows * TOK
    quarter = zs // 4

    d = lax.axis_index("depth")
    r = lax.axis_index("row")
    c = lax.axis_index("col")
    core = lax.rem(r, 2)
    other = 1 - core
    chip = r // 2
    lo = chip // ys
    y = lax.rem(chip, ys)
    x = d * los + lo
    here = x * ys + y

    sibling = (d, chip * 2 + other, c)

    def z_at(by):
        return lax.rem(c + by % zs, zs)

    def z_device(by):
        return (d, r, z_at(by))

    def plane_device(at):
        to_x, to_y = at // ys, lax.rem(at, ys)
        return (to_x // los, (lax.rem(to_x, los) * ys + to_y) * 2 + core, c)

    def remote(src, dst, send, recv, device):
        return pltpu.make_async_remote_copy(
            src_ref=src, dst_ref=dst, send_sem=send, recv_sem=recv, device_id=device, device_id_type=MESH
        )

    inputs = (lat_hbm, og_hbm, gain_hbm, wk_hbm, wv_hbm, wq_hbm, wo_hbm)
    staged = (lat_ref, og_ref, gain_ref, wk_ref, wv_ref, wq_ref, wo_ref)
    fetches = [pltpu.make_async_copy(a, b, in_sem.at[i]) for i, (a, b) in enumerate(zip(inputs, staged))]
    for fetch in fetches:
        fetch.start()

    barrier = pltpu.get_barrier_semaphore()

    def greet(device):
        pl.semaphore_signal(barrier, inc=1, device_id=device, device_id_type=MESH)

    for by in sorted({by % zs for by in (1, -1, 2, -2)}):
        greet(z_device(by))
    greet(sibling)

    @pl.loop(1, planes)
    def _(i):
        greet(plane_device(lax.rem(here + i, planes)))

    for fetch in fetches:
        fetch.wait()

    row_at = lax.broadcasted_iota(jnp.int32, (PAD, TOK), 0)
    nothing = jnp.zeros((PAD - FEAT, WIDE), BF16)

    def padded(ref):
        return jnp.concatenate([ref[...], nothing], axis=0)

    og_all[c] = padded(og_ref)
    xt = padded(lat_ref).astype(F32)
    gain_wide = dot_nt(eye(PAD, FEAT) * gain_ref[...].reshape(1, FEAT), jnp.ones((TOK, FEAT), BF16))
    squares = jnp.sum(xt * xt, axis=0, keepdims=True)
    square_hi = squares.astype(BF16).astype(F32)
    rest = squares - square_hi
    square_mid = rest.astype(BF16).astype(F32)
    square_lo = rest - square_mid
    sent = xt * gain_wide
    sent = jnp.where(row_at == FEAT, square_hi, sent)
    sent = jnp.where(row_at == FEAT + 1, square_mid, sent)
    sent = jnp.where(row_at == FEAT + 2, square_lo, sent)
    xt_all[c] = sent.astype(BF16)
    xt_own[...] = xt
    og_own[...] = padded(og_ref).astype(F32)
    gain_own[...] = gain_wide
    wkv_all[lo, y, core] = jnp.concatenate([padded(wk_ref), padded(wv_ref)], axis=1)
    wqo_all[lo, y, core] = jnp.concatenate([padded(wq_ref), padded(wo_ref)], axis=1)

    pl.semaphore_wait(barrier, len({by % zs for by in (1, -1, 2, -2)}) + planes)

    streams = (xt_all, og_all)

    def tree(stream, side, leaf, k):
        sign = -1 if side else 1
        slot = streams[stream].at[z_at(-2 * k * sign)]
        to = z_device(sign if leaf else 2 * sign)
        return remote(slot, slot, z_send.at[stream], z_recv.at[stream, side, leaf, k], to)

    def tree_came(stream, side, leaf, k):
        sign = -1 if side else 1
        slot = streams[stream].at[z_at(-(2 * k + (1 if leaf else 2)) * sign)]
        remote(slot, slot, z_send.at[stream], z_recv.at[stream, side, leaf, k], sibling).wait_recv()

    def tree_round(stream, k):
        if k:
            tree_came(stream, 0, 0, k - 1)
        tree(stream, 0, 0, k).start()
        if k:
            tree(stream, 0, 1, k).start()
            tree_came(stream, 1, 0, k - 1)
        if k < quarter - 1:
            tree(stream, 1, 0, k).start()
        if not k:
            tree(stream, 0, 1, k).start()
        tree(stream, 1, 1, k).start()

    def tree_end(stream):
        tree_came(stream, 0, 0, quarter - 1)
        for k in range(quarter):
            tree_came(stream, 0, 1, k)
            tree_came(stream, 1, 1, k)

    def column_device(up):
        return (d, (lo * ys + lax.rem(y + up % ys, ys)) * 2 + core, c)

    def x_device(by):
        return plane_device(lax.rem(x + by % xs, xs) * ys + y)

    def y_at(up):
        return lax.rem(y + up % ys, ys)

    weights = (wkv_all, wqo_all)

    def weight_y(array, up, start, size, to):
        slot = weights[array].at[lo, y_at(up), core, pl.ds(start, size)]
        return remote(slot, slot, w_send.at[array, 0], w_recv.at[array, y_at(up)], column_device(to))

    def weight_y_came(array, up):
        weight_y(array, up, 0, PAD, 0).wait_recv()

    def weight_x(array, side):
        slot = weights[array].at[lo, :, core, pl.ds(side * HALF, HALF)]
        return remote(slot, slot, w_send.at[array, 1], w_recv.at[array, ys], x_device(-1 if side else 1))

    def weight_x_one(array, up):
        for side in range(2):
            slot = weights[array].at[lo, y_at(up), core, pl.ds(side * HALF, HALF)]
            to = x_device(-1 if side else 1)
            remote(slot, slot, w_send.at[array, 1], w_recv.at[array, ys], to).start()

    def weight_sibling(array, of_lo):
        slot = weights[array].at[of_lo, :, core]
        return remote(slot, slot, w_send.at[array, 2], wsib_recv.at[array], sibling)

    def weight_first(array):
        if ys == 4:
            weight_y(array, 0, 0, PAD, 1).start()
            weight_y(array, 0, 0, PAD, -1).start()
        elif ys == 2:
            weight_y(array, 0, 0, PAD, 1).start()

    def weight_near(array):
        if ys == 4:
            weight_y_came(array, -1)
            weight_y(array, -1, 0, HALF, 1).start()
            weight_y_came(array, 1)
            weight_y(array, 1, HALF, HALF, -1).start()
            if array == 0:
                weight_x_one(array, -1)
                weight_x_one(array, 1)
        elif ys == 2:
            weight_y_came(array, 1)
            if array == 0:
                weight_x_one(array, 1)

    def weight_column(array):
        if ys == 4:
            weight_y_came(array, 2)
            if array == 0:
                weight_x_one(array, 2)
        if array == 1:
            weight_x(array, 0).start()
            weight_x(array, 1).start()
        weight_sibling(array, lo).start()

    def weight_crossed(array):
        slot = weights[array].at[1 - lo, :, core]
        remote(slot, slot, w_send.at[array, 2], w_recv.at[array, ys], sibling).wait_recv()
        weight_sibling(array, 1 - lo).start()

    def weight_all(array):
        slot = weights[array].at[:, :, other]
        remote(slot, slot, w_send.at[array, 2], wsib_recv.at[array], sibling).wait_recv()

    def sent(ref, sem):
        remote(ref, ref, sem, p_recv.at[0], sibling).wait_send()

    tree_round(0, 0)
    weight_first(0)
    weight_x_one(0, 0)
    weight_first(1)
    for k in range(1, quarter):
        tree_round(0, k)
        if k == 1:
            weight_near(0)
        if k == 2:
            weight_column(0)
            weight_near(1)
    if quarter < 2:
        weight_near(0)
    tree_round(1, 0)
    if quarter < 3:
        weight_column(0)
        weight_near(1)
    weight_column(1)
    weight_crossed(0)
    tree_end(0)
    weight_all(0)
    if quarter > 1:
        tree_round(1, 1)

    tails = jnp.zeros((16, TOK), F32)
    for j in range(zs):
        tails = tails + xt_all[j, PAD - 16 : PAD, :].astype(F32)
    square_sum = jnp.sum(tails[8:16], axis=0, keepdims=True)
    scale_row = lax.rsqrt(square_sum * (1.0 / (zs * FEAT)) + epsilon)
    scale_wide = jnp.transpose(jnp.broadcast_to(scale_row, (TOK, TOK)))
    scale_two = jnp.concatenate([scale_wide, scale_wide], axis=1)
    pair = min(ys, 2)

    pairs = ys // pair

    def pair_at(n):
        return n // pairs, pl.ds(lax.rem(n, pairs) * pair, pair)

    def project(source, weight, lanes):
        width = lanes.stop - lanes.start

        def body(n, total):
            of_lo, of_ys = pair_at(n)
            a = source[pl.ds(n * 2 * pair, 2 * pair)].reshape(2 * pair * PAD, TOK)
            b = weight[of_lo, of_ys, :, :, lanes].reshape(2 * pair * PAD, width)
            return total + dot_tn(a, b)

        return lax.fori_loop(0, los * pairs, body, jnp.zeros((TOK, width), F32))

    gathered = (kv_all, qd_all)
    half = TOK // 2

    def column(across):
        return 1 - lo if across else lo

    def slot_x(array):
        slot = gathered[array].at[lo, y, core]
        to = (d, ((1 - lo) * ys + y) * 2 + core, c)
        return remote(slot, slot, a_send.at[array, 1], a_recv.at[array, lo, y], to)

    def slot_y(array, across, up, start, size, to):
        slot = gathered[array].at[column(across), y_at(up), core, pl.ds(start, size)]
        recv = a_recv.at[array, column(across), y_at(up)]
        return remote(slot, slot, a_send.at[array, 0], recv, column_device(to))

    def slot_came(array, across, up):
        slot_y(array, across, up, 0, TOK, 0).wait_recv()

    def slot_out(array, across):
        if across:
            slot_came(array, 1, 0)
        if ys == 4:
            slot_y(array, across, 0, 0, TOK, 1).start()
            slot_y(array, across, 0, 0, TOK, -1).start()
        elif ys == 2:
            slot_y(array, across, 0, 0, TOK, 1).start()

    def slot_start(array):
        slot_x(array).start()
        slot_out(array, 0)

    def slot_near(array, across):
        if ys == 4:
            slot_came(array, across, -1)
            slot_y(array, across, -1, 0, half, 1).start()
            slot_came(array, across, 1)
            slot_y(array, across, 1, half, half, -1).start()
        elif ys == 2:
            slot_came(array, across, 1)

    def slot_far(array, across):
        if ys == 4:
            slot_came(array, across, 2)
        slot = gathered[array].at[column(across), :, core]
        remote(slot, slot, a_send.at[array, 2], asib_recv.at[array], sibling).start()

    def slot_all(array):
        slot = gathered[array].at[:, :, other]
        remote(slot, slot, a_send.at[array, 2], asib_recv.at[array], sibling).wait_recv()

    kv = (project(xt_all, wkv_all, slice(0, SLOT)) * scale_two).astype(BF16)
    kv_all[lo, y, core] = kv
    slot_start(0)
    weight_crossed(1)
    if quarter > 2:
        tree_round(1, 2)
    weight_all(1)
    queries = (project(xt_all, wqo_all, slice(0, WIDE)) * scale_wide).astype(BF16)
    slot_out(0, 1)
    slot_near(0, 0)
    if quarter > 3:
        tree_round(1, 3)
    slot_near(0, 1)
    slot_far(0, 0)
    tree_end(1)
    out_dir = project(og_all, wqo_all, slice(WIDE, SLOT)).astype(BF16)
    scaled_queries = (queries.astype(F32) * 0.125).astype(BF16)
    qd_all[lo, y, core] = jnp.concatenate([scaled_queries, out_dir], axis=1)
    slot_start(1)
    slot_far(0, 1)
    low = lax.broadcasted_iota(jnp.int32, (TOK, WIDE), 1) < HDIM

    def stacked(a):
        wide = a.astype(F32)
        parts = [jnp.where(low, wide, 0.0), jnp.where(low, 0.0, wide)]
        return jnp.concatenate(parts, axis=0).astype(BF16)

    query_stack = stacked(scaled_queries)
    dir_stack = stacked(out_dir)

    def slots_of(ref, parity, lanes):
        return ref[:, :, parity, :, lanes].reshape(chips * TOK, lanes.stop - lanes.start)

    def scores_of(parity):
        keys = slots_of(kv_all, parity, slice(0, WIDE))
        scores = dot_nt(keys, query_stack)
        s_ref[:, :, parity] = scores.reshape(los, ys, TOK, SLOT)
        prob_grad = dot_nt(slots_of(kv_all, parity, slice(WIDE, SLOT)), dir_stack)
        dp_ref[:, :, parity] = prob_grad.reshape(los, ys, TOK, SLOT)
        kt_ref[parity] = jnp.transpose(keys)
        return jnp.max(scores.reshape(chips * TOK // 8, 8, SLOT), axis=0)

    most = scores_of(core)
    slot_out(1, 1)
    slot_near(1, 0)
    slot_all(0)
    most = jnp.max(jnp.maximum(most, scores_of(other)), axis=0, keepdims=True)
    slot_near(1, 1)
    slot_far(1, 0)

    def tile_at(i):
        return i // (2 * ys), lax.rem(i // 2, ys), lax.rem(i, 2)

    def folded(a):
        return jnp.sum(a.reshape(TOK // 8, 8, SLOT), axis=0)

    def expo_body(i, sums):
        at = tile_at(i)
        expo = jnp.exp(s_ref[at] - most)
        s_ref[at] = expo
        return sums[0] + folded(expo), sums[1] + folded(expo * dp_ref[at])

    zero = jnp.zeros((8, SLOT), F32)
    totals, delta = lax.fori_loop(0, rows, expo_body, (zero, zero), unroll=2)
    totals = jnp.sum(totals, axis=0, keepdims=True)
    inverse = 1.0 / totals
    delta = jnp.sum(delta, axis=0, keepdims=True) * inverse
    slot_far(1, 1)

    def stat_copy(i):
        to = lax.rem(r + i, rows)
        return remote(st_all.at[r], st_all.at[r], st_send, st_recv, (d, to, c))

    def small_came(ref, count, sem):
        some = ref.at[pl.ds(0, count)]
        remote(some, some, p_send.at[0], sem, sibling).wait_recv()

    st_all[r] = jnp.concatenate([most + jnp.log(totals), delta, jnp.zeros((6, SLOT), F32)], axis=0)

    @pl.loop(1, rows)
    def _(i):
        stat_copy(i).start()

    def score_grad_body(i, nothing):
        at = tile_at(i)
        ds_ref[at] = (s_ref[at] * (dp_ref[at] - delta)).astype(BF16)
        return nothing

    lax.fori_loop(0, rows, score_grad_body, 0, unroll=2)
    query_grad = jnp.zeros((WIDE, SLOT), F32)
    for parity in range(2):
        query_grad = query_grad + dot_nn(kt_ref[parity], slots_of(ds_ref, parity, slice(0, SLOT)))
    query_grad = query_grad * (inverse * 0.125)
    query_grad = jnp.concatenate([query_grad[0:HDIM, 0:TOK], query_grad[HDIM:WIDE, TOK:SLOT]], axis=0)
    query_grad = query_grad.astype(BF16)

    key_stack = stacked(kv[:, 0:WIDE])
    value_stack = stacked(kv[:, WIDE:SLOT])
    wide = pair * TOK
    blocks = los * pairs
    parities = (core, other)

    def block_of(n, parity):
        of_lo, of_ys = pair_at(n)
        return qd_all[of_lo, of_ys, parity].reshape(wide, SLOT)

    def own_scores(side):
        @pl.loop(0, blocks)
        def _(n):
            block = block_of(n, parities[side])
            s2_ref[side * blocks + n] = dot_nt(key_stack, block[:, 0:WIDE])
            dp2_ref[side * blocks + n] = dot_nt(value_stack, block[:, WIDE:SLOT])

    own_scores(0)
    slot_all(1)
    own_scores(1)
    small_came(st_all, rows - 1, st_recv)

    def key_body(at, grads):
        parity = jnp.where(at < blocks, core, other)
        n = lax.rem(at, blocks)
        first = (n // pairs) * ys + lax.rem(n, pairs) * pair
        stats = [st_all[(first + i) * 2 + parity] for i in range(pair)]
        probs, score_grad = [], []
        for head in range(2):
            part = slice(head * TOK, (head + 1) * TOK)
            total = jnp.concatenate([stat[0:1, part] for stat in stats], axis=1)
            shift = jnp.concatenate([stat[1:2, part] for stat in stats], axis=1)
            prob = jnp.exp(s2_ref[at, part] - total)
            probs.append(prob.astype(BF16))
            score_grad.append((prob * (dp2_ref[at, part] - shift)).astype(BF16))
        block = block_of(n, parity)
        key_grad = grads[0] + dot_nn(jnp.concatenate(score_grad, axis=0), block[:, 0:WIDE])
        value_grad = grads[1] + dot_nn(jnp.concatenate(probs, axis=0), block[:, WIDE:SLOT])
        return key_grad, value_grad

    zero = jnp.zeros((SLOT, WIDE), F32)
    key_grad, value_grad = lax.fori_loop(0, 2 * blocks, key_body, (zero, zero))
    key_grad = jnp.where(low, key_grad[0:TOK], key_grad[TOK:SLOT])
    value_grad = jnp.where(low, value_grad[0:TOK], value_grad[TOK:SLOT])
    kv_grad = jnp.concatenate([key_grad, value_grad], axis=1)
    turned = jnp.concatenate([jnp.transpose(key_grad), jnp.transpose(value_grad)], axis=0).astype(BF16)
    kv_grad = kv_grad.astype(BF16)
    grads_turned = jnp.concatenate([turned, query_grad], axis=0)

    queries_turned = dot_nt(eye(WIDE, WIDE), queries)
    inner = jnp.sum(query_grad.astype(F32) * queries_turned, axis=0, keepdims=True)
    kv_inner = kv_grad.astype(F32) * kv.astype(F32)
    kv_hi = kv_inner.astype(BF16)
    kv_lo = (kv_inner - kv_hi.astype(F32)).astype(BF16)
    ones = jnp.ones((8, SLOT), BF16)
    kv_inner = dot_nt(ones, kv_hi) + dot_nt(ones, kv_lo)
    inner = inner + kv_inner[0:1]

    def partials(places):
        slots = []
        for by in places:
            j = lax.rem(c + by + zs, zs)
            at = (j // (2 * ys), lax.rem(j // 2, ys), lax.rem(j, 2))
            slots.append(jnp.concatenate([wkv_all[at], wqo_all[at + (slice(None), slice(0, WIDE))]], axis=1))
        value = dot_nn(jnp.concatenate(slots, axis=0), grads_turned)
        parts = [value[i * PAD : (i + 1) * PAD] for i in range(len(places))]
        return [jnp.where(row_at == FEAT, inner, part) for part in parts]

    some = pl.ds(0, zs - 1)
    for i in range(2):
        sent(streams[i].at[some], z_send.at[i])
        for group, sems, x_slots in ((weights[i], w_send, slice(0, ys)), (gathered[i], a_send, slice(0, 1))):
            if ys > 1:
                columns = slice(0, 1) if group is weights[i] else slice(0, 2)
                sent(group.at[columns, pl.ds(0, ys - 1), 0], sems.at[i, 0])
            sent(group.at[0, x_slots, 0], sems.at[i, 1])
            sent(group.at[:, :, 0], sems.at[i, 2])

    sent(st_all.at[pl.ds(0, rows - 1)], st_send)

    far = 2 * quarter

    def rs_leaf_copy(side, m):
        to = z_device(-1 if side else 1)
        return remote(rs_leaf_tx.at[side, m], rs_leaf.at[side, m + 1], rs_send.at[side], rs_recv.at[side, 1, m], to)

    def rs_hub_copy(side, k):
        to = z_device(-2 if side else 2)
        return remote(rs_hub_tx.at[side, k], rs_hub.at[side, k + 1], rs_send.at[side], rs_recv.at[side, 0, k], to)

    for side in range(2):
        rs_hub[side, 0] = jnp.zeros((PAD, TOK), BF16)
        rs_leaf[side, 0] = jnp.zeros((PAD, TOK), BF16)

    @pl.loop(0, quarter)
    def _(k):
        by = far - 2 * k
        to_right, to_left, right_part, left_part = partials([by, -by, by - 1, 1 - by])

        @pl.when(k > 0)
        def _():
            rs_hub_copy(0, k - 1).wait_recv()
            rs_leaf_copy(0, k - 1).wait_recv()

        total = to_right + rs_hub[0, k].astype(F32) + rs_leaf[0, k].astype(F32)
        rs_hub_tx[0, k] = total.astype(BF16)
        rs_hub_copy(0, k).start()
        rs_leaf_tx[0, k] = right_part.astype(BF16)
        rs_leaf_tx[1, k] = left_part.astype(BF16)

        @pl.when(k > 0)
        def _():
            rs_leaf_copy(1, k - 1).wait_recv()

            @pl.when(k > 1)
            def _():
                rs_hub_copy(1, k - 2).wait_recv()

            total = to_left + rs_leaf[1, k].astype(F32) + rs_hub[1, k - 1].astype(F32)
            rs_hub_tx[1, k - 1] = total.astype(BF16)
            rs_hub_copy(1, k - 1).start()

        rs_leaf_copy(0, k).start()
        rs_leaf_copy(1, k).start()

    own = partials([0])[0]
    for side in range(2):
        last = quarter - 1 - side
        rs_leaf_copy(side, quarter - 1).wait_recv()
        own = own + rs_leaf[side, quarter].astype(F32)
        if last >= 0:
            rs_hub_copy(side, last).wait_recv()
            own = own + rs_hub[side, last + 1].astype(F32)

    inner = own[FEAT : FEAT + 1] * (1.0 / (zs * FEAT))
    scaled = own * gain_own[...]
    normalized = xt_own[...] * scale_row
    raw = og_own[...] + scale_row * (scaled - normalized * inner)
    power = jnp.sum((raw * raw).reshape(PAD // 8, 8, TOK), axis=0)

    def power_sibling():
        return remote(pw_tx.at[0], pw0, p_send.at[0], p_recv.at[0], sibling)

    def power_plane(i):
        to = plane_device(lax.rem(here + i, planes))
        return remote(pw_tx.at[1], pw1.at[here], p_send.at[1], p_recv.at[1], to)

    def power_col(i):
        return remote(pw_tx.at[2], pw2.at[c], p_send.at[2], p_recv.at[2], (d, r, lax.rem(c + i, zs)))

    pw_tx[0] = power
    power_sibling().start()
    power_sibling().wait_recv()
    power = power + pw0[...]
    pw_tx[1] = power
    pw1[here] = power

    @pl.loop(1, planes)
    def _(i):
        power_plane(i).start()

    small_came(pw1, planes - 1, p_recv.at[1])

    sent(xt_all.at[pl.ds(0, far)], rs_send.at[0])
    sent(xt_all.at[pl.ds(0, far - 1)], rs_send.at[1])
    power = jnp.sum(pw1[...], axis=0)
    pw_tx[2] = power
    pw2[c] = power

    @pl.loop(1, zs)
    def _(i):
        power_col(i).start()

    small_came(pw2, zs - 1, p_recv.at[2])

    power_sibling().wait_send()
    sent(pw1.at[pl.ds(0, planes - 1)], p_send.at[1])
    sent(pw2.at[pl.ds(0, zs - 1)], p_send.at[2])
    power = jnp.sum(jnp.sum(pw2[...], axis=0), axis=0, keepdims=True)
    power = jnp.sum(power, axis=1, keepdims=True)
    cells = depths * seq * zs * FEAT
    final = raw * lax.rsqrt(power * (1.0 / cells) + epsilon)
    out_ref[...] = final[0:FEAT].astype(BF16)


def sizes_of(mesh):
    depths, rows, zs = mesh.shape["depth"], mesh.shape["row"], mesh.shape["col"]
    los = 2
    return depths, los, rows // (2 * los), zs


def solution(mesh):
    depths, los, ys, zs = sizes_of(mesh)
    chips, planes = los * ys, depths * los * ys
    rows = chips * 2
    quarter = zs // 4
    dma = pltpu.SemaphoreType.DMA
    scratch = [
        *([pltpu.VMEM((FEAT, TOK), BF16)] * 6),
        pltpu.VMEM((FEAT,), BF16),
        pltpu.VMEM((zs, PAD, TOK), BF16),
        pltpu.VMEM((zs, PAD, TOK), BF16),
        pltpu.VMEM((los, ys, 2, PAD, SLOT), BF16),
        pltpu.VMEM((los, ys, 2, PAD, SLOT), BF16),
        pltpu.VMEM((los, ys, 2, TOK, SLOT), BF16),
        pltpu.VMEM((los, ys, 2, TOK, SLOT), BF16),
        pltpu.VMEM((rows, 8, SLOT), F32),
        pltpu.VMEM((PAD, TOK), F32),
        pltpu.VMEM((PAD, TOK), F32),
        pltpu.VMEM((PAD, TOK), F32),
        pltpu.VMEM((los, ys, 2, TOK, SLOT), F32),
        pltpu.VMEM((los, ys, 2, TOK, SLOT), F32),
        pltpu.VMEM((2, WIDE, chips * TOK), BF16),
        pltpu.VMEM((los, ys, 2, TOK, SLOT), BF16),
        pltpu.VMEM((rows // min(ys, 2), SLOT, min(ys, 2) * TOK), F32),
        pltpu.VMEM((rows // min(ys, 2), SLOT, min(ys, 2) * TOK), F32),
        *([pltpu.VMEM((2, quarter, PAD, TOK), BF16)] * 2),
        *([pltpu.VMEM((2, quarter + 1, PAD, TOK), BF16)] * 2),
        pltpu.VMEM((3, 8, TOK), F32),
        pltpu.VMEM((8, TOK), F32),
        pltpu.VMEM((planes, 8, TOK), F32),
        pltpu.VMEM((zs, 8, TOK), F32),
        dma((7,)),
        dma((2,)), dma((2, 2, 2, quarter)),
        dma((2, 3)), dma((2, ys + 1)), dma((2,)),
        dma((2, 3)), dma((2, los, ys)), dma((2,)),
        dma, dma,
        dma((2,)), dma((2, 2, quarter)),
        dma((3,)), dma((3,)),
    ]

    def shards(latents, out_grad, w_query, w_key, w_value, w_out, gain):
        return pl.pallas_call(
            functools.partial(kernel, (depths, los, ys, zs)),
            out_shape=jax.ShapeDtypeStruct((FEAT, TOK), BF16),
            in_specs=[pl.BlockSpec(memory_space=pl.ANY)] * 7,
            out_specs=pl.BlockSpec(memory_space=pltpu.VMEM),
            scratch_shapes=scratch,
            compiler_params=pltpu.CompilerParams(
                collective_id=0, has_side_effects=True, vmem_limit_bytes=56 * 1024 * 1024
            ),
        )(latents.T, out_grad.T, w_query, w_key, w_value, w_out, gain).T

    return jax.shard_map(
        shards,
        mesh=mesh,
        in_specs=(
            P(("depth", "row"), "col"),
            P(("depth", "row"), "col"),
            P("row", "col"),
            P("row", "col"),
            P("row", "col"),
            P("row", "col"),
            P("col"),
        ),
        out_specs=P(("depth", "row"), "col"),
        check_vma=False,
    )
```

```python
import functools

import jax
import jax.numpy as jnp
from jax import lax
from jax.experimental import pallas as pl
from jax.experimental.pallas import tpu as pltpu
from jax.sharding import PartitionSpec as P

MESH = pl.DeviceIdType.MESH
F32 = jnp.float32
BF16 = jnp.bfloat16
FEAT = 152
PAD = 160
HALF = 80
TOK = 128
WIDE = 128
HDIM = 64
SLOT = 256
epsilon = 1e-06


def dot_nt(a, b):
    return lax.dot_general(a, b, (((1,), (1,)), ((), ())), preferred_element_type=F32)


def dot_tn(a, b):
    return lax.dot_general(a, b, (((0,), (0,)), ((), ())), preferred_element_type=F32)


def dot_nn(a, b):
    return jnp.dot(a, b, preferred_element_type=F32)


def eye(rows, columns):
    at = lax.broadcasted_iota(jnp.int32, (rows, columns), 0)
    to = lax.broadcasted_iota(jnp.int32, (rows, columns), 1)
    return jnp.where(at == to, 1.0, 0.0).astype(BF16)


def kernel(
    sizes,
    lat_hbm, og_hbm, wq_hbm, wk_hbm, wv_hbm, wo_hbm, gain_hbm,
    out_ref,
    lat_ref, og_ref, wq_ref, wk_ref, wv_ref, wo_ref, gain_ref,
    xt_all, og_all, wkv_all, wqo_all, kv_all, qd_all, st_all,
    xt_own, og_own, gain_own,
    s_ref, dp_ref, kt_ref, ds_ref, s2_ref, dp2_ref, p2_ref, ds2_ref,
    rs_leaf_tx, rs_hub_tx, rs_leaf, rs_hub,
    pw_tx, pw1, pw2,
    in_sem,
    z_send, z_recv,
    w_send, w_recv, wsib_recv,
    a_send, a_recv, asib_recv,
    st_send, st_recv,
    rs_send, rs_recv,
    p_send, p_recv,
):
    depths, los, ys, zs = sizes
    xs = depths * los
    chips = los * ys
    planes = xs * ys
    rows = chips * 2
    seq = rows * TOK
    quarter = zs // 4

    d = lax.axis_index("depth")
    r = lax.axis_index("row")
    c = lax.axis_index("col")
    core = lax.rem(r, 2)
    other = 1 - core
    chip = r // 2
    lo = chip // ys
    y = lax.rem(chip, ys)
    x = d * los + lo
    here = x * ys + y

    sibling = (d, chip * 2 + other, c)

    def z_at(by):
        return lax.rem(c + by % zs, zs)

    def z_device(by):
        return (d, r, z_at(by))

    def plane_device(at):
        to_x, to_y = at // ys, lax.rem(at, ys)
        return (to_x // los, (lax.rem(to_x, los) * ys + to_y) * 2 + core, c)

    def remote(src, dst, send, recv, device):
        return pltpu.make_async_remote_copy(
            src_ref=src, dst_ref=dst, send_sem=send, recv_sem=recv, device_id=device, device_id_type=MESH
        )

    inputs = (lat_hbm, og_hbm, gain_hbm, wk_hbm, wv_hbm, wq_hbm, wo_hbm)
    staged = (lat_ref, og_ref, gain_ref, wk_ref, wv_ref, wq_ref, wo_ref)
    fetches = [pltpu.make_async_copy(a, b, in_sem.at[i]) for i, (a, b) in enumerate(zip(inputs, staged))]
    for fetch in fetches:
        fetch.start()

    barrier = pltpu.get_barrier_semaphore()

    def greet(device):
        pl.semaphore_signal(barrier, inc=1, device_id=device, device_id_type=MESH)

    for by in sorted({by % zs for by in (1, -1, 2, -2)}):
        greet(z_device(by))
    greet(sibling)

    @pl.loop(1, planes)
    def _(i):
        greet(plane_device(lax.rem(here + i, planes)))

    fetches[0].wait()
    fetches[2].wait()

    row_at = lax.broadcasted_iota(jnp.int32, (PAD, TOK), 0)
    nothing = jnp.zeros((PAD - FEAT, WIDE), BF16)

    def padded(ref):
        return jnp.concatenate([ref[...], nothing], axis=0)

    xt = padded(lat_ref).astype(F32)
    gain_wide = dot_nt(eye(PAD, FEAT) * gain_ref[...].reshape(1, FEAT), jnp.ones((TOK, FEAT), BF16))
    squares = jnp.sum(xt * xt, axis=0, keepdims=True)
    square_hi = squares.astype(BF16).astype(F32)
    rest = squares - square_hi
    square_mid = rest.astype(BF16).astype(F32)
    square_lo = rest - square_mid
    sent = xt * gain_wide
    sent = jnp.where(row_at == FEAT, square_hi, sent)
    sent = jnp.where(row_at == FEAT + 1, square_mid, sent)
    sent = jnp.where(row_at == FEAT + 2, square_lo, sent)
    xt_all[c] = sent.astype(BF16)
    xt_own[...] = xt
    gain_own[...] = gain_wide
    pl.semaphore_wait(barrier, len({by % zs for by in (1, -1, 2, -2)}) + planes)

    streams = (xt_all, og_all)

    def tree(stream, side, leaf, k):
        sign = -1 if side else 1
        slot = streams[stream].at[z_at(-2 * k * sign)]
        to = z_device(sign if leaf else 2 * sign)
        return remote(slot, slot, z_send.at[stream], z_recv.at[stream, side, leaf, k], to)

    def tree_came(stream, side, leaf, k):
        sign = -1 if side else 1
        slot = streams[stream].at[z_at(-(2 * k + (1 if leaf else 2)) * sign)]
        remote(slot, slot, z_send.at[stream], z_recv.at[stream, side, leaf, k], sibling).wait_recv()

    def tree_round(stream, k):
        if k:
            tree_came(stream, 0, 0, k - 1)
        tree(stream, 0, 0, k).start()
        if k:
            tree(stream, 0, 1, k).start()
            tree_came(stream, 1, 0, k - 1)
        if k < quarter - 1:
            tree(stream, 1, 0, k).start()
        if not k:
            tree(stream, 0, 1, k).start()
        tree(stream, 1, 1, k).start()

    def tree_end(stream):
        tree_came(stream, 0, 0, quarter - 1)
        for k in range(quarter):
            tree_came(stream, 0, 1, k)
            tree_came(stream, 1, 1, k)

    def column_device(up):
        return (d, (lo * ys + lax.rem(y + up % ys, ys)) * 2 + core, c)

    def x_device(by):
        return plane_device(lax.rem(x + by % xs, xs) * ys + y)

    def y_at(up):
        return lax.rem(y + up % ys, ys)

    weights = (wkv_all, wqo_all)

    def weight_y(array, up, start, size, to):
        slot = weights[array].at[lo, y_at(up), core, pl.ds(start, size)]
        return remote(slot, slot, w_send.at[array, 0], w_recv.at[array, y_at(up)], column_device(to))

    def weight_y_came(array, up):
        weight_y(array, up, 0, PAD, 0).wait_recv()

    def weight_x(array, side):
        slot = weights[array].at[lo, :, core, pl.ds(side * HALF, HALF)]
        return remote(slot, slot, w_send.at[array, 1], w_recv.at[array, ys], x_device(-1 if side else 1))

    def weight_x_one(array, up):
        for side in range(2):
            slot = weights[array].at[lo, y_at(up), core, pl.ds(side * HALF, HALF)]
            to = x_device(-1 if side else 1)
            remote(slot, slot, w_send.at[array, 1], w_recv.at[array, ys], to).start()

    def weight_sibling(array, of_lo):
        slot = weights[array].at[of_lo, :, core]
        return remote(slot, slot, w_send.at[array, 2], wsib_recv.at[array], sibling)

    def weight_first(array):
        if ys == 4:
            weight_y(array, 0, 0, PAD, 1).start()
            weight_y(array, 0, 0, PAD, -1).start()
        elif ys == 2:
            weight_y(array, 0, 0, PAD, 1).start()

    def weight_near(array):
        if ys == 4:
            weight_y_came(array, -1)
            weight_y(array, -1, 0, HALF, 1).start()
            weight_y_came(array, 1)
            weight_y(array, 1, HALF, HALF, -1).start()
            if array == 0:
                weight_x_one(array, -1)
                weight_x_one(array, 1)
        elif ys == 2:
            weight_y_came(array, 1)
            if array == 0:
                weight_x_one(array, 1)

    def weight_column(array):
        if ys == 4:
            weight_y_came(array, 2)
            if array == 0:
                weight_x_one(array, 2)
        if array == 1:
            weight_x(array, 0).start()
            weight_x(array, 1).start()
        weight_sibling(array, lo).start()

    def weight_crossed(array):
        slot = weights[array].at[1 - lo, :, core]
        remote(slot, slot, w_send.at[array, 2], w_recv.at[array, ys], sibling).wait_recv()
        weight_sibling(array, 1 - lo).start()

    def weight_all(array):
        slot = weights[array].at[:, :, other]
        remote(slot, slot, w_send.at[array, 2], wsib_recv.at[array], sibling).wait_recv()

    def sent(ref, sem):
        remote(ref, ref, sem, p_recv.at[0], sibling).wait_send()

    tree_round(0, 0)
    fetches[3].wait()
    fetches[4].wait()
    wkv_all[lo, y, core] = jnp.concatenate([padded(wk_ref), padded(wv_ref)], axis=1)
    weight_first(0)
    weight_x_one(0, 0)
    for i in (1, 5, 6):
        fetches[i].wait()
    wqo_all[lo, y, core] = jnp.concatenate([padded(wq_ref), padded(wo_ref)], axis=1)
    og_own[...] = padded(og_ref).astype(F32)
    og_all[c] = padded(og_ref)
    for k in range(1, quarter):
        tree_round(0, k)
        if k == 1:
            weight_near(0)
        if k == 2:
            weight_column(0)
    if quarter < 2:
        weight_near(0)
    if quarter < 3:
        weight_column(0)
    weight_first(1)
    tree_round(1, 0)
    weight_crossed(0)
    tree_end(0)
    weight_near(1)
    weight_all(0)
    if quarter > 1:
        tree_round(1, 1)

    tails = jnp.zeros((16, TOK), F32)
    for j in range(zs):
        tails = tails + xt_all[j, PAD - 16 : PAD, :].astype(F32)
    square_sum = jnp.sum(tails[8:16], axis=0, keepdims=True)
    scale_row = lax.rsqrt(square_sum * (1.0 / (zs * FEAT)) + epsilon)
    scale_wide = jnp.transpose(jnp.broadcast_to(scale_row, (TOK, TOK)))
    scale_two = jnp.concatenate([scale_wide, scale_wide], axis=1)
    pair = min(ys, 2)

    def project(source, weight, lanes):
        total = None
        for of_lo in range(los):
            for of_y in range(0, ys, pair):
                first = (of_lo * ys + of_y) * 2
                a = source[first : first + 2 * pair].reshape(2 * pair * PAD, TOK)
                b = weight[of_lo, of_y : of_y + pair, :, :, lanes]
                term = dot_tn(a, b.reshape(2 * pair * PAD, b.shape[-1]))
                total = term if total is None else total + term
        return total

    gathered = (kv_all, qd_all)
    half = TOK // 2

    def column(across):
        return 1 - lo if across else lo

    def slot_x(array):
        slot = gathered[array].at[lo, y, core]
        to = (d, ((1 - lo) * ys + y) * 2 + core, c)
        return remote(slot, slot, a_send.at[array, 1], a_recv.at[array, lo, y], to)

    def slot_y(array, across, up, start, size, to):
        slot = gathered[array].at[column(across), y_at(up), core, pl.ds(start, size)]
        recv = a_recv.at[array, column(across), y_at(up)]
        return remote(slot, slot, a_send.at[array, 0], recv, column_device(to))

    def slot_came(array, across, up):
        slot_y(array, across, up, 0, TOK, 0).wait_recv()

    def slot_out(array, across):
        if across:
            slot_came(array, 1, 0)
        if ys == 4:
            slot_y(array, across, 0, 0, TOK, 1).start()
            slot_y(array, across, 0, 0, TOK, -1).start()
        elif ys == 2:
            slot_y(array, across, 0, 0, TOK, 1).start()

    def slot_start(array):
        slot_x(array).start()
        slot_out(array, 0)

    def slot_near(array, across):
        if ys == 4:
            slot_came(array, across, -1)
            slot_y(array, across, -1, 0, half, 1).start()
            slot_came(array, across, 1)
            slot_y(array, across, 1, half, half, -1).start()
        elif ys == 2:
            slot_came(array, across, 1)

    def slot_far(array, across):
        if ys == 4:
            slot_came(array, across, 2)
        slot = gathered[array].at[column(across), :, core]
        remote(slot, slot, a_send.at[array, 2], asib_recv.at[array], sibling).start()

    def slot_all(array):
        slot = gathered[array].at[:, :, other]
        remote(slot, slot, a_send.at[array, 2], asib_recv.at[array], sibling).wait_recv()

    kv = (project(xt_all, wkv_all, slice(0, SLOT)) * scale_two).astype(BF16)
    kv_all[lo, y, core] = kv
    slot_start(0)
    weight_column(1)
    if quarter > 2:
        tree_round(1, 2)
    slot_out(0, 1)
    slot_near(0, 0)
    weight_crossed(1)
    if quarter > 3:
        tree_round(1, 3)
    slot_near(0, 1)
    weight_all(1)
    queries = (project(xt_all, wqo_all, slice(0, WIDE)) * scale_wide).astype(BF16)
    slot_far(0, 0)
    tree_end(1)
    out_dir = project(og_all, wqo_all, slice(WIDE, SLOT)).astype(BF16)
    scaled_queries = (queries.astype(F32) * 0.125).astype(BF16)
    qd_all[lo, y, core] = jnp.concatenate([scaled_queries, out_dir], axis=1)
    slot_start(1)
    slot_far(0, 1)
    low = lax.broadcasted_iota(jnp.int32, (TOK, WIDE), 1) < HDIM

    def stacked(a):
        wide = a.astype(F32)
        parts = [jnp.where(low, wide, 0.0), jnp.where(low, 0.0, wide)]
        return jnp.concatenate(parts, axis=0).astype(BF16)

    query_stack = stacked(scaled_queries)
    dir_stack = stacked(out_dir)

    def slots_of(ref, parity, lanes):
        return ref[:, :, parity, :, lanes].reshape(chips * TOK, lanes.stop - lanes.start)

    def scores_of(parity):
        keys = slots_of(kv_all, parity, slice(0, WIDE))
        scores = dot_nt(keys, query_stack)
        s_ref[:, :, parity] = scores.reshape(los, ys, TOK, SLOT)
        prob_grad = dot_nt(slots_of(kv_all, parity, slice(WIDE, SLOT)), dir_stack)
        dp_ref[:, :, parity] = prob_grad.reshape(los, ys, TOK, SLOT)
        kt_ref[parity] = jnp.transpose(keys)
        return jnp.max(scores.reshape(chips * TOK // 8, 8, SLOT), axis=0)

    most = scores_of(core)
    slot_out(1, 1)
    slot_near(1, 0)
    slot_all(0)
    most = jnp.max(jnp.maximum(most, scores_of(other)), axis=0, keepdims=True)
    slot_near(1, 1)
    slot_far(1, 0)

    def tile_at(i):
        return i // (2 * ys), lax.rem(i // 2, ys), lax.rem(i, 2)

    def folded(a):
        return jnp.sum(a.reshape(TOK // 8, 8, SLOT), axis=0)

    def expo_body(i, sums):
        at = tile_at(i)
        expo = jnp.exp(s_ref[at] - most)
        s_ref[at] = expo
        return sums[0] + folded(expo), sums[1] + folded(expo * dp_ref[at])

    zero = jnp.zeros((8, SLOT), F32)
    totals, delta = lax.fori_loop(0, rows, expo_body, (zero, zero), unroll=2)
    totals = jnp.sum(totals, axis=0, keepdims=True)
    inverse = 1.0 / totals
    delta = jnp.sum(delta, axis=0, keepdims=True) * inverse
    slot_far(1, 1)

    def stat_copy(i):
        to = lax.rem(r + i, rows)
        return remote(st_all.at[r], st_all.at[r], st_send, st_recv, (d, to, c))

    def small_came(ref, count, sem):
        some = ref.at[pl.ds(0, count)]
        remote(some, some, p_send.at[1], sem, sibling).wait_recv()

    st_all[r] = jnp.concatenate([most + jnp.log(totals), delta, jnp.zeros((6, SLOT), F32)], axis=0)

    @pl.loop(1, rows)
    def _(i):
        stat_copy(i).start()

    def score_grad_body(i, nothing):
        at = tile_at(i)
        ds_ref[at] = (s_ref[at] * (dp_ref[at] - delta)).astype(BF16)
        return nothing

    lax.fori_loop(0, rows, score_grad_body, 0, unroll=2)
    query_grad = jnp.zeros((WIDE, SLOT), F32)
    for parity in range(2):
        query_grad = query_grad + dot_nn(kt_ref[parity], slots_of(ds_ref, parity, slice(0, SLOT)))
    query_grad = query_grad * (inverse * 0.125)
    query_grad = jnp.concatenate([query_grad[0:HDIM, 0:TOK], query_grad[HDIM:WIDE, TOK:SLOT]], axis=0)
    query_grad = query_grad.astype(BF16)

    key_stack = stacked(kv[:, 0:WIDE])
    value_stack = stacked(kv[:, WIDE:SLOT])
    wide = pair * TOK
    blocks = [(of_lo, of_y) for of_lo in range(los) for of_y in range(0, ys, pair)]
    parities = (core, other)

    def own_scores(side):
        for n, (of_lo, of_y) in enumerate(blocks):
            block = qd_all[of_lo, of_y : of_y + pair, parities[side]].reshape(wide, SLOT)
            s2_ref[side * len(blocks) + n] = dot_nt(key_stack, block[:, 0:WIDE])
            dp2_ref[side * len(blocks) + n] = dot_nt(value_stack, block[:, WIDE:SLOT])

    own_scores(0)
    slot_all(1)
    own_scores(1)
    small_came(st_all, rows - 1, st_recv)

    for side in range(2):
        for n, (of_lo, of_y) in enumerate(blocks):
            stats = [st_all[(of_lo * ys + of_y + i) * 2 + parities[side]] for i in range(pair)]
            at = side * len(blocks) + n
            lanes = slice(at * wide, (at + 1) * wide)
            for head in range(2):
                part = slice(head * TOK, (head + 1) * TOK)
                total = jnp.concatenate([stat[0:1, part] for stat in stats], axis=1)
                shift = jnp.concatenate([stat[1:2, part] for stat in stats], axis=1)
                probs = jnp.exp(s2_ref[at, part] - total)
                p2_ref[part, lanes] = probs.astype(BF16)
                ds2_ref[part, lanes] = (probs * (dp2_ref[at, part] - shift)).astype(BF16)

    key_grad = jnp.zeros((SLOT, WIDE), F32)
    value_grad = jnp.zeros((SLOT, WIDE), F32)
    for side in range(2):
        lanes = slice(side * chips * TOK, (side + 1) * chips * TOK)
        key_grad = key_grad + dot_nn(ds2_ref[:, lanes], slots_of(qd_all, parities[side], slice(0, WIDE)))
        value_grad = value_grad + dot_nn(p2_ref[:, lanes], slots_of(qd_all, parities[side], slice(WIDE, SLOT)))
    key_grad = jnp.where(low, key_grad[0:TOK], key_grad[TOK:SLOT])
    value_grad = jnp.where(low, value_grad[0:TOK], value_grad[TOK:SLOT])
    kv_grad = jnp.concatenate([key_grad, value_grad], axis=1)
    turned = jnp.concatenate([jnp.transpose(key_grad), jnp.transpose(value_grad)], axis=0).astype(BF16)
    kv_grad = kv_grad.astype(BF16)
    grads_turned = jnp.concatenate([turned, query_grad], axis=0)

    queries_turned = dot_nt(eye(WIDE, WIDE), queries)
    inner = jnp.sum(query_grad.astype(F32) * queries_turned, axis=0, keepdims=True)
    kv_inner = kv_grad.astype(F32) * kv.astype(F32)
    kv_hi = kv_inner.astype(BF16)
    kv_lo = (kv_inner - kv_hi.astype(F32)).astype(BF16)
    ones = jnp.ones((8, SLOT), BF16)
    kv_inner = dot_nt(ones, kv_hi) + dot_nt(ones, kv_lo)
    inner = inner + kv_inner[0:1]

    def partials(places):
        slots = []
        for by in places:
            j = z_at(by)
            at = (j // (2 * ys), lax.rem(j // 2, ys), lax.rem(j, 2))
            slots.append(jnp.concatenate([wkv_all[at], wqo_all[at + (slice(None), slice(0, WIDE))]], axis=1))
        value = dot_nn(jnp.concatenate(slots, axis=0), grads_turned)
        parts = [value[i * PAD : (i + 1) * PAD] for i in range(len(places))]
        return [jnp.where(row_at == FEAT, inner, part) for part in parts]

    some = pl.ds(0, zs - 1)
    for i in range(2):
        sent(streams[i].at[some], z_send.at[i])
        for group, sems, x_slots in ((weights[i], w_send, slice(0, ys)), (gathered[i], a_send, slice(0, 1))):
            if ys > 1:
                columns = slice(0, 1) if group is weights[i] else slice(0, 2)
                sent(group.at[columns, pl.ds(0, ys - 1), 0], sems.at[i, 0])
            sent(group.at[0, x_slots, 0], sems.at[i, 1])
            sent(group.at[:, :, 0], sems.at[i, 2])

    sent(st_all.at[pl.ds(0, rows - 1)], st_send)

    far = 2 * quarter

    def rs_leaf_copy(side, m):
        to = z_device(-1 if side else 1)
        return remote(rs_leaf_tx.at[side, m], rs_leaf.at[side, m], rs_send.at[side], rs_recv.at[side, 1, m], to)

    def rs_hub_copy(side, k):
        to = z_device(-2 if side else 2)
        return remote(rs_hub_tx.at[side, k], rs_hub.at[side, k], rs_send.at[side], rs_recv.at[side, 0, k], to)

    def leaf(side, m, part):
        rs_leaf_tx[side, m] = part.astype(BF16)
        rs_leaf_copy(side, m).start()

    hub_part, right_part, left_part = partials([far, far - 1, 1 - far])
    rs_hub_tx[0, 0] = hub_part.astype(BF16)
    rs_hub_copy(0, 0).start()
    leaf(0, 0, right_part)
    leaf(1, 0, left_part)
    for k in range(1, quarter):
        by = far - 2 * k
        to_right, to_left, right_part, left_part = partials([by, -by, by - 1, 1 - by])
        rs_hub_copy(0, k - 1).wait_recv()
        rs_leaf_copy(0, k - 1).wait_recv()
        total = to_right + rs_hub[0, k - 1].astype(F32) + rs_leaf[0, k - 1].astype(F32)
        rs_hub_tx[0, k] = total.astype(BF16)
        rs_hub_copy(0, k).start()
        rs_leaf_copy(1, k - 1).wait_recv()
        total = to_left + rs_leaf[1, k - 1].astype(F32)
        if k > 1:
            rs_hub_copy(1, k - 2).wait_recv()
            total = total + rs_hub[1, k - 2].astype(F32)
        rs_hub_tx[1, k - 1] = total.astype(BF16)
        rs_hub_copy(1, k - 1).start()
        leaf(0, k, right_part)
        leaf(1, k, left_part)

    own = partials([0])[0]
    for side in range(2):
        last = quarter - 1 - side
        rs_leaf_copy(side, quarter - 1).wait_recv()
        own = own + rs_leaf[side, quarter - 1].astype(F32)
        if last >= 0:
            rs_hub_copy(side, last).wait_recv()
            own = own + rs_hub[side, last].astype(F32)

    inner = own[FEAT : FEAT + 1] * (1.0 / (zs * FEAT))
    scaled = own * gain_own[...]
    normalized = xt_own[...] * scale_row
    raw = og_own[...] + scale_row * (scaled - normalized * inner)
    power = jnp.sum((raw * raw).reshape(PAD // 8, 8, TOK), axis=0)

    def power_sibling():
        return remote(pw_tx.at[0], pw1.at[here * 2 + core], p_send.at[0], p_recv.at[0], sibling)

    def power_plane(i, of_core):
        to = lax.rem(here + i, planes)
        to_d, to_r, to_c = plane_device(to)
        to_r = to_r - core + of_core
        return remote(pw_tx.at[0], pw1.at[here * 2 + core], p_send.at[0], p_recv.at[0], (to_d, to_r, to_c))

    def power_col(i):
        return remote(pw_tx.at[2], pw2.at[c], p_send.at[2], p_recv.at[2], (d, r, lax.rem(c + i, zs)))

    pw_tx[0] = power
    pw1[here * 2 + core] = power
    power_sibling().start()

    @pl.loop(1, planes)
    def _(i):
        power_plane(i, 0).start()
        power_plane(i, 1).start()

    small_came(pw1, 2 * planes - 1, p_recv.at[0])

    sent(xt_all.at[pl.ds(0, far)], rs_send.at[0])
    sent(xt_all.at[pl.ds(0, far - 1)], rs_send.at[1])
    power = jnp.sum(pw1[...], axis=0)
    pw_tx[2] = power
    pw2[c] = power

    @pl.loop(1, zs)
    def _(i):
        power_col(i).start()

    small_came(pw2, zs - 1, p_recv.at[2])

    sent(pw1.at[pl.ds(0, 2 * planes - 1)], p_send.at[0])
    sent(pw2.at[pl.ds(0, zs - 1)], p_send.at[2])
    power = jnp.sum(jnp.sum(pw2[...], axis=0), axis=0, keepdims=True)
    power = jnp.sum(power, axis=1, keepdims=True)
    cells = depths * seq * zs * FEAT
    final = raw * lax.rsqrt(power * (1.0 / cells) + epsilon)
    out_ref[...] = final[0:FEAT].astype(BF16)


def sizes_of(mesh):
    depths, rows, zs = mesh.shape["depth"], mesh.shape["row"], mesh.shape["col"]
    los = 2
    return depths, los, rows // (2 * los), zs


def solution(mesh):
    depths, los, ys, zs = sizes_of(mesh)
    chips, planes = los * ys, depths * los * ys
    rows = chips * 2
    quarter = zs // 4
    dma = pltpu.SemaphoreType.DMA
    scratch = [
        *([pltpu.VMEM((FEAT, TOK), BF16)] * 6),
        pltpu.VMEM((FEAT,), BF16),
        pltpu.VMEM((zs, PAD, TOK), BF16),
        pltpu.VMEM((zs, PAD, TOK), BF16),
        pltpu.VMEM((los, ys, 2, PAD, SLOT), BF16),
        pltpu.VMEM((los, ys, 2, PAD, SLOT), BF16),
        pltpu.VMEM((los, ys, 2, TOK, SLOT), BF16),
        pltpu.VMEM((los, ys, 2, TOK, SLOT), BF16),
        pltpu.VMEM((rows, 8, SLOT), F32),
        pltpu.VMEM((PAD, TOK), F32),
        pltpu.VMEM((PAD, TOK), F32),
        pltpu.VMEM((PAD, TOK), F32),
        pltpu.VMEM((los, ys, 2, TOK, SLOT), F32),
        pltpu.VMEM((los, ys, 2, TOK, SLOT), F32),
        pltpu.VMEM((2, WIDE, chips * TOK), BF16),
        pltpu.VMEM((los, ys, 2, TOK, SLOT), BF16),
        pltpu.VMEM((rows // min(ys, 2), SLOT, min(ys, 2) * TOK), F32),
        pltpu.VMEM((rows // min(ys, 2), SLOT, min(ys, 2) * TOK), F32),
        pltpu.VMEM((SLOT, rows * TOK), BF16),
        pltpu.VMEM((SLOT, rows * TOK), BF16),
        *([pltpu.VMEM((2, quarter, PAD, TOK), BF16)] * 4),
        pltpu.VMEM((3, 8, TOK), F32),
        pltpu.VMEM((2 * planes, 8, TOK), F32),
        pltpu.VMEM((zs, 8, TOK), F32),
        dma((7,)),
        dma((2,)), dma((2, 2, 2, quarter)),
        dma((2, 3)), dma((2, ys + 1)), dma((2,)),
        dma((2, 3)), dma((2, los, ys)), dma((2,)),
        dma, dma,
        dma((2,)), dma((2, 2, quarter)),
        dma((3,)), dma((3,)),
    ]

    def shards(latents, out_grad, w_query, w_key, w_value, w_out, gain):
        return pl.pallas_call(
            functools.partial(kernel, (depths, los, ys, zs)),
            out_shape=jax.ShapeDtypeStruct((FEAT, TOK), BF16),
            in_specs=[pl.BlockSpec(memory_space=pl.ANY)] * 7,
            out_specs=pl.BlockSpec(memory_space=pltpu.VMEM),
            scratch_shapes=scratch,
            compiler_params=pltpu.CompilerParams(
                collective_id=0, has_side_effects=True, vmem_limit_bytes=56 * 1024 * 1024
            ),
        )(latents.T, out_grad.T, w_query, w_key, w_value, w_out, gain).T

    return jax.shard_map(
        shards,
        mesh=mesh,
        in_specs=(
            P(("depth", "row"), "col"),
            P(("depth", "row"), "col"),
            P("row", "col"),
            P("row", "col"),
            P("row", "col"),
            P("row", "col"),
            P("col"),
        ),
        out_specs=P(("depth", "row"), "col"),
        check_vma=False,
    )
```

```python
import functools

import jax
import jax.numpy as jnp
from jax import lax
from jax.experimental import pallas as pl
from jax.experimental.pallas import tpu as pltpu
from jax.sharding import PartitionSpec as P

MESH = pl.DeviceIdType.MESH
F32 = jnp.float32
BF16 = jnp.bfloat16
FEAT = 152
PAD = 160
HALF = 80
TOK = 128
WIDE = 128
HDIM = 64
SLOT = 256
epsilon = 1e-06


def dot_nt(a, b):
    return lax.dot_general(a, b, (((1,), (1,)), ((), ())), preferred_element_type=F32)


def dot_tn(a, b):
    return lax.dot_general(a, b, (((0,), (0,)), ((), ())), preferred_element_type=F32)


def dot_nn(a, b):
    return jnp.dot(a, b, preferred_element_type=F32)


def eye(rows, columns):
    at = lax.broadcasted_iota(jnp.int32, (rows, columns), 0)
    to = lax.broadcasted_iota(jnp.int32, (rows, columns), 1)
    return jnp.where(at == to, 1.0, 0.0).astype(BF16)


def kernel(
    sizes,
    lat_hbm, og_hbm, wq_hbm, wk_hbm, wv_hbm, wo_hbm, gain_hbm,
    out_ref,
    lat_ref, og_ref, wq_ref, wk_ref, wv_ref, wo_ref, gain_ref,
    xt_all, og_all, wkv_all, wqo_all, kv_all, qd_all, st_all,
    xt_own, og_own, gain_own,
    s_ref, dp_ref, kt_ref, ds_ref, s2_ref, dp2_ref, p2_ref, ds2_ref,
    rs_leaf_tx, rs_hub_tx, rs_leaf, rs_hub,
    pw_tx, pw1, pw2,
    in_sem,
    z_send, z_recv,
    w_send, w_recv, wsib_recv,
    a_send, a_recv, asib_recv,
    st_send, st_recv,
    rs_send, rs_recv,
    p_send, p_recv,
):
    depths, los, ys, zs = sizes
    xs = depths * los
    chips = los * ys
    planes = xs * ys
    rows = chips * 2
    seq = rows * TOK
    quarter = zs // 4

    d = lax.axis_index("depth")
    r = lax.axis_index("row")
    c = lax.axis_index("col")
    core = lax.rem(r, 2)
    other = 1 - core
    chip = r // 2
    lo = chip // ys
    y = lax.rem(chip, ys)
    x = d * los + lo
    here = x * ys + y

    sibling = (d, chip * 2 + other, c)

    def z_at(by):
        return lax.rem(c + by % zs, zs)

    def z_device(by):
        return (d, r, z_at(by))

    def plane_device(at):
        to_x, to_y = at // ys, lax.rem(at, ys)
        return (to_x // los, (lax.rem(to_x, los) * ys + to_y) * 2 + core, c)

    def remote(src, dst, send, recv, device):
        return pltpu.make_async_remote_copy(
            src_ref=src, dst_ref=dst, send_sem=send, recv_sem=recv, device_id=device, device_id_type=MESH
        )

    inputs = (lat_hbm, og_hbm, gain_hbm, wk_hbm, wv_hbm, wq_hbm, wo_hbm)
    staged = (lat_ref, og_ref, gain_ref, wk_ref, wv_ref, wq_ref, wo_ref)
    fetches = [pltpu.make_async_copy(a, b, in_sem.at[i]) for i, (a, b) in enumerate(zip(inputs, staged))]
    for fetch in fetches:
        fetch.start()

    barrier = pltpu.get_barrier_semaphore()

    def greet(device):
        pl.semaphore_signal(barrier, inc=1, device_id=device, device_id_type=MESH)

    for by in sorted({by % zs for by in (1, -1, 2, -2)}):
        greet(z_device(by))
    greet(sibling)

    @pl.loop(1, planes)
    def _(i):
        greet(plane_device(lax.rem(here + i, planes)))

    fetches[0].wait()
    fetches[2].wait()

    row_at = lax.broadcasted_iota(jnp.int32, (PAD, TOK), 0)
    nothing = jnp.zeros((PAD - FEAT, WIDE), BF16)

    def padded(ref):
        return jnp.concatenate([ref[...], nothing], axis=0)

    xt = padded(lat_ref).astype(F32)
    gain_wide = dot_nt(eye(PAD, FEAT) * gain_ref[...].reshape(1, FEAT), jnp.ones((TOK, FEAT), BF16))
    squares = jnp.sum(xt * xt, axis=0, keepdims=True)
    square_hi = squares.astype(BF16).astype(F32)
    rest = squares - square_hi
    square_mid = rest.astype(BF16).astype(F32)
    square_lo = rest - square_mid
    sent = xt * gain_wide
    sent = jnp.where(row_at == FEAT, square_hi, sent)
    sent = jnp.where(row_at == FEAT + 1, square_mid, sent)
    sent = jnp.where(row_at == FEAT + 2, square_lo, sent)
    xt_all[c] = sent.astype(BF16)
    xt_own[...] = xt
    gain_own[...] = gain_wide
    pl.semaphore_wait(barrier, len({by % zs for by in (1, -1, 2, -2)}) + planes)

    streams = (xt_all, og_all)
    steps = (zs // 2, zs - 1 - zs // 2)

    def ring(stream, side, step):
        sign = -1 if side else 1
        slot = streams[stream].at[z_at(-sign * step)]
        return remote(slot, slot, z_send.at[stream], z_recv.at[stream, side, step], z_device(sign))

    def ring_came(stream, side, step):
        sign = -1 if side else 1
        slot = streams[stream].at[z_at(-sign * (step + 1))]
        remote(slot, slot, z_send.at[stream], z_recv.at[stream, side, step], sibling).wait_recv()

    def column_device(up):
        return (d, (lo * ys + lax.rem(y + up % ys, ys)) * 2 + core, c)

    def x_device(by):
        return plane_device(lax.rem(x + by % xs, xs) * ys + y)

    def y_at(up):
        return lax.rem(y + up % ys, ys)

    weights = (wkv_all, wqo_all)

    def weight_y(array, up, start, size, to):
        slot = weights[array].at[lo, y_at(up), core, pl.ds(start, size)]
        return remote(slot, slot, w_send.at[array, 0], w_recv.at[array, y_at(up)], column_device(to))

    def weight_y_came(array, up):
        weight_y(array, up, 0, PAD, 0).wait_recv()

    def weight_x(array, side):
        slot = weights[array].at[lo, :, core, pl.ds(side * HALF, HALF)]
        return remote(slot, slot, w_send.at[array, 1], w_recv.at[array, ys], x_device(-1 if side else 1))

    def weight_x_one(array, up):
        for side in range(2):
            slot = weights[array].at[lo, y_at(up), core, pl.ds(side * HALF, HALF)]
            to = x_device(-1 if side else 1)
            remote(slot, slot, w_send.at[array, 1], w_recv.at[array, ys], to).start()

    def weight_sibling(array, of_lo):
        slot = weights[array].at[of_lo, :, core]
        return remote(slot, slot, w_send.at[array, 2], wsib_recv.at[array], sibling)

    def weight_first(array):
        if ys == 4:
            weight_y(array, 0, 0, PAD, 1).start()
            weight_y(array, 0, 0, PAD, -1).start()
        elif ys == 2:
            weight_y(array, 0, 0, PAD, 1).start()

    def weight_near(array):
        if ys == 4:
            weight_y_came(array, -1)
            weight_y(array, -1, 0, HALF, 1).start()
            weight_y_came(array, 1)
            weight_y(array, 1, HALF, HALF, -1).start()
            if array == 0:
                weight_x_one(array, -1)
                weight_x_one(array, 1)
        elif ys == 2:
            weight_y_came(array, 1)
            if array == 0:
                weight_x_one(array, 1)

    def weight_column(array):
        if ys == 4:
            weight_y_came(array, 2)
            if array == 0:
                weight_x_one(array, 2)
        if array == 1:
            weight_x(array, 0).start()
            weight_x(array, 1).start()
        weight_sibling(array, lo).start()

    def weight_crossed(array):
        slot = weights[array].at[1 - lo, :, core]
        remote(slot, slot, w_send.at[array, 2], w_recv.at[array, ys], sibling).wait_recv()
        weight_sibling(array, 1 - lo).start()

    def weight_all(array):
        slot = weights[array].at[:, :, other]
        remote(slot, slot, w_send.at[array, 2], wsib_recv.at[array], sibling).wait_recv()

    def sent(ref, sem):
        remote(ref, ref, sem, p_recv.at[0], sibling).wait_send()

    for side in range(2):
        ring(0, side, 0).start()
    fetches[1].wait()
    og_all[c] = padded(og_ref)
    for side in range(2):
        ring(1, side, 0).start()
    fetches[3].wait()
    fetches[4].wait()
    wkv_all[lo, y, core] = jnp.concatenate([padded(wk_ref), padded(wv_ref)], axis=1)
    weight_first(0)
    weight_x_one(0, 0)
    fetches[5].wait()
    fetches[6].wait()
    wqo_all[lo, y, core] = jnp.concatenate([padded(wq_ref), padded(wo_ref)], axis=1)
    weight_first(1)
    og_own[...] = padded(og_ref).astype(F32)
    schedule = [
        [lambda: weight_near(0)],
        [lambda: weight_near(1)],
        [lambda: weight_column(0)],
        [lambda: weight_column(1)],
        [lambda: weight_crossed(0)],
        [],
        [lambda: weight_crossed(1)],
    ]

    for step in range(1, steps[0]):
        for stream in range(2):
            for side in range(2):
                ring_came(stream, side, step - 1)
                if step < steps[side]:
                    ring(stream, side, step).start()
        last = step == steps[0] - 1
        for events in schedule[step - 1 :] if last else schedule[step - 1 : step]:
            for event in events:
                event()

    ring_came(0, 0, steps[0] - 1)
    weight_all(0)

    tails = jnp.zeros((16, TOK), F32)
    for j in range(zs):
        tails = tails + xt_all[j, PAD - 16 : PAD, :].astype(F32)
    square_sum = jnp.sum(tails[8:16], axis=0, keepdims=True)
    scale_row = lax.rsqrt(square_sum * (1.0 / (zs * FEAT)) + epsilon)
    scale_wide = jnp.transpose(jnp.broadcast_to(scale_row, (TOK, TOK)))
    scale_two = jnp.concatenate([scale_wide, scale_wide], axis=1)
    pair = min(ys, 2)

    def project(source, weight, lanes):
        total = None
        for of_lo in range(los):
            for of_y in range(0, ys, pair):
                first = (of_lo * ys + of_y) * 2
                a = source[first : first + 2 * pair].reshape(2 * pair * PAD, TOK)
                b = weight[of_lo, of_y : of_y + pair, :, :, lanes]
                term = dot_tn(a, b.reshape(2 * pair * PAD, b.shape[-1]))
                total = term if total is None else total + term
        return total

    gathered = (kv_all, qd_all)
    half = TOK // 2

    def column(across):
        return 1 - lo if across else lo

    def slot_x(array):
        slot = gathered[array].at[lo, y, core]
        to = (d, ((1 - lo) * ys + y) * 2 + core, c)
        return remote(slot, slot, a_send.at[array, 1], a_recv.at[array, lo, y], to)

    def slot_y(array, across, up, start, size, to):
        slot = gathered[array].at[column(across), y_at(up), core, pl.ds(start, size)]
        recv = a_recv.at[array, column(across), y_at(up)]
        return remote(slot, slot, a_send.at[array, 0], recv, column_device(to))

    def slot_came(array, across, up):
        slot_y(array, across, up, 0, TOK, 0).wait_recv()

    def slot_out(array, across):
        if across:
            slot_came(array, 1, 0)
        if ys == 4:
            slot_y(array, across, 0, 0, TOK, 1).start()
            slot_y(array, across, 0, 0, TOK, -1).start()
        elif ys == 2:
            slot_y(array, across, 0, 0, TOK, 1).start()

    def slot_start(array):
        slot_x(array).start()
        slot_out(array, 0)

    def slot_near(array, across):
        if ys == 4:
            slot_came(array, across, -1)
            slot_y(array, across, -1, 0, half, 1).start()
            slot_came(array, across, 1)
            slot_y(array, across, 1, half, half, -1).start()
        elif ys == 2:
            slot_came(array, across, 1)

    def slot_far(array, across):
        if ys == 4:
            slot_came(array, across, 2)
        slot = gathered[array].at[column(across), :, core]
        remote(slot, slot, a_send.at[array, 2], asib_recv.at[array], sibling).start()

    def slot_all(array):
        slot = gathered[array].at[:, :, other]
        remote(slot, slot, a_send.at[array, 2], asib_recv.at[array], sibling).wait_recv()

    kv = (project(xt_all, wkv_all, slice(0, SLOT)) * scale_two).astype(BF16)
    kv_all[lo, y, core] = kv
    slot_start(0)
    ring_came(1, 0, steps[0] - 1)
    weight_all(1)
    queries = (project(xt_all, wqo_all, slice(0, WIDE)) * scale_wide).astype(BF16)
    out_dir = project(og_all, wqo_all, slice(WIDE, SLOT)).astype(BF16)
    scaled_queries = (queries.astype(F32) * 0.125).astype(BF16)
    qd_all[lo, y, core] = jnp.concatenate([scaled_queries, out_dir], axis=1)
    slot_start(1)
    low = lax.broadcasted_iota(jnp.int32, (TOK, WIDE), 1) < HDIM

    def stacked(a):
        wide = a.astype(F32)
        parts = [jnp.where(low, wide, 0.0), jnp.where(low, 0.0, wide)]
        return jnp.concatenate(parts, axis=0).astype(BF16)

    query_stack = stacked(scaled_queries)
    dir_stack = stacked(out_dir)

    def slots_of(ref, parity, lanes):
        return ref[:, :, parity, :, lanes].reshape(chips * TOK, lanes.stop - lanes.start)

    def scores_of(parity):
        keys = slots_of(kv_all, parity, slice(0, WIDE))
        scores = dot_nt(keys, query_stack)
        s_ref[:, :, parity] = scores.reshape(los, ys, TOK, SLOT)
        prob_grad = dot_nt(slots_of(kv_all, parity, slice(WIDE, SLOT)), dir_stack)
        dp_ref[:, :, parity] = prob_grad.reshape(los, ys, TOK, SLOT)
        kt_ref[parity] = jnp.transpose(keys)
        return jnp.max(scores.reshape(chips * TOK // 8, 8, SLOT), axis=0)

    slot_out(0, 1)
    slot_near(0, 0)
    slot_out(1, 1)
    slot_near(0, 1)
    slot_far(0, 0)
    slot_near(1, 0)
    slot_far(0, 1)
    most = scores_of(core)
    slot_near(1, 1)
    slot_far(1, 0)
    slot_all(0)
    most = jnp.max(jnp.maximum(most, scores_of(other)), axis=0, keepdims=True)

    def tile_at(i):
        return i // (2 * ys), lax.rem(i // 2, ys), lax.rem(i, 2)

    def folded(a):
        return jnp.sum(a.reshape(TOK // 8, 8, SLOT), axis=0)

    def expo_body(i, sums):
        at = tile_at(i)
        expo = jnp.exp(s_ref[at] - most)
        s_ref[at] = expo
        return sums[0] + folded(expo), sums[1] + folded(expo * dp_ref[at])

    zero = jnp.zeros((8, SLOT), F32)
    totals, delta = lax.fori_loop(0, rows, expo_body, (zero, zero), unroll=2)
    totals = jnp.sum(totals, axis=0, keepdims=True)
    inverse = 1.0 / totals
    delta = jnp.sum(delta, axis=0, keepdims=True) * inverse
    slot_far(1, 1)

    def stat_copy(i):
        to = lax.rem(r + i, rows)
        return remote(st_all.at[r], st_all.at[r], st_send, st_recv, (d, to, c))

    def small_came(ref, count, sem):
        some = ref.at[pl.ds(0, count)]
        remote(some, some, p_send.at[1], sem, sibling).wait_recv()

    st_all[r] = jnp.concatenate([most + jnp.log(totals), delta, jnp.zeros((6, SLOT), F32)], axis=0)

    @pl.loop(1, rows)
    def _(i):
        stat_copy(i).start()

    def score_grad_body(i, nothing):
        at = tile_at(i)
        ds_ref[at] = (s_ref[at] * (dp_ref[at] - delta)).astype(BF16)
        return nothing

    lax.fori_loop(0, rows, score_grad_body, 0, unroll=2)
    query_grad = jnp.zeros((WIDE, SLOT), F32)
    for parity in range(2):
        query_grad = query_grad + dot_nn(kt_ref[parity], slots_of(ds_ref, parity, slice(0, SLOT)))
    query_grad = query_grad * (inverse * 0.125)
    query_grad = jnp.concatenate([query_grad[0:HDIM, 0:TOK], query_grad[HDIM:WIDE, TOK:SLOT]], axis=0)
    query_grad = query_grad.astype(BF16)

    key_stack = stacked(kv[:, 0:WIDE])
    value_stack = stacked(kv[:, WIDE:SLOT])
    wide = pair * TOK
    blocks = [(of_lo, of_y) for of_lo in range(los) for of_y in range(0, ys, pair)]
    parities = (core, other)

    def own_scores(side):
        for n, (of_lo, of_y) in enumerate(blocks):
            block = qd_all[of_lo, of_y : of_y + pair, parities[side]].reshape(wide, SLOT)
            s2_ref[side * len(blocks) + n] = dot_nt(key_stack, block[:, 0:WIDE])
            dp2_ref[side * len(blocks) + n] = dot_nt(value_stack, block[:, WIDE:SLOT])

    own_scores(0)
    slot_all(1)
    own_scores(1)
    small_came(st_all, rows - 1, st_recv)

    for side in range(2):
        for n, (of_lo, of_y) in enumerate(blocks):
            stats = [st_all[(of_lo * ys + of_y + i) * 2 + parities[side]] for i in range(pair)]
            at = side * len(blocks) + n
            lanes = slice(at * wide, (at + 1) * wide)
            for head in range(2):
                part = slice(head * TOK, (head + 1) * TOK)
                total = jnp.concatenate([stat[0:1, part] for stat in stats], axis=1)
                shift = jnp.concatenate([stat[1:2, part] for stat in stats], axis=1)
                probs = jnp.exp(s2_ref[at, part] - total)
                p2_ref[part, lanes] = probs.astype(BF16)
                ds2_ref[part, lanes] = (probs * (dp2_ref[at, part] - shift)).astype(BF16)

    key_grad = jnp.zeros((SLOT, WIDE), F32)
    value_grad = jnp.zeros((SLOT, WIDE), F32)
    for side in range(2):
        lanes = slice(side * chips * TOK, (side + 1) * chips * TOK)
        key_grad = key_grad + dot_nn(ds2_ref[:, lanes], slots_of(qd_all, parities[side], slice(0, WIDE)))
        value_grad = value_grad + dot_nn(p2_ref[:, lanes], slots_of(qd_all, parities[side], slice(WIDE, SLOT)))
    key_grad = jnp.where(low, key_grad[0:TOK], key_grad[TOK:SLOT])
    value_grad = jnp.where(low, value_grad[0:TOK], value_grad[TOK:SLOT])
    kv_grad = jnp.concatenate([key_grad, value_grad], axis=1)
    turned = jnp.concatenate([jnp.transpose(key_grad), jnp.transpose(value_grad)], axis=0).astype(BF16)
    kv_grad = kv_grad.astype(BF16)
    grads_turned = jnp.concatenate([turned, query_grad], axis=0)

    queries_turned = dot_nt(eye(WIDE, WIDE), queries)
    inner = jnp.sum(query_grad.astype(F32) * queries_turned, axis=0, keepdims=True)
    kv_inner = kv_grad.astype(F32) * kv.astype(F32)
    kv_hi = kv_inner.astype(BF16)
    kv_lo = (kv_inner - kv_hi.astype(F32)).astype(BF16)
    ones = jnp.ones((8, SLOT), BF16)
    kv_inner = dot_nt(ones, kv_hi) + dot_nt(ones, kv_lo)
    inner = inner + kv_inner[0:1]

    def partials(places):
        slots = []
        for by in places:
            j = z_at(by)
            at = (j // (2 * ys), lax.rem(j // 2, ys), lax.rem(j, 2))
            slots.append(jnp.concatenate([wkv_all[at], wqo_all[at + (slice(None), slice(0, WIDE))]], axis=1))
        value = dot_nn(jnp.concatenate(slots, axis=0), grads_turned)
        parts = [value[i * PAD : (i + 1) * PAD] for i in range(len(places))]
        return [jnp.where(row_at == FEAT, inner, part) for part in parts]

    some = pl.ds(0, zs - 1)
    for i in range(2):
        sent(streams[i].at[some], z_send.at[i])
        for group, sems, x_slots in ((weights[i], w_send, slice(0, ys)), (gathered[i], a_send, slice(0, 1))):
            if ys > 1:
                columns = slice(0, 1) if group is weights[i] else slice(0, 2)
                sent(group.at[columns, pl.ds(0, ys - 1), 0], sems.at[i, 0])
            sent(group.at[0, x_slots, 0], sems.at[i, 1])
            sent(group.at[:, :, 0], sems.at[i, 2])

    sent(st_all.at[pl.ds(0, rows - 1)], st_send)

    far = 2 * quarter

    def rs_leaf_copy(side, m):
        to = z_device(-1 if side else 1)
        return remote(rs_leaf_tx.at[side, m], rs_leaf.at[side, m], rs_send.at[side], rs_recv.at[side, 1, m], to)

    def rs_hub_copy(side, k):
        to = z_device(-2 if side else 2)
        return remote(rs_hub_tx.at[side, k], rs_hub.at[side, k], rs_send.at[side], rs_recv.at[side, 0, k], to)

    def leaf(side, m, part):
        rs_leaf_tx[side, m] = part.astype(BF16)
        rs_leaf_copy(side, m).start()

    hub_part, right_part, left_part = partials([far, far - 1, 1 - far])
    rs_hub_tx[0, 0] = hub_part.astype(BF16)
    rs_hub_copy(0, 0).start()
    leaf(0, 0, right_part)
    leaf(1, 0, left_part)
    for k in range(1, quarter):
        by = far - 2 * k
        to_right, to_left, right_part, left_part = partials([by, -by, by - 1, 1 - by])
        rs_hub_copy(0, k - 1).wait_recv()
        rs_leaf_copy(0, k - 1).wait_recv()
        total = to_right + rs_hub[0, k - 1].astype(F32) + rs_leaf[0, k - 1].astype(F32)
        rs_hub_tx[0, k] = total.astype(BF16)
        rs_hub_copy(0, k).start()
        rs_leaf_copy(1, k - 1).wait_recv()
        total = to_left + rs_leaf[1, k - 1].astype(F32)
        if k > 1:
            rs_hub_copy(1, k - 2).wait_recv()
            total = total + rs_hub[1, k - 2].astype(F32)
        rs_hub_tx[1, k - 1] = total.astype(BF16)
        rs_hub_copy(1, k - 1).start()
        leaf(0, k, right_part)
        leaf(1, k, left_part)

    own = partials([0])[0]
    for side in range(2):
        last = quarter - 1 - side
        rs_leaf_copy(side, quarter - 1).wait_recv()
        own = own + rs_leaf[side, quarter - 1].astype(F32)
        if last >= 0:
            rs_hub_copy(side, last).wait_recv()
            own = own + rs_hub[side, last].astype(F32)

    inner = own[FEAT : FEAT + 1] * (1.0 / (zs * FEAT))
    scaled = own * gain_own[...]
    normalized = xt_own[...] * scale_row
    raw = og_own[...] + scale_row * (scaled - normalized * inner)
    power = jnp.sum((raw * raw).reshape(PAD // 8, 8, TOK), axis=0)

    def power_sibling():
        return remote(pw_tx.at[0], pw1.at[here * 2 + core], p_send.at[0], p_recv.at[0], sibling)

    def power_plane(i, of_core):
        to = lax.rem(here + i, planes)
        to_d, to_r, to_c = plane_device(to)
        to_r = to_r - core + of_core
        return remote(pw_tx.at[0], pw1.at[here * 2 + core], p_send.at[0], p_recv.at[0], (to_d, to_r, to_c))

    def power_col(i):
        return remote(pw_tx.at[2], pw2.at[c], p_send.at[2], p_recv.at[2], (d, r, lax.rem(c + i, zs)))

    pw_tx[0] = power
    pw1[here * 2 + core] = power
    power_sibling().start()

    @pl.loop(1, planes)
    def _(i):
        power_plane(i, 0).start()
        power_plane(i, 1).start()

    small_came(pw1, 2 * planes - 1, p_recv.at[0])

    sent(xt_all.at[pl.ds(0, far)], rs_send.at[0])
    sent(xt_all.at[pl.ds(0, far - 1)], rs_send.at[1])
    power = jnp.sum(pw1[...], axis=0)
    pw_tx[2] = power
    pw2[c] = power

    @pl.loop(1, zs)
    def _(i):
        power_col(i).start()

    small_came(pw2, zs - 1, p_recv.at[2])

    sent(pw1.at[pl.ds(0, 2 * planes - 1)], p_send.at[0])
    sent(pw2.at[pl.ds(0, zs - 1)], p_send.at[2])
    power = jnp.sum(jnp.sum(pw2[...], axis=0), axis=0, keepdims=True)
    power = jnp.sum(power, axis=1, keepdims=True)
    cells = depths * seq * zs * FEAT
    final = raw * lax.rsqrt(power * (1.0 / cells) + epsilon)
    out_ref[...] = final[0:FEAT].astype(BF16)


def sizes_of(mesh):
    depths, rows, zs = mesh.shape["depth"], mesh.shape["row"], mesh.shape["col"]
    los = 2
    return depths, los, rows // (2 * los), zs


def solution(mesh):
    depths, los, ys, zs = sizes_of(mesh)
    chips, planes = los * ys, depths * los * ys
    rows = chips * 2
    quarter = zs // 4
    dma = pltpu.SemaphoreType.DMA
    scratch = [
        *([pltpu.VMEM((FEAT, TOK), BF16)] * 6),
        pltpu.VMEM((FEAT,), BF16),
        pltpu.VMEM((zs, PAD, TOK), BF16),
        pltpu.VMEM((zs, PAD, TOK), BF16),
        pltpu.VMEM((los, ys, 2, PAD, SLOT), BF16),
        pltpu.VMEM((los, ys, 2, PAD, SLOT), BF16),
        pltpu.VMEM((los, ys, 2, TOK, SLOT), BF16),
        pltpu.VMEM((los, ys, 2, TOK, SLOT), BF16),
        pltpu.VMEM((rows, 8, SLOT), F32),
        pltpu.VMEM((PAD, TOK), F32),
        pltpu.VMEM((PAD, TOK), F32),
        pltpu.VMEM((PAD, TOK), F32),
        pltpu.VMEM((los, ys, 2, TOK, SLOT), F32),
        pltpu.VMEM((los, ys, 2, TOK, SLOT), F32),
        pltpu.VMEM((2, WIDE, chips * TOK), BF16),
        pltpu.VMEM((los, ys, 2, TOK, SLOT), BF16),
        pltpu.VMEM((rows // min(ys, 2), SLOT, min(ys, 2) * TOK), F32),
        pltpu.VMEM((rows // min(ys, 2), SLOT, min(ys, 2) * TOK), F32),
        pltpu.VMEM((SLOT, rows * TOK), BF16),
        pltpu.VMEM((SLOT, rows * TOK), BF16),
        *([pltpu.VMEM((2, quarter, PAD, TOK), BF16)] * 4),
        pltpu.VMEM((3, 8, TOK), F32),
        pltpu.VMEM((2 * planes, 8, TOK), F32),
        pltpu.VMEM((zs, 8, TOK), F32),
        dma((7,)),
        dma((2,)), dma((2, 2, 2 * quarter)),
        dma((2, 3)), dma((2, ys + 1)), dma((2,)),
        dma((2, 3)), dma((2, los, ys)), dma((2,)),
        dma, dma,
        dma((2,)), dma((2, 2, quarter)),
        dma((3,)), dma((3,)),
    ]

    def shards(latents, out_grad, w_query, w_key, w_value, w_out, gain):
        return pl.pallas_call(
            functools.partial(kernel, (depths, los, ys, zs)),
            out_shape=jax.ShapeDtypeStruct((FEAT, TOK), BF16),
            in_specs=[pl.BlockSpec(memory_space=pl.ANY)] * 7,
            out_specs=pl.BlockSpec(memory_space=pltpu.VMEM),
            scratch_shapes=scratch,
            compiler_params=pltpu.CompilerParams(
                collective_id=0, has_side_effects=True, vmem_limit_bytes=56 * 1024 * 1024
            ),
        )(latents.T, out_grad.T, w_query, w_key, w_value, w_out, gain).T

    return jax.shard_map(
        shards,
        mesh=mesh,
        in_specs=(
            P(("depth", "row"), "col"),
            P(("depth", "row"), "col"),
            P("row", "col"),
            P("row", "col"),
            P("row", "col"),
            P("row", "col"),
            P("col"),
        ),
        out_specs=P(("depth", "row"), "col"),
        check_vma=False,
    )
```

```python
import functools

import jax
import jax.numpy as jnp
from jax import lax
from jax.experimental import pallas as pl
from jax.experimental.pallas import tpu as pltpu
from jax.sharding import PartitionSpec as P

MESH = pl.DeviceIdType.MESH
F32 = jnp.float32
BF16 = jnp.bfloat16
FEAT = 152
PAD = 160
HALF = 80
TOK = 128
WIDE = 128
HDIM = 64
SLOT = 256
epsilon = 1e-06


def dot_nt(a, b):
    return lax.dot_general(a, b, (((1,), (1,)), ((), ())), preferred_element_type=F32)


def dot_tn(a, b):
    return lax.dot_general(a, b, (((0,), (0,)), ((), ())), preferred_element_type=F32)


def dot_nn(a, b):
    return jnp.dot(a, b, preferred_element_type=F32)


def eye(rows, columns):
    at = lax.broadcasted_iota(jnp.int32, (rows, columns), 0)
    to = lax.broadcasted_iota(jnp.int32, (rows, columns), 1)
    return jnp.where(at == to, 1.0, 0.0).astype(BF16)


def kernel(
    sizes,
    lat_hbm, og_hbm, wq_hbm, wk_hbm, wv_hbm, wo_hbm, gain_hbm,
    out_ref,
    lat_ref, og_ref, wq_ref, wk_ref, wv_ref, wo_ref, gain_ref,
    xt_all, og_all, wkv_all, wqo_all, kv_all, qd_all, st_all,
    xt_own, og_own, gain_own,
    s_ref, dp_ref, kt_ref, ds_ref, s2_ref, dp2_ref, p2_ref, ds2_ref,
    rs_leaf_tx, rs_hub_tx, rs_leaf, rs_hub,
    pw_tx, pw0, pw1, pw2,
    in_sem,
    z_send, z_recv,
    w_send, w_recv, wsib_recv,
    a_send, a_recv, asib_recv,
    st_send, st_recv,
    rs_send, rs_recv,
    p_send, p_recv,
):
    depths, los, ys, zs = sizes
    xs = depths * los
    chips = los * ys
    planes = xs * ys
    rows = chips * 2
    seq = rows * TOK
    quarter = zs // 4

    d = lax.axis_index("depth")
    r = lax.axis_index("row")
    c = lax.axis_index("col")
    core = lax.rem(r, 2)
    other = 1 - core
    chip = r // 2
    lo = chip // ys
    y = lax.rem(chip, ys)
    x = d * los + lo
    here = x * ys + y

    sibling = (d, chip * 2 + other, c)

    def z_at(by):
        return lax.rem(c + by % zs, zs)

    def z_device(by):
        return (d, r, z_at(by))

    def plane_device(at):
        to_x, to_y = at // ys, lax.rem(at, ys)
        return (to_x // los, (lax.rem(to_x, los) * ys + to_y) * 2 + core, c)

    def remote(src, dst, send, recv, device):
        return pltpu.make_async_remote_copy(
            src_ref=src, dst_ref=dst, send_sem=send, recv_sem=recv, device_id=device, device_id_type=MESH
        )

    inputs = (lat_hbm, og_hbm, gain_hbm, wk_hbm, wv_hbm, wq_hbm, wo_hbm)
    staged = (lat_ref, og_ref, gain_ref, wk_ref, wv_ref, wq_ref, wo_ref)
    fetches = [pltpu.make_async_copy(a, b, in_sem.at[i]) for i, (a, b) in enumerate(zip(inputs, staged))]
    for i in (0, 2, 1, 3, 4, 5, 6):
        fetches[i].start()

    near_z = sorted({by % zs for by in (1, -1, 2, -2)})
    near_y = sorted({by % ys for by in (1, -1)} - {0})
    near_x = sorted({by % xs for by in (1, -1)})
    barrier = pltpu.get_barrier_semaphore()
    partners = [(d, r, lax.rem(c + by, zs)) for by in near_z]
    partners += [plane_device(x * ys + lax.rem(y + by, ys)) for by in near_y]
    partners += [plane_device(lax.rem(x + by, xs) * ys + y) for by in near_x]
    partners += [sibling]
    for device in partners:
        pl.semaphore_signal(barrier, inc=1, device_id=device, device_id_type=MESH)

    fetches[0].wait()
    fetches[2].wait()

    row_at = lax.broadcasted_iota(jnp.int32, (PAD, TOK), 0)
    nothing = jnp.zeros((PAD - FEAT, WIDE), BF16)

    def padded(ref):
        return jnp.concatenate([ref[...], nothing], axis=0)

    xt = padded(lat_ref).astype(F32)
    gain_wide = dot_nt(eye(PAD, FEAT) * gain_ref[...].reshape(1, FEAT), jnp.ones((TOK, FEAT), BF16))
    squares = jnp.sum(xt * xt, axis=0, keepdims=True)
    square_hi = squares.astype(BF16).astype(F32)
    rest = squares - square_hi
    square_mid = rest.astype(BF16).astype(F32)
    square_lo = rest - square_mid
    sent = xt * gain_wide
    sent = jnp.where(row_at == FEAT, square_hi, sent)
    sent = jnp.where(row_at == FEAT + 1, square_mid, sent)
    sent = jnp.where(row_at == FEAT + 2, square_lo, sent)
    xt_all[c] = sent.astype(BF16)
    xt_own[...] = xt
    gain_own[...] = gain_wide
    pl.semaphore_wait(barrier, len(partners))

    streams = (xt_all, og_all)

    def edges(most):
        a, found = 0, []
        while a < most:
            if a + 2 <= most and a < 4:
                found += [(a, a + 2), (a, a + 1)]
                a += 2
            else:
                found += [(a, a + 1)]
                a += 1
        return found

    ways = (edges(zs // 2), edges(zs - 1 - zs // 2))
    stops = sorted({a for way in ways for a, b in way})

    def ring(stream, side, a, b):
        sign = -1 if side else 1
        slot = streams[stream].at[z_at(-sign * a)]
        return remote(slot, slot, z_send.at[stream], z_recv.at[stream, side, b - 1], z_device(sign * (b - a)))

    def ring_came(stream, side, b):
        sign = -1 if side else 1
        slot = streams[stream].at[z_at(-sign * b)]
        remote(slot, slot, z_send.at[stream], z_recv.at[stream, side, b - 1], sibling).wait_recv()

    def ring_round(stream, stop):
        for side in range(2):
            out = [edge for edge in ways[side] if edge[0] == stop]
            if out and stop:
                ring_came(stream, side, stop)
            for edge in out:
                ring(stream, side, *edge).start()

    def ring_end(stream):
        for side in range(2):
            for a, b in ways[side]:
                if b not in [start for start, end in ways[side]]:
                    ring_came(stream, side, b)

    def column_device(up):
        return (d, (lo * ys + lax.rem(y + up % ys, ys)) * 2 + core, c)

    def x_device(by):
        return plane_device(lax.rem(x + by % xs, xs) * ys + y)

    def y_at(up):
        return lax.rem(y + up % ys, ys)

    weights = (wkv_all, wqo_all)

    def weight_y(array, up, start, size, to):
        slot = weights[array].at[lo, y_at(up), core, pl.ds(start, size)]
        return remote(slot, slot, w_send.at[array, 0], w_recv.at[array, y_at(up)], column_device(to))

    def weight_y_came(array, up):
        weight_y(array, up, 0, PAD, 0).wait_recv()

    def weight_x(array, side):
        slot = weights[array].at[lo, :, core, pl.ds(side * HALF, HALF)]
        return remote(slot, slot, w_send.at[array, 1], w_recv.at[array, ys], x_device(-1 if side else 1))

    def weight_x_one(array, up):
        for side in range(2):
            slot = weights[array].at[lo, y_at(up), core, pl.ds(side * HALF, HALF)]
            to = x_device(-1 if side else 1)
            remote(slot, slot, w_send.at[array, 1], w_recv.at[array, ys], to).start()

    def weight_sibling(array, of_lo):
        slot = weights[array].at[of_lo, :, core]
        return remote(slot, slot, w_send.at[array, 2], wsib_recv.at[array], sibling)

    def weight_first(array):
        if ys == 4:
            weight_y(array, 0, 0, PAD, 1).start()
            weight_y(array, 0, 0, PAD, -1).start()
        elif ys == 2:
            weight_y(array, 0, 0, PAD, 1).start()

    def weight_near(array):
        if ys == 4:
            weight_y_came(array, -1)
            weight_y(array, -1, 0, HALF, 1).start()
            weight_y_came(array, 1)
            weight_y(array, 1, HALF, HALF, -1).start()
            if array == 0:
                weight_x_one(array, -1)
                weight_x_one(array, 1)
        elif ys == 2:
            weight_y_came(array, 1)
            if array == 0:
                weight_x_one(array, 1)

    def weight_column(array):
        if ys == 4:
            weight_y_came(array, 2)
            if array == 0:
                weight_x_one(array, 2)
        if array == 1:
            weight_x(array, 0).start()
            weight_x(array, 1).start()
        weight_sibling(array, lo).start()

    def weight_crossed(array):
        slot = weights[array].at[1 - lo, :, core]
        remote(slot, slot, w_send.at[array, 2], w_recv.at[array, ys], sibling).wait_recv()
        weight_sibling(array, 1 - lo).start()

    def weight_all(array):
        slot = weights[array].at[:, :, other]
        remote(slot, slot, w_send.at[array, 2], wsib_recv.at[array], sibling).wait_recv()

    def sent(ref, sem):
        remote(ref, ref, sem, p_recv.at[0], sibling).wait_send()

    ring_round(0, 0)
    fetches[1].wait()
    og_all[c] = padded(og_ref)
    ring_round(1, 0)
    fetches[3].wait()
    fetches[4].wait()
    wkv_all[lo, y, core] = jnp.concatenate([padded(wk_ref), padded(wv_ref)], axis=1)
    weight_first(0)
    weight_x_one(0, 0)
    fetches[5].wait()
    fetches[6].wait()
    wqo_all[lo, y, core] = jnp.concatenate([padded(wq_ref), padded(wo_ref)], axis=1)
    weight_first(1)
    og_own[...] = padded(og_ref).astype(F32)
    schedule = [
        [lambda: weight_near(0)],
        [lambda: weight_near(1)],
        [lambda: weight_column(0)],
        [lambda: weight_column(1), lambda: weight_crossed(0)],
        [lambda: weight_crossed(1)],
    ]

    for n, stop in enumerate(stops[1:]):
        ring_round(0, stop)
        ring_round(1, stop)
        last = n == len(stops) - 2
        for events in schedule[n:] if last else schedule[n : n + 1]:
            for event in events:
                event()

    if len(stops) == 1:
        for events in schedule:
            for event in events:
                event()

    ring_end(0)
    weight_all(0)

    tails = jnp.zeros((16, TOK), F32)
    for j in range(zs):
        tails = tails + xt_all[j, PAD - 16 : PAD, :].astype(F32)
    square_sum = jnp.sum(tails[8:16], axis=0, keepdims=True)
    scale_row = lax.rsqrt(square_sum * (1.0 / (zs * FEAT)) + epsilon)
    scale_wide = jnp.transpose(jnp.broadcast_to(scale_row, (TOK, TOK)))
    scale_two = jnp.concatenate([scale_wide, scale_wide], axis=1)
    pair = min(ys, 2)

    def project(source, weight, lanes):
        total = None
        for of_lo in range(los):
            for of_y in range(0, ys, pair):
                first = (of_lo * ys + of_y) * 2
                a = source[first : first + 2 * pair].reshape(2 * pair * PAD, TOK)
                b = weight[of_lo, of_y : of_y + pair, :, :, lanes]
                term = dot_tn(a, b.reshape(2 * pair * PAD, b.shape[-1]))
                total = term if total is None else total + term
        return total

    gathered = (kv_all, qd_all)
    half = TOK // 2

    def column(across):
        return 1 - lo if across else lo

    def slot_x(array):
        slot = gathered[array].at[lo, y, core]
        to = (d, ((1 - lo) * ys + y) * 2 + core, c)
        return remote(slot, slot, a_send.at[array, 1], a_recv.at[array, lo, y], to)

    def slot_y(array, across, up, start, size, to):
        slot = gathered[array].at[column(across), y_at(up), core, pl.ds(start, size)]
        recv = a_recv.at[array, column(across), y_at(up)]
        return remote(slot, slot, a_send.at[array, 0], recv, column_device(to))

    def slot_came(array, across, up):
        slot_y(array, across, up, 0, TOK, 0).wait_recv()

    def slot_out(array, across):
        if across:
            slot_came(array, 1, 0)
        if ys == 4:
            slot_y(array, across, 0, 0, TOK, 1).start()
            slot_y(array, across, 0, 0, TOK, -1).start()
        elif ys == 2:
            slot_y(array, across, 0, 0, TOK, 1).start()

    def slot_start(array):
        slot_x(array).start()
        slot_out(array, 0)

    def slot_near(array, across):
        if ys == 4:
            slot_came(array, across, -1)
            slot_y(array, across, -1, 0, half, 1).start()
            slot_came(array, across, 1)
            slot_y(array, across, 1, half, half, -1).start()
        elif ys == 2:
            slot_came(array, across, 1)

    def slot_far(array, across):
        if ys == 4:
            slot_came(array, across, 2)
        slot = gathered[array].at[column(across), :, core]
        remote(slot, slot, a_send.at[array, 2], asib_recv.at[array], sibling).start()

    def slot_all(array):
        slot = gathered[array].at[:, :, other]
        remote(slot, slot, a_send.at[array, 2], asib_recv.at[array], sibling).wait_recv()

    kv = (project(xt_all, wkv_all, slice(0, SLOT)) * scale_two).astype(BF16)
    kv_all[lo, y, core] = kv
    slot_start(0)
    ring_end(1)
    weight_all(1)
    queries = (project(xt_all, wqo_all, slice(0, WIDE)) * scale_wide).astype(BF16)
    out_dir = project(og_all, wqo_all, slice(WIDE, SLOT)).astype(BF16)
    scaled_queries = (queries.astype(F32) * 0.125).astype(BF16)
    qd_all[lo, y, core] = jnp.concatenate([scaled_queries, out_dir], axis=1)
    slot_start(1)
    low = lax.broadcasted_iota(jnp.int32, (TOK, WIDE), 1) < HDIM

    def stacked(a):
        wide = a.astype(F32)
        parts = [jnp.where(low, wide, 0.0), jnp.where(low, 0.0, wide)]
        return jnp.concatenate(parts, axis=0).astype(BF16)

    query_stack = stacked(scaled_queries)
    dir_stack = stacked(out_dir)

    def slots_of(ref, parity, lanes):
        return ref[:, :, parity, :, lanes].reshape(chips * TOK, lanes.stop - lanes.start)

    def scores_of(parity):
        keys = slots_of(kv_all, parity, slice(0, WIDE))
        scores = dot_nt(keys, query_stack)
        s_ref[:, :, parity] = scores.reshape(los, ys, TOK, SLOT)
        prob_grad = dot_nt(slots_of(kv_all, parity, slice(WIDE, SLOT)), dir_stack)
        dp_ref[:, :, parity] = prob_grad.reshape(los, ys, TOK, SLOT)
        kt_ref[parity] = jnp.transpose(keys)
        return jnp.max(scores.reshape(chips * TOK // 8, 8, SLOT), axis=0)

    slot_out(0, 1)
    slot_near(0, 0)
    slot_out(1, 1)
    slot_near(0, 1)
    slot_far(0, 0)
    slot_near(1, 0)
    slot_far(0, 1)
    most = scores_of(core)
    slot_near(1, 1)
    slot_far(1, 0)
    slot_all(0)
    most = jnp.max(jnp.maximum(most, scores_of(other)), axis=0, keepdims=True)

    def tile_at(i):
        return i // (2 * ys), lax.rem(i // 2, ys), lax.rem(i, 2)

    def folded(a):
        return jnp.sum(a.reshape(TOK // 8, 8, SLOT), axis=0)

    def expo_body(i, sums):
        at = tile_at(i)
        expo = jnp.exp(s_ref[at] - most)
        s_ref[at] = expo
        return sums[0] + folded(expo), sums[1] + folded(expo * dp_ref[at])

    zero = jnp.zeros((8, SLOT), F32)
    totals, delta = lax.fori_loop(0, rows, expo_body, (zero, zero), unroll=2)
    totals = jnp.sum(totals, axis=0, keepdims=True)
    inverse = 1.0 / totals
    delta = jnp.sum(delta, axis=0, keepdims=True) * inverse
    slot_far(1, 1)

    def stat_copy(i):
        to = lax.rem(r + i, rows)
        return remote(st_all.at[r], st_all.at[r], st_send, st_recv, (d, to, c))

    def small_came(ref, count, sem):
        some = ref.at[pl.ds(0, count)]
        remote(some, some, p_send.at[0], sem, sibling).wait_recv()

    st_all[r] = jnp.concatenate([most + jnp.log(totals), delta, jnp.zeros((6, SLOT), F32)], axis=0)

    def score_grad(i):
        at = tile_at(i)
        ds_ref[at] = (s_ref[at] * (dp_ref[at] - delta)).astype(BF16)

    def score_grad_body(i, nothing):
        stat_copy(lax.rem(rows // 2 + i, rows)).start()
        score_grad(i)
        return nothing

    stat_copy(rows // 2).start()
    lax.fori_loop(1, rows // 2, score_grad_body, 0)
    lax.fori_loop(rows // 2 + 1, rows, score_grad_body, 0)
    score_grad(0)
    score_grad(rows // 2)
    query_grad = jnp.zeros((WIDE, SLOT), F32)
    for parity in range(2):
        query_grad = query_grad + dot_nn(kt_ref[parity], slots_of(ds_ref, parity, slice(0, SLOT)))
    query_grad = query_grad * (inverse * 0.125)
    query_grad = jnp.concatenate([query_grad[0:HDIM, 0:TOK], query_grad[HDIM:WIDE, TOK:SLOT]], axis=0)
    query_grad = query_grad.astype(BF16)

    key_stack = stacked(kv[:, 0:WIDE])
    value_stack = stacked(kv[:, WIDE:SLOT])
    wide = pair * TOK
    blocks = [(of_lo, of_y) for of_lo in range(los) for of_y in range(0, ys, pair)]
    parities = (core, other)

    def own_scores(side):
        for n, (of_lo, of_y) in enumerate(blocks):
            block = qd_all[of_lo, of_y : of_y + pair, parities[side]].reshape(wide, SLOT)
            s2_ref[side * len(blocks) + n] = dot_nt(key_stack, block[:, 0:WIDE])
            dp2_ref[side * len(blocks) + n] = dot_nt(value_stack, block[:, WIDE:SLOT])

    own_scores(0)
    slot_all(1)
    own_scores(1)
    small_came(st_all, rows - 1, st_recv)

    for side in range(2):
        for n, (of_lo, of_y) in enumerate(blocks):
            stats = [st_all[(of_lo * ys + of_y + i) * 2 + parities[side]] for i in range(pair)]
            at = side * len(blocks) + n
            lanes = slice(at * wide, (at + 1) * wide)
            for head in range(2):
                part = slice(head * TOK, (head + 1) * TOK)
                total = jnp.concatenate([stat[0:1, part] for stat in stats], axis=1)
                shift = jnp.concatenate([stat[1:2, part] for stat in stats], axis=1)
                probs = jnp.exp(s2_ref[at, part] - total)
                p2_ref[part, lanes] = probs.astype(BF16)
                ds2_ref[part, lanes] = (probs * (dp2_ref[at, part] - shift)).astype(BF16)

    key_grad = jnp.zeros((SLOT, WIDE), F32)
    value_grad = jnp.zeros((SLOT, WIDE), F32)
    for side in range(2):
        lanes = slice(side * chips * TOK, (side + 1) * chips * TOK)
        key_grad = key_grad + dot_nn(ds2_ref[:, lanes], slots_of(qd_all, parities[side], slice(0, WIDE)))
        value_grad = value_grad + dot_nn(p2_ref[:, lanes], slots_of(qd_all, parities[side], slice(WIDE, SLOT)))
    key_grad = jnp.where(low, key_grad[0:TOK], key_grad[TOK:SLOT])
    value_grad = jnp.where(low, value_grad[0:TOK], value_grad[TOK:SLOT])
    kv_grad = jnp.concatenate([key_grad, value_grad], axis=1)
    turned = jnp.concatenate([jnp.transpose(key_grad), jnp.transpose(value_grad)], axis=0).astype(BF16)
    kv_grad = kv_grad.astype(BF16)
    grads_turned = jnp.concatenate([turned, query_grad], axis=0)

    queries_turned = dot_nt(eye(WIDE, WIDE), queries)
    inner = jnp.sum(query_grad.astype(F32) * queries_turned, axis=0, keepdims=True)
    kv_inner = kv_grad.astype(F32) * kv.astype(F32)
    kv_hi = kv_inner.astype(BF16)
    kv_lo = (kv_inner - kv_hi.astype(F32)).astype(BF16)
    ones = jnp.ones((8, SLOT), BF16)
    kv_inner = dot_nt(ones, kv_hi) + dot_nt(ones, kv_lo)
    inner = inner + kv_inner[0:1]

    def partials(places):
        slots = []
        for by in places:
            j = z_at(by)
            at = (j // (2 * ys), lax.rem(j // 2, ys), lax.rem(j, 2))
            slots.append(jnp.concatenate([wkv_all[at], wqo_all[at + (slice(None), slice(0, WIDE))]], axis=1))
        value = dot_nn(jnp.concatenate(slots, axis=0), grads_turned)
        parts = [value[i * PAD : (i + 1) * PAD] for i in range(len(places))]
        return [jnp.where(row_at == FEAT, inner, part) for part in parts]

    some = pl.ds(0, zs - 1)
    for i in range(2):
        sent(streams[i].at[some], z_send.at[i])
        for group, sems, x_slots in ((weights[i], w_send, slice(0, ys)), (gathered[i], a_send, slice(0, 1))):
            if ys > 1:
                columns = slice(0, 1) if group is weights[i] else slice(0, 2)
                sent(group.at[columns, pl.ds(0, ys - 1), 0], sems.at[i, 0])
            sent(group.at[0, x_slots, 0], sems.at[i, 1])
            sent(group.at[:, :, 0], sems.at[i, 2])

    sent(st_all.at[pl.ds(0, rows - 1)], st_send)

    far = 2 * quarter

    def rs_leaf_copy(side, m):
        to = z_device(-1 if side else 1)
        return remote(rs_leaf_tx.at[side, m], rs_leaf.at[side, m], rs_send.at[side], rs_recv.at[side, 1, m], to)

    def rs_hub_copy(side, k):
        to = z_device(-2 if side else 2)
        return remote(rs_hub_tx.at[side, k], rs_hub.at[side, k], rs_send.at[side], rs_recv.at[side, 0, k], to)

    def leaf(side, m, part):
        rs_leaf_tx[side, m] = part.astype(BF16)
        rs_leaf_copy(side, m).start()

    hub_part, right_part, left_part = partials([far, far - 1, 1 - far])
    rs_hub_tx[0, 0] = hub_part.astype(BF16)
    rs_hub_copy(0, 0).start()
    leaf(0, 0, right_part)
    leaf(1, 0, left_part)
    for k in range(1, quarter):
        by = far - 2 * k
        to_right, to_left, right_part, left_part = partials([by, -by, by - 1, 1 - by])
        rs_hub_copy(0, k - 1).wait_recv()
        rs_leaf_copy(0, k - 1).wait_recv()
        total = to_right + rs_hub[0, k - 1].astype(F32) + rs_leaf[0, k - 1].astype(F32)
        rs_hub_tx[0, k] = total.astype(BF16)
        rs_hub_copy(0, k).start()
        rs_leaf_copy(1, k - 1).wait_recv()
        total = to_left + rs_leaf[1, k - 1].astype(F32)
        if k > 1:
            rs_hub_copy(1, k - 2).wait_recv()
            total = total + rs_hub[1, k - 2].astype(F32)
        rs_hub_tx[1, k - 1] = total.astype(BF16)
        rs_hub_copy(1, k - 1).start()
        leaf(0, k, right_part)
        leaf(1, k, left_part)

    own = partials([0])[0]
    for side in range(2):
        last = quarter - 1 - side
        rs_leaf_copy(side, quarter - 1).wait_recv()
        own = own + rs_leaf[side, quarter - 1].astype(F32)
        if last >= 0:
            rs_hub_copy(side, last).wait_recv()
            own = own + rs_hub[side, last].astype(F32)

    inner = own[FEAT : FEAT + 1] * (1.0 / (zs * FEAT))
    scaled = own * gain_own[...]
    normalized = xt_own[...] * scale_row
    raw = og_own[...] + scale_row * (scaled - normalized * inner)
    power = jnp.sum((raw * raw).reshape(PAD // 8, 8, TOK), axis=0)

    def far_first(n):
        return sorted(range(1, n), key=lambda i: -min(i, n - i))

    def power_stage(stage, landing, me, n, device):
        copies = [
            remote(pw_tx.at[stage], landing.at[me], p_send.at[stage], p_recv.at[stage], device(i)) for i in far_first(n)
        ]
        for copy in copies:
            copy.start()
        return copies

    def power_column(i):
        at = lax.rem(y * 2 + core + i, 2 * ys)
        return (d, lo * ys * 2 + at, c)

    def power_x(i):
        return plane_device(lax.rem(x + i, xs) * ys + y)

    stages = (
        (pw0, y * 2 + core, 2 * ys, power_column),
        (pw1, x, xs, power_x),
        (pw2, c, zs, z_device),
    )
    for stage, (landing, me, n, device) in enumerate(stages):
        pw_tx[stage] = power
        landing[me] = power
        power_stage(stage, landing, me, n, device)
        if stage == 0:
            sent(xt_all.at[pl.ds(0, far)], rs_send.at[0])
            sent(xt_all.at[pl.ds(0, far - 1)], rs_send.at[1])
        small_came(landing, n - 1, p_recv.at[stage])
        sent(landing.at[pl.ds(0, n - 1)], p_send.at[stage])
        power = jnp.sum(landing[...], axis=0)

    power = jnp.sum(power, axis=0, keepdims=True)
    power = jnp.sum(power, axis=1, keepdims=True)
    cells = depths * seq * zs * FEAT
    final = raw * lax.rsqrt(power * (1.0 / cells) + epsilon)
    out_ref[...] = final[0:FEAT].astype(BF16)


def sizes_of(mesh):
    depths, rows, zs = mesh.shape["depth"], mesh.shape["row"], mesh.shape["col"]
    los = 2
    return depths, los, rows // (2 * los), zs


def solution(mesh):
    depths, los, ys, zs = sizes_of(mesh)
    chips, planes = los * ys, depths * los * ys
    rows = chips * 2
    quarter = zs // 4
    dma = pltpu.SemaphoreType.DMA
    scratch = [
        *([pltpu.VMEM((FEAT, TOK), BF16)] * 6),
        pltpu.VMEM((FEAT,), BF16),
        pltpu.VMEM((zs, PAD, TOK), BF16),
        pltpu.VMEM((zs, PAD, TOK), BF16),
        pltpu.VMEM((los, ys, 2, PAD, SLOT), BF16),
        pltpu.VMEM((los, ys, 2, PAD, SLOT), BF16),
        pltpu.VMEM((los, ys, 2, TOK, SLOT), BF16),
        pltpu.VMEM((los, ys, 2, TOK, SLOT), BF16),
        pltpu.VMEM((rows, 8, SLOT), F32),
        pltpu.VMEM((PAD, TOK), F32),
        pltpu.VMEM((PAD, TOK), F32),
        pltpu.VMEM((PAD, TOK), F32),
        pltpu.VMEM((los, ys, 2, TOK, SLOT), F32),
        pltpu.VMEM((los, ys, 2, TOK, SLOT), F32),
        pltpu.VMEM((2, WIDE, chips * TOK), BF16),
        pltpu.VMEM((los, ys, 2, TOK, SLOT), BF16),
        pltpu.VMEM((rows // min(ys, 2), SLOT, min(ys, 2) * TOK), F32),
        pltpu.VMEM((rows // min(ys, 2), SLOT, min(ys, 2) * TOK), F32),
        pltpu.VMEM((SLOT, rows * TOK), BF16),
        pltpu.VMEM((SLOT, rows * TOK), BF16),
        *([pltpu.VMEM((2, quarter, PAD, TOK), BF16)] * 4),
        pltpu.VMEM((3, 8, TOK), F32),
        pltpu.VMEM((2 * ys, 8, TOK), F32),
        pltpu.VMEM((depths * los, 8, TOK), F32),
        pltpu.VMEM((zs, 8, TOK), F32),
        dma((7,)),
        dma((2,)), dma((2, 2, 2 * quarter)),
        dma((2, 3)), dma((2, ys + 1)), dma((2,)),
        dma((2, 3)), dma((2, los, ys)), dma((2,)),
        dma, dma,
        dma((2,)), dma((2, 2, quarter)),
        dma((3,)), dma((3,)),
    ]

    def shards(latents, out_grad, w_query, w_key, w_value, w_out, gain):
        return pl.pallas_call(
            functools.partial(kernel, (depths, los, ys, zs)),
            out_shape=jax.ShapeDtypeStruct((FEAT, TOK), BF16),
            in_specs=[pl.BlockSpec(memory_space=pl.ANY)] * 7,
            out_specs=pl.BlockSpec(memory_space=pltpu.VMEM),
            scratch_shapes=scratch,
            compiler_params=pltpu.CompilerParams(
                collective_id=0, has_side_effects=True, vmem_limit_bytes=56 * 1024 * 1024
            ),
        )(latents.T, out_grad.T, w_query, w_key, w_value, w_out, gain).T

    return jax.shard_map(
        shards,
        mesh=mesh,
        in_specs=(
            P(("depth", "row"), "col"),
            P(("depth", "row"), "col"),
            P("row", "col"),
            P("row", "col"),
            P("row", "col"),
            P("row", "col"),
            P("col"),
        ),
        out_specs=P(("depth", "row"), "col"),
        check_vma=False,
    )
```

```python
import functools

import jax
import jax.numpy as jnp
from jax import lax
from jax.experimental import pallas as pl
from jax.experimental.pallas import tpu as pltpu
from jax.sharding import PartitionSpec as P

MESH = pl.DeviceIdType.MESH
F32 = jnp.float32
BF16 = jnp.bfloat16
FEAT = 152
PAD = 160
HALF = 80
TOK = 128
WIDE = 128
HDIM = 64
SLOT = 256
epsilon = 1e-06


def dot_nt(a, b):
    return lax.dot_general(a, b, (((1,), (1,)), ((), ())), preferred_element_type=F32)


def dot_tn(a, b):
    return lax.dot_general(a, b, (((0,), (0,)), ((), ())), preferred_element_type=F32)


def dot_nn(a, b):
    return jnp.dot(a, b, preferred_element_type=F32)


def eye(rows, columns):
    at = lax.broadcasted_iota(jnp.int32, (rows, columns), 0)
    to = lax.broadcasted_iota(jnp.int32, (rows, columns), 1)
    return jnp.where(at == to, 1.0, 0.0).astype(BF16)


def kernel(
    sizes,
    lat_hbm, og_hbm, wq_hbm, wk_hbm, wv_hbm, wo_hbm, gain_hbm,
    out_ref,
    lat_ref, og_ref, wq_ref, wk_ref, wv_ref, wo_ref, gain_ref,
    xt_all, og_all, xn_all, on_all, wkv_all, wqo_all, kv_all, qd_all, st_all,
    xt_own, og_own, gain_own,
    s_ref, dp_ref, kt_ref, ds_ref, s2_ref, dp2_ref, p2_ref, ds2_ref,
    rs_leaf_tx, rs_hub_tx, rs_leaf, rs_hub,
    pw_tx, pw0, pw1, pw2,
    in_sem,
    z_send, z_recv,
    w_send, w_recv, wsib_recv,
    a_send, a_recv, asib_recv,
    st_send, st_recv,
    rs_send, rs_recv,
    p_send, p_recv,
):
    depths, los, ys, zs = sizes
    xs = depths * los
    chips = los * ys
    planes = xs * ys
    rows = chips * 2
    seq = rows * TOK
    quarter = zs // 4

    d = lax.axis_index("depth")
    r = lax.axis_index("row")
    c = lax.axis_index("col")
    core = lax.rem(r, 2)
    other = 1 - core
    chip = r // 2
    lo = chip // ys
    y = lax.rem(chip, ys)
    x = d * los + lo
    here = x * ys + y

    sibling = (d, chip * 2 + other, c)

    def z_at(by):
        return lax.rem(c + by % zs, zs)

    def z_device(by):
        return (d, r, z_at(by))

    def plane_device(at):
        to_x, to_y = at // ys, lax.rem(at, ys)
        return (to_x // los, (lax.rem(to_x, los) * ys + to_y) * 2 + core, c)

    def remote(src, dst, send, recv, device):
        return pltpu.make_async_remote_copy(
            src_ref=src, dst_ref=dst, send_sem=send, recv_sem=recv, device_id=device, device_id_type=MESH
        )

    inputs = (lat_hbm, og_hbm, gain_hbm, wk_hbm, wv_hbm, wq_hbm, wo_hbm)
    staged = (lat_ref, og_ref, gain_ref, wk_ref, wv_ref, wq_ref, wo_ref)
    fetches = [pltpu.make_async_copy(a, b, in_sem.at[i]) for i, (a, b) in enumerate(zip(inputs, staged))]
    for i in (0, 2, 1, 3, 4, 5, 6):
        fetches[i].start()

    near_z = sorted({by % zs for by in (1, -1, 2, -2)})
    near_y = sorted({by % ys for by in (1, -1)} - {0})
    near_x = sorted({by % xs for by in (1, -1)})
    barrier = pltpu.get_barrier_semaphore()
    partners = [(d, r, lax.rem(c + by, zs)) for by in near_z]
    partners += [plane_device(x * ys + lax.rem(y + by, ys)) for by in near_y]
    partners += [plane_device(lax.rem(x + by, xs) * ys + y) for by in near_x]
    partners += [sibling]
    for device in partners:
        pl.semaphore_signal(barrier, inc=1, device_id=device, device_id_type=MESH)

    fetches[0].wait()
    fetches[2].wait()

    row_at = lax.broadcasted_iota(jnp.int32, (PAD, TOK), 0)
    nothing = jnp.zeros((PAD - FEAT, WIDE), BF16)

    def padded(ref):
        return jnp.concatenate([ref[...], nothing], axis=0)

    xt = padded(lat_ref).astype(F32)
    gain_wide = dot_nt(eye(PAD, FEAT) * gain_ref[...].reshape(1, FEAT), jnp.ones((TOK, FEAT), BF16))
    squares = jnp.sum(xt * xt, axis=0, keepdims=True)
    square_hi = squares.astype(BF16).astype(F32)
    rest = squares - square_hi
    square_mid = rest.astype(BF16).astype(F32)
    square_lo = rest - square_mid
    sent = xt * gain_wide
    sent = jnp.where(row_at == FEAT, square_hi, sent)
    sent = jnp.where(row_at == FEAT + 1, square_mid, sent)
    sent = jnp.where(row_at == FEAT + 2, square_lo, sent)
    xt_all[c] = sent.astype(BF16)
    xt_own[...] = xt
    gain_own[...] = gain_wide
    pl.semaphore_wait(barrier, len(partners))

    streams = (xt_all, og_all)

    def edges(most):
        a, found = 0, []
        while a < most:
            found += [(a, a + 1)]
            a += 1
        return found

    ways = (edges(zs // 2), edges(zs - 1 - zs // 2))
    stops = sorted({a for way in ways for a, b in way})

    def ring(stream, side, a, b):
        sign = -1 if side else 1
        slot = streams[stream].at[z_at(-sign * a)]
        return remote(slot, slot, z_send.at[stream], z_recv.at[stream, side, b - 1], z_device(sign * (b - a)))

    def ring_came(stream, side, b):
        sign = -1 if side else 1
        slot = streams[stream].at[z_at(-sign * b)]
        remote(slot, slot, z_send.at[stream], z_recv.at[stream, side, b - 1], sibling).wait_recv()

    turn = eye(TOK, TOK)

    def turn_block(stream, by):
        j = z_at(by)
        (xn_all, on_all)[stream][j] = dot_nt(turn, streams[stream][j]).astype(BF16)

    def ring_round(stream, stop):
        sides = [side for side in range(2) if (stop, stop + 1) in ways[side]]
        for side in sides:
            if stop:
                ring_came(stream, side, stop)
            ring(stream, side, stop, stop + 1).start()

    def ring_turn(stream, stop):
        turn_block(stream, -stop)
        if stop and (stop, stop + 1) in ways[1]:
            turn_block(stream, stop)

    def ring_end(stream):
        for side in range(2):
            stop = len(ways[side])
            if stop:
                ring_came(stream, side, stop)
                turn_block(stream, stop if side else -stop)

    def column_device(up):
        return (d, (lo * ys + lax.rem(y + up % ys, ys)) * 2 + core, c)

    def x_device(by):
        return plane_device(lax.rem(x + by % xs, xs) * ys + y)

    def y_at(up):
        return lax.rem(y + up % ys, ys)

    weights = (wkv_all, wqo_all)

    def weight_y(array, up, start, size, to):
        slot = weights[array].at[lo, y_at(up), core, pl.ds(start, size)]
        return remote(slot, slot, w_send.at[array, 0], w_recv.at[array, y_at(up)], column_device(to))

    def weight_y_came(array, up):
        weight_y(array, up, 0, PAD, 0).wait_recv()

    def weight_x(array, side):
        slot = weights[array].at[lo, :, core, pl.ds(side * HALF, HALF)]
        return remote(slot, slot, w_send.at[array, 1], w_recv.at[array, ys], x_device(-1 if side else 1))

    def weight_x_one(array, up):
        for side in range(2):
            slot = weights[array].at[lo, y_at(up), core, pl.ds(side * HALF, HALF)]
            to = x_device(-1 if side else 1)
            remote(slot, slot, w_send.at[array, 1], w_recv.at[array, ys], to).start()

    def weight_sibling(array, of_lo):
        slot = weights[array].at[of_lo, :, core]
        return remote(slot, slot, w_send.at[array, 2], wsib_recv.at[array], sibling)

    def weight_first(array):
        if ys == 4:
            weight_y(array, 0, 0, PAD, 1).start()
            weight_y(array, 0, 0, PAD, -1).start()
        elif ys == 2:
            weight_y(array, 0, 0, PAD, 1).start()

    def weight_near(array):
        if ys == 4:
            weight_y_came(array, -1)
            weight_y(array, -1, 0, HALF, 1).start()
            weight_y_came(array, 1)
            weight_y(array, 1, HALF, HALF, -1).start()
            if array == 0:
                weight_x_one(array, -1)
                weight_x_one(array, 1)
        elif ys == 2:
            weight_y_came(array, 1)
            if array == 0:
                weight_x_one(array, 1)

    def weight_column(array):
        if ys == 4:
            weight_y_came(array, 2)
            if array == 0:
                weight_x_one(array, 2)
        if array == 1:
            weight_x(array, 0).start()
            weight_x(array, 1).start()
        weight_sibling(array, lo).start()

    def weight_crossed(array):
        slot = weights[array].at[1 - lo, :, core]
        remote(slot, slot, w_send.at[array, 2], w_recv.at[array, ys], sibling).wait_recv()
        weight_sibling(array, 1 - lo).start()

    def weight_all(array):
        slot = weights[array].at[:, :, other]
        remote(slot, slot, w_send.at[array, 2], wsib_recv.at[array], sibling).wait_recv()

    def sent(ref, sem):
        remote(ref, ref, sem, p_recv.at[0], sibling).wait_send()

    ring_round(0, 0)
    fetches[1].wait()
    og_all[c] = padded(og_ref)
    ring_round(1, 0)
    fetches[3].wait()
    fetches[4].wait()
    wkv_all[lo, y, core] = jnp.concatenate([padded(wk_ref), padded(wv_ref)], axis=1)
    weight_first(0)
    weight_x_one(0, 0)
    fetches[5].wait()
    fetches[6].wait()
    wqo_all[lo, y, core] = jnp.concatenate([padded(wq_ref), padded(wo_ref)], axis=1)
    weight_first(1)
    og_own[...] = padded(og_ref).astype(F32)
    ring_turn(0, 0)
    ring_turn(1, 0)
    schedule = [
        [lambda: weight_near(0)],
        [lambda: weight_near(1)],
        [lambda: weight_column(0)],
        [lambda: weight_column(1)],
        [lambda: weight_crossed(0)],
        [],
        [lambda: weight_crossed(1)],
    ]

    for n, stop in enumerate(stops[1:]):
        ring_round(0, stop)
        ring_round(1, stop)
        ring_turn(0, stop)
        ring_turn(1, stop)
        last = n == len(stops) - 2
        for events in schedule[n:] if last else schedule[n : n + 1]:
            for event in events:
                event()

    if len(stops) == 1:
        for events in schedule:
            for event in events:
                event()

    ring_end(0)
    weight_all(0)

    tails = jnp.zeros((16, TOK), F32)
    for j in range(zs):
        tails = tails + xt_all[j, PAD - 16 : PAD, :].astype(F32)
    square_sum = jnp.sum(tails[8:16], axis=0, keepdims=True)
    scale_row = lax.rsqrt(square_sum * (1.0 / (zs * FEAT)) + epsilon)
    scale_wide = jnp.transpose(jnp.broadcast_to(scale_row, (TOK, TOK)))
    scale_two = jnp.concatenate([scale_wide, scale_wide], axis=1)
    pair = min(ys, 2)

    def project(source, weight, lanes):
        total = None
        for j in range(zs):
            at = (j // (2 * ys), j // 2 % ys, j % 2, slice(None), lanes)
            term = dot_nn(source[j], weight[at])
            total = term if total is None else total + term
        return total

    gathered = (kv_all, qd_all)
    half = TOK // 2

    def column(across):
        return 1 - lo if across else lo

    def slot_x(array):
        slot = gathered[array].at[lo, y, core]
        to = (d, ((1 - lo) * ys + y) * 2 + core, c)
        return remote(slot, slot, a_send.at[array, 1], a_recv.at[array, lo, y], to)

    def slot_y(array, across, up, start, size, to):
        slot = gathered[array].at[column(across), y_at(up), core, pl.ds(start, size)]
        recv = a_recv.at[array, column(across), y_at(up)]
        return remote(slot, slot, a_send.at[array, 0], recv, column_device(to))

    def slot_came(array, across, up):
        slot_y(array, across, up, 0, TOK, 0).wait_recv()

    def slot_out(array, across):
        if across:
            slot_came(array, 1, 0)
        if ys == 4:
            slot_y(array, across, 0, 0, TOK, 1).start()
            slot_y(array, across, 0, 0, TOK, -1).start()
        elif ys == 2:
            slot_y(array, across, 0, 0, TOK, 1).start()

    def slot_start(array):
        slot_x(array).start()
        slot_out(array, 0)

    def slot_near(array, across):
        if ys == 4:
            slot_came(array, across, -1)
            slot_y(array, across, -1, 0, half, 1).start()
            slot_came(array, across, 1)
            slot_y(array, across, 1, half, half, -1).start()
        elif ys == 2:
            slot_came(array, across, 1)

    def slot_far(array, across):
        if ys == 4:
            slot_came(array, across, 2)
        slot = gathered[array].at[column(across), :, core]
        remote(slot, slot, a_send.at[array, 2], asib_recv.at[array], sibling).start()

    def slot_all(array):
        slot = gathered[array].at[:, :, other]
        remote(slot, slot, a_send.at[array, 2], asib_recv.at[array], sibling).wait_recv()

    kv = (project(xn_all, wkv_all, slice(0, SLOT)) * scale_two).astype(BF16)
    kv_all[lo, y, core] = kv
    slot_start(0)
    ring_end(1)
    weight_all(1)
    queries = (project(xn_all, wqo_all, slice(0, WIDE)) * scale_wide).astype(BF16)
    out_dir = project(on_all, wqo_all, slice(WIDE, SLOT)).astype(BF16)
    scaled_queries = (queries.astype(F32) * 0.125).astype(BF16)
    qd_all[lo, y, core] = jnp.concatenate([scaled_queries, out_dir], axis=1)
    slot_start(1)
    low = lax.broadcasted_iota(jnp.int32, (TOK, WIDE), 1) < HDIM

    def stacked(a):
        wide = a.astype(F32)
        parts = [jnp.where(low, wide, 0.0), jnp.where(low, 0.0, wide)]
        return jnp.concatenate(parts, axis=0).astype(BF16)

    query_stack = stacked(scaled_queries)
    dir_stack = stacked(out_dir)

    def slots_of(ref, parity, lanes):
        return ref[:, :, parity, :, lanes].reshape(chips * TOK, lanes.stop - lanes.start)

    def scores_of(parity):
        keys = slots_of(kv_all, parity, slice(0, WIDE))
        scores = dot_nt(keys, query_stack)
        s_ref[:, :, parity] = scores.reshape(los, ys, TOK, SLOT)
        prob_grad = dot_nt(slots_of(kv_all, parity, slice(WIDE, SLOT)), dir_stack)
        dp_ref[:, :, parity] = prob_grad.reshape(los, ys, TOK, SLOT)
        kt_ref[parity] = jnp.transpose(keys)
        return jnp.max(scores.reshape(chips * TOK // 8, 8, SLOT), axis=0)

    slot_out(0, 1)
    slot_near(0, 0)
    slot_out(1, 1)
    slot_near(0, 1)
    slot_far(0, 0)
    slot_near(1, 0)
    slot_far(0, 1)
    most = scores_of(core)
    slot_near(1, 1)
    slot_far(1, 0)
    slot_all(0)
    most = jnp.max(jnp.maximum(most, scores_of(other)), axis=0, keepdims=True)

    def tile_at(i):
        return i // (2 * ys), lax.rem(i // 2, ys), lax.rem(i, 2)

    def folded(a):
        return jnp.sum(a.reshape(TOK // 8, 8, SLOT), axis=0)

    def expo_body(i, sums):
        at = tile_at(i)
        expo = jnp.exp(s_ref[at] - most)
        s_ref[at] = expo
        return sums[0] + folded(expo), sums[1] + folded(expo * dp_ref[at])

    zero = jnp.zeros((8, SLOT), F32)
    totals, delta = lax.fori_loop(0, rows, expo_body, (zero, zero), unroll=2)
    totals = jnp.sum(totals, axis=0, keepdims=True)
    inverse = 1.0 / totals
    delta = jnp.sum(delta, axis=0, keepdims=True) * inverse
    slot_far(1, 1)

    def stat_copy(i):
        to = lax.rem(r + i, rows)
        return remote(st_all.at[r], st_all.at[r], st_send, st_recv, (d, to, c))

    def small_came(ref, count, sem):
        some = ref.at[pl.ds(0, count)]
        remote(some, some, p_send.at[0], sem, sibling).wait_recv()

    st_all[r] = jnp.concatenate([most + jnp.log(totals), delta, jnp.zeros((6, SLOT), F32)], axis=0)

    def score_grad(i):
        at = tile_at(i)
        ds_ref[at] = (s_ref[at] * (dp_ref[at] - delta)).astype(BF16)

    def score_grad_body(i, nothing):
        stat_copy(lax.rem(rows // 2 + i, rows)).start()
        score_grad(i)
        return nothing

    stat_copy(rows // 2).start()
    lax.fori_loop(1, rows // 2, score_grad_body, 0)
    lax.fori_loop(rows // 2 + 1, rows, score_grad_body, 0)
    score_grad(0)
    score_grad(rows // 2)
    query_grad = jnp.zeros((WIDE, SLOT), F32)
    for parity in range(2):
        query_grad = query_grad + dot_nn(kt_ref[parity], slots_of(ds_ref, parity, slice(0, SLOT)))
    query_grad = query_grad * (inverse * 0.125)
    query_grad = jnp.concatenate([query_grad[0:HDIM, 0:TOK], query_grad[HDIM:WIDE, TOK:SLOT]], axis=0)
    query_grad = query_grad.astype(BF16)

    key_stack = stacked(kv[:, 0:WIDE])
    value_stack = stacked(kv[:, WIDE:SLOT])
    wide = pair * TOK
    blocks = [(of_lo, of_y) for of_lo in range(los) for of_y in range(0, ys, pair)]
    parities = (core, other)

    def own_scores(side):
        for n, (of_lo, of_y) in enumerate(blocks):
            block = qd_all[of_lo, of_y : of_y + pair, parities[side]].reshape(wide, SLOT)
            s2_ref[side * len(blocks) + n] = dot_nt(key_stack, block[:, 0:WIDE])
            dp2_ref[side * len(blocks) + n] = dot_nt(value_stack, block[:, WIDE:SLOT])

    own_scores(0)
    slot_all(1)
    own_scores(1)
    small_came(st_all, rows - 1, st_recv)

    for side in range(2):
        for n, (of_lo, of_y) in enumerate(blocks):
            stats = [st_all[(of_lo * ys + of_y + i) * 2 + parities[side]] for i in range(pair)]
            at = side * len(blocks) + n
            lanes = slice(at * wide, (at + 1) * wide)
            for head in range(2):
                part = slice(head * TOK, (head + 1) * TOK)
                total = jnp.concatenate([stat[0:1, part] for stat in stats], axis=1)
                shift = jnp.concatenate([stat[1:2, part] for stat in stats], axis=1)
                probs = jnp.exp(s2_ref[at, part] - total)
                p2_ref[part, lanes] = probs.astype(BF16)
                ds2_ref[part, lanes] = (probs * (dp2_ref[at, part] - shift)).astype(BF16)

    key_grad = jnp.zeros((SLOT, WIDE), F32)
    value_grad = jnp.zeros((SLOT, WIDE), F32)
    for side in range(2):
        lanes = slice(side * chips * TOK, (side + 1) * chips * TOK)
        key_grad = key_grad + dot_nn(ds2_ref[:, lanes], slots_of(qd_all, parities[side], slice(0, WIDE)))
        value_grad = value_grad + dot_nn(p2_ref[:, lanes], slots_of(qd_all, parities[side], slice(WIDE, SLOT)))
    key_grad = jnp.where(low, key_grad[0:TOK], key_grad[TOK:SLOT])
    value_grad = jnp.where(low, value_grad[0:TOK], value_grad[TOK:SLOT])
    kv_grad = jnp.concatenate([key_grad, value_grad], axis=1)
    turned = jnp.concatenate([jnp.transpose(key_grad), jnp.transpose(value_grad)], axis=0).astype(BF16)
    kv_grad = kv_grad.astype(BF16)
    grads_turned = jnp.concatenate([turned, query_grad], axis=0)

    queries_turned = dot_nt(eye(WIDE, WIDE), queries)
    inner = jnp.sum(query_grad.astype(F32) * queries_turned, axis=0, keepdims=True)
    kv_inner = kv_grad.astype(F32) * kv.astype(F32)
    kv_hi = kv_inner.astype(BF16)
    kv_lo = (kv_inner - kv_hi.astype(F32)).astype(BF16)
    ones = jnp.ones((8, SLOT), BF16)
    kv_inner = dot_nt(ones, kv_hi) + dot_nt(ones, kv_lo)
    inner = inner + kv_inner[0:1]

    def partials(places):
        slots = []
        for by in places:
            j = z_at(by)
            at = (j // (2 * ys), lax.rem(j // 2, ys), lax.rem(j, 2))
            slots.append(jnp.concatenate([wkv_all[at], wqo_all[at + (slice(None), slice(0, WIDE))]], axis=1))
        value = dot_nn(jnp.concatenate(slots, axis=0), grads_turned)
        parts = [value[i * PAD : (i + 1) * PAD] for i in range(len(places))]
        return [jnp.where(row_at == FEAT, inner, part) for part in parts]

    some = pl.ds(0, zs - 1)
    for i in range(2):
        sent(streams[i].at[some], z_send.at[i])
        for group, sems, x_slots in ((weights[i], w_send, slice(0, ys)), (gathered[i], a_send, slice(0, 1))):
            if ys > 1:
                columns = slice(0, 1) if group is weights[i] else slice(0, 2)
                sent(group.at[columns, pl.ds(0, ys - 1), 0], sems.at[i, 0])
            sent(group.at[0, x_slots, 0], sems.at[i, 1])
            sent(group.at[:, :, 0], sems.at[i, 2])

    sent(st_all.at[pl.ds(0, rows - 1)], st_send)

    far = 2 * quarter

    def rs_leaf_copy(side, m):
        to = z_device(-1 if side else 1)
        return remote(rs_leaf_tx.at[side, m], rs_leaf.at[side, m], rs_send.at[side], rs_recv.at[side, 1, m], to)

    def rs_hub_copy(side, k):
        to = z_device(-2 if side else 2)
        return remote(rs_hub_tx.at[side, k], rs_hub.at[side, k], rs_send.at[side], rs_recv.at[side, 0, k], to)

    def leaf(side, m, part):
        rs_leaf_tx[side, m] = part.astype(BF16)
        rs_leaf_copy(side, m).start()

    hub_part, right_part, left_part = partials([far, far - 1, 1 - far])
    rs_hub_tx[0, 0] = hub_part.astype(BF16)
    rs_hub_copy(0, 0).start()
    leaf(0, 0, right_part)
    leaf(1, 0, left_part)
    for k in range(1, quarter):
        by = far - 2 * k
        to_right, to_left, right_part, left_part = partials([by, -by, by - 1, 1 - by])
        rs_hub_copy(0, k - 1).wait_recv()
        rs_leaf_copy(0, k - 1).wait_recv()
        total = to_right + rs_hub[0, k - 1].astype(F32) + rs_leaf[0, k - 1].astype(F32)
        rs_hub_tx[0, k] = total.astype(BF16)
        rs_hub_copy(0, k).start()
        rs_leaf_copy(1, k - 1).wait_recv()
        total = to_left + rs_leaf[1, k - 1].astype(F32)
        if k > 1:
            rs_hub_copy(1, k - 2).wait_recv()
            total = total + rs_hub[1, k - 2].astype(F32)
        rs_hub_tx[1, k - 1] = total.astype(BF16)
        rs_hub_copy(1, k - 1).start()
        leaf(0, k, right_part)
        leaf(1, k, left_part)

    own = partials([0])[0]
    for side in range(2):
        last = quarter - 1 - side
        rs_leaf_copy(side, quarter - 1).wait_recv()
        own = own + rs_leaf[side, quarter - 1].astype(F32)
        if last >= 0:
            rs_hub_copy(side, last).wait_recv()
            own = own + rs_hub[side, last].astype(F32)

    inner = own[FEAT : FEAT + 1] * (1.0 / (zs * FEAT))
    scaled = own * gain_own[...]
    normalized = xt_own[...] * scale_row
    raw = og_own[...] + scale_row * (scaled - normalized * inner)
    power = jnp.sum((raw * raw).reshape(PAD // 8, 8, TOK), axis=0)

    def far_first(n):
        return sorted(range(1, n), key=lambda i: -min(i, n - i))

    def power_stage(stage, landing, me, n, device):
        copies = [
            remote(pw_tx.at[stage], landing.at[me], p_send.at[stage], p_recv.at[stage], device(i)) for i in far_first(n)
        ]
        for copy in copies:
            copy.start()
        return copies

    def power_column(i):
        at = lax.rem(y * 2 + core + i, 2 * ys)
        return (d, lo * ys * 2 + at, c)

    def power_x(i):
        return plane_device(lax.rem(x + i, xs) * ys + y)

    stages = (
        (pw0, y * 2 + core, 2 * ys, power_column),
        (pw1, x, xs, power_x),
        (pw2, c, zs, z_device),
    )
    for stage, (landing, me, n, device) in enumerate(stages):
        pw_tx[stage] = power
        landing[me] = power
        power_stage(stage, landing, me, n, device)
        if stage == 0:
            sent(xt_all.at[pl.ds(0, far)], rs_send.at[0])
            sent(xt_all.at[pl.ds(0, far - 1)], rs_send.at[1])
        small_came(landing, n - 1, p_recv.at[stage])
        sent(landing.at[pl.ds(0, n - 1)], p_send.at[stage])
        power = jnp.sum(landing[...], axis=0)

    power = jnp.sum(power, axis=0, keepdims=True)
    power = jnp.sum(power, axis=1, keepdims=True)
    cells = depths * seq * zs * FEAT
    final = raw * lax.rsqrt(power * (1.0 / cells) + epsilon)
    out_ref[...] = final[0:FEAT].astype(BF16)


def sizes_of(mesh):
    depths, rows, zs = mesh.shape["depth"], mesh.shape["row"], mesh.shape["col"]
    los = 2
    return depths, los, rows // (2 * los), zs


def solution(mesh):
    depths, los, ys, zs = sizes_of(mesh)
    chips, planes = los * ys, depths * los * ys
    rows = chips * 2
    quarter = zs // 4
    dma = pltpu.SemaphoreType.DMA
    scratch = [
        *([pltpu.VMEM((FEAT, TOK), BF16)] * 6),
        pltpu.VMEM((FEAT,), BF16),
        pltpu.VMEM((zs, PAD, TOK), BF16),
        pltpu.VMEM((zs, PAD, TOK), BF16),
        pltpu.VMEM((zs, TOK, PAD), BF16),
        pltpu.VMEM((zs, TOK, PAD), BF16),
        pltpu.VMEM((los, ys, 2, PAD, SLOT), BF16),
        pltpu.VMEM((los, ys, 2, PAD, SLOT), BF16),
        pltpu.VMEM((los, ys, 2, TOK, SLOT), BF16),
        pltpu.VMEM((los, ys, 2, TOK, SLOT), BF16),
        pltpu.VMEM((rows, 8, SLOT), F32),
        pltpu.VMEM((PAD, TOK), F32),
        pltpu.VMEM((PAD, TOK), F32),
        pltpu.VMEM((PAD, TOK), F32),
        pltpu.VMEM((los, ys, 2, TOK, SLOT), F32),
        pltpu.VMEM((los, ys, 2, TOK, SLOT), F32),
        pltpu.VMEM((2, WIDE, chips * TOK), BF16),
        pltpu.VMEM((los, ys, 2, TOK, SLOT), BF16),
        pltpu.VMEM((rows // min(ys, 2), SLOT, min(ys, 2) * TOK), F32),
        pltpu.VMEM((rows // min(ys, 2), SLOT, min(ys, 2) * TOK), F32),
        pltpu.VMEM((SLOT, rows * TOK), BF16),
        pltpu.VMEM((SLOT, rows * TOK), BF16),
        *([pltpu.VMEM((2, quarter, PAD, TOK), BF16)] * 4),
        pltpu.VMEM((3, 8, TOK), F32),
        pltpu.VMEM((2 * ys, 8, TOK), F32),
        pltpu.VMEM((depths * los, 8, TOK), F32),
        pltpu.VMEM((zs, 8, TOK), F32),
        dma((7,)),
        dma((2,)), dma((2, 2, 2 * quarter)),
        dma((2, 3)), dma((2, ys + 1)), dma((2,)),
        dma((2, 3)), dma((2, los, ys)), dma((2,)),
        dma, dma,
        dma((2,)), dma((2, 2, quarter)),
        dma((3,)), dma((3,)),
    ]

    def shards(latents, out_grad, w_query, w_key, w_value, w_out, gain):
        return pl.pallas_call(
            functools.partial(kernel, (depths, los, ys, zs)),
            out_shape=jax.ShapeDtypeStruct((FEAT, TOK), BF16),
            in_specs=[pl.BlockSpec(memory_space=pl.ANY)] * 7,
            out_specs=pl.BlockSpec(memory_space=pltpu.VMEM),
            scratch_shapes=scratch,
            compiler_params=pltpu.CompilerParams(
                collective_id=0, has_side_effects=True, vmem_limit_bytes=56 * 1024 * 1024
            ),
        )(latents.T, out_grad.T, w_query, w_key, w_value, w_out, gain).T

    return jax.shard_map(
        shards,
        mesh=mesh,
        in_specs=(
            P(("depth", "row"), "col"),
            P(("depth", "row"), "col"),
            P("row", "col"),
            P("row", "col"),
            P("row", "col"),
            P("row", "col"),
            P("col"),
        ),
        out_specs=P(("depth", "row"), "col"),
        check_vma=False,
    )
```

```python
import functools

import jax
import jax.numpy as jnp
from jax import lax
from jax.experimental import pallas as pl
from jax.experimental.pallas import tpu as pltpu
from jax.sharding import PartitionSpec as P

MESH = pl.DeviceIdType.MESH
F32 = jnp.float32
BF16 = jnp.bfloat16
FEAT = 152
PAD = 160
HALF = 80
TOK = 128
WIDE = 128
HDIM = 64
SLOT = 256
epsilon = 1e-06


def dot_nt(a, b):
    return lax.dot_general(a, b, (((1,), (1,)), ((), ())), preferred_element_type=F32)


def dot_tn(a, b):
    return lax.dot_general(a, b, (((0,), (0,)), ((), ())), preferred_element_type=F32)


def dot_nn(a, b):
    return jnp.dot(a, b, preferred_element_type=F32)


def eye(rows, columns):
    at = lax.broadcasted_iota(jnp.int32, (rows, columns), 0)
    to = lax.broadcasted_iota(jnp.int32, (rows, columns), 1)
    return jnp.where(at == to, 1.0, 0.0).astype(BF16)


def kernel(
    sizes,
    lat_hbm, og_hbm, wq_hbm, wk_hbm, wv_hbm, wo_hbm, gain_hbm,
    out_ref,
    lat_ref, og_ref, wq_ref, wk_ref, wv_ref, wo_ref, gain_ref,
    xt_all, og_all, wkv_all, wqo_all, kv_all, qd_all, st_all,
    xt_own, og_own, gain_own,
    s_ref, dp_ref, kt_ref, ds_ref, s2_ref, dp2_ref, p2_ref, ds2_ref,
    rs_leaf_tx, rs_hub_tx, rs_leaf, rs_hub,
    pw_tx, pw0, pw1, pw2,
    in_sem,
    z_send, z_recv,
    w_send, w_recv, wsib_recv,
    a_send, a_recv, asib_recv,
    st_send, st_recv,
    rs_send, rs_recv,
    p_send, p_recv,
):
    depths, los, ys, zs = sizes
    xs = depths * los
    chips = los * ys
    planes = xs * ys
    rows = chips * 2
    seq = rows * TOK
    quarter = zs // 4

    d = lax.axis_index("depth")
    r = lax.axis_index("row")
    c = lax.axis_index("col")
    core = lax.rem(r, 2)
    other = 1 - core
    chip = r // 2
    lo = chip // ys
    y = lax.rem(chip, ys)
    x = d * los + lo
    here = x * ys + y

    sibling = (d, chip * 2 + other, c)

    def z_at(by):
        return lax.rem(c + by % zs, zs)

    def z_device(by):
        return (d, r, z_at(by))

    def plane_device(at):
        to_x, to_y = at // ys, lax.rem(at, ys)
        return (to_x // los, (lax.rem(to_x, los) * ys + to_y) * 2 + core, c)

    def remote(src, dst, send, recv, device):
        return pltpu.make_async_remote_copy(
            src_ref=src, dst_ref=dst, send_sem=send, recv_sem=recv, device_id=device, device_id_type=MESH
        )

    inputs = (lat_hbm, og_hbm, gain_hbm, wk_hbm, wv_hbm, wq_hbm, wo_hbm)
    staged = (lat_ref, og_ref, gain_ref, wk_ref, wv_ref, wq_ref, wo_ref)
    fetches = [pltpu.make_async_copy(a, b, in_sem.at[i]) for i, (a, b) in enumerate(zip(inputs, staged))]
    for i in (0, 2, 1, 3, 4, 5, 6):
        fetches[i].start()

    near_z = sorted({by % zs for by in (1, -1, 2, -2)})
    near_y = sorted({by % ys for by in (1, -1)} - {0})
    near_x = sorted({by % xs for by in (1, -1)})
    barrier = pltpu.get_barrier_semaphore()
    partners = [(d, r, lax.rem(c + by, zs)) for by in near_z]
    partners += [plane_device(x * ys + lax.rem(y + by, ys)) for by in near_y]
    partners += [plane_device(lax.rem(x + by, xs) * ys + y) for by in near_x]
    partners += [sibling]
    for device in partners:
        pl.semaphore_signal(barrier, inc=1, device_id=device, device_id_type=MESH)

    fetches[0].wait()
    fetches[2].wait()

    row_at = lax.broadcasted_iota(jnp.int32, (PAD, TOK), 0)
    nothing = jnp.zeros((PAD - FEAT, WIDE), BF16)

    def padded(ref):
        return jnp.concatenate([ref[...], nothing], axis=0)

    xt = padded(lat_ref).astype(F32)
    gain_wide = dot_nt(eye(PAD, FEAT) * gain_ref[...].reshape(1, FEAT), jnp.ones((TOK, FEAT), BF16))
    squares = jnp.sum(xt * xt, axis=0, keepdims=True)
    square_hi = squares.astype(BF16).astype(F32)
    rest = squares - square_hi
    square_mid = rest.astype(BF16).astype(F32)
    square_lo = rest - square_mid
    sent = xt * gain_wide
    sent = jnp.where(row_at == FEAT, square_hi, sent)
    sent = jnp.where(row_at == FEAT + 1, square_mid, sent)
    sent = jnp.where(row_at == FEAT + 2, square_lo, sent)
    xt_all[c] = sent.astype(BF16)
    xt_own[...] = xt
    gain_own[...] = gain_wide
    pl.semaphore_wait(barrier, len(partners))

    streams = (xt_all, og_all)

    def edges(most):
        a, found = 0, []
        while a < most:
            if a + 2 <= most and a < 4:
                found += [(a, a + 2), (a, a + 1)]
                a += 2
            else:
                found += [(a, a + 1)]
                a += 1
        return found

    ways = (edges(zs // 2), edges(zs - 1 - zs // 2))
    stops = sorted({a for way in ways for a, b in way})

    def ring(stream, side, a, b):
        sign = -1 if side else 1
        slot = streams[stream].at[z_at(-sign * a)]
        return remote(slot, slot, z_send.at[stream], z_recv.at[stream, side, b - 1], z_device(sign * (b - a)))

    def ring_came(stream, side, b):
        sign = -1 if side else 1
        slot = streams[stream].at[z_at(-sign * b)]
        remote(slot, slot, z_send.at[stream], z_recv.at[stream, side, b - 1], sibling).wait_recv()

    def ring_round(stream, stop):
        for side in range(2):
            out = [edge for edge in ways[side] if edge[0] == stop]
            if out and stop:
                ring_came(stream, side, stop)
            for edge in out:
                ring(stream, side, *edge).start()

    def ring_end(stream):
        for side in range(2):
            for a, b in ways[side]:
                if b not in [start for start, end in ways[side]]:
                    ring_came(stream, side, b)

    def column_device(up):
        return (d, (lo * ys + lax.rem(y + up % ys, ys)) * 2 + core, c)

    def x_device(by):
        return plane_device(lax.rem(x + by % xs, xs) * ys + y)

    def y_at(up):
        return lax.rem(y + up % ys, ys)

    weights = (wkv_all, wqo_all)

    def weight_y(array, up, start, size, to):
        slot = weights[array].at[lo, y_at(up), core, pl.ds(start, size)]
        return remote(slot, slot, w_send.at[array, 0], w_recv.at[array, y_at(up)], column_device(to))

    def weight_y_came(array, up):
        weight_y(array, up, 0, PAD, 0).wait_recv()

    def weight_x(array, side):
        slot = weights[array].at[lo, :, core, pl.ds(side * HALF, HALF)]
        return remote(slot, slot, w_send.at[array, 1], w_recv.at[array, ys], x_device(-1 if side else 1))

    def weight_x_one(array, up):
        for side in range(2):
            slot = weights[array].at[lo, y_at(up), core, pl.ds(side * HALF, HALF)]
            to = x_device(-1 if side else 1)
            remote(slot, slot, w_send.at[array, 1], w_recv.at[array, ys], to).start()

    def weight_sibling(array, of_lo):
        slot = weights[array].at[of_lo, :, core]
        return remote(slot, slot, w_send.at[array, 2], wsib_recv.at[array], sibling)

    def weight_first(array):
        if ys == 4:
            weight_y(array, 0, 0, PAD, 1).start()
            weight_y(array, 0, 0, PAD, -1).start()
        elif ys == 2:
            weight_y(array, 0, 0, PAD, 1).start()

    def weight_near(array):
        if ys == 4:
            weight_y_came(array, -1)
            weight_y(array, -1, 0, HALF, 1).start()
            weight_y_came(array, 1)
            weight_y(array, 1, HALF, HALF, -1).start()
            if array == 0:
                weight_x_one(array, -1)
                weight_x_one(array, 1)
        elif ys == 2:
            weight_y_came(array, 1)
            if array == 0:
                weight_x_one(array, 1)

    def weight_column(array):
        if ys == 4:
            weight_y_came(array, 2)
            if array == 0:
                weight_x_one(array, 2)
        if array == 1:
            weight_x(array, 0).start()
            weight_x(array, 1).start()
        weight_sibling(array, lo).start()

    def weight_crossed(array):
        slot = weights[array].at[1 - lo, :, core]
        remote(slot, slot, w_send.at[array, 2], w_recv.at[array, ys], sibling).wait_recv()
        weight_sibling(array, 1 - lo).start()

    def weight_all(array):
        slot = weights[array].at[:, :, other]
        remote(slot, slot, w_send.at[array, 2], wsib_recv.at[array], sibling).wait_recv()

    def sent(ref, sem):
        remote(ref, ref, sem, p_recv.at[0], sibling).wait_send()

    ring_round(0, 0)
    fetches[1].wait()
    og_all[c] = padded(og_ref)
    ring_round(1, 0)
    fetches[3].wait()
    fetches[4].wait()
    wkv_all[lo, y, core] = jnp.concatenate([padded(wk_ref), padded(wv_ref)], axis=1)
    weight_first(0)
    weight_x_one(0, 0)
    fetches[5].wait()
    fetches[6].wait()
    wqo_all[lo, y, core] = jnp.concatenate([padded(wq_ref), padded(wo_ref)], axis=1)
    weight_first(1)
    og_own[...] = padded(og_ref).astype(F32)
    schedule = [
        [lambda: weight_near(0)],
        [lambda: weight_near(1)],
        [lambda: weight_column(0)],
        [lambda: weight_crossed(0), lambda: weight_column(1)],
    ]

    for n, stop in enumerate(stops[1:]):
        ring_round(0, stop)
        ring_round(1, stop)
        last = n == len(stops) - 2
        for events in schedule[n:] if last else schedule[n : n + 1]:
            for event in events:
                event()

    if len(stops) == 1:
        for events in schedule:
            for event in events:
                event()

    ring_end(0)
    weight_all(0)

    tails = jnp.zeros((16, TOK), F32)
    for j in range(zs):
        tails = tails + xt_all[j, PAD - 16 : PAD, :].astype(F32)
    square_sum = jnp.sum(tails[8:16], axis=0, keepdims=True)
    scale_row = lax.rsqrt(square_sum * (1.0 / (zs * FEAT)) + epsilon)
    scale_wide = jnp.transpose(jnp.broadcast_to(scale_row, (TOK, TOK)))
    scale_two = jnp.concatenate([scale_wide, scale_wide], axis=1)
    pair = min(ys, 2)

    def project(source, weight, lanes):
        total = None
        for of_lo in range(los):
            for of_y in range(0, ys, pair):
                first = (of_lo * ys + of_y) * 2
                a = source[first : first + 2 * pair].reshape(2 * pair * PAD, TOK)
                b = weight[of_lo, of_y : of_y + pair, :, :, lanes]
                term = dot_tn(a, b.reshape(2 * pair * PAD, b.shape[-1]))
                total = term if total is None else total + term
        return total

    gathered = (kv_all, qd_all)
    half = TOK // 2

    def column(across):
        return 1 - lo if across else lo

    def slot_x(array):
        slot = gathered[array].at[lo, y, core]
        to = (d, ((1 - lo) * ys + y) * 2 + core, c)
        return remote(slot, slot, a_send.at[array, 1], a_recv.at[array, lo, y], to)

    def slot_y(array, across, up, start, size, to):
        slot = gathered[array].at[column(across), y_at(up), core, pl.ds(start, size)]
        recv = a_recv.at[array, column(across), y_at(up)]
        return remote(slot, slot, a_send.at[array, 0], recv, column_device(to))

    def slot_came(array, across, up):
        slot_y(array, across, up, 0, TOK, 0).wait_recv()

    def slot_out(array, across):
        if across:
            slot_came(array, 1, 0)
        if ys == 4:
            slot_y(array, across, 0, 0, TOK, 1).start()
            slot_y(array, across, 0, 0, TOK, -1).start()
        elif ys == 2:
            slot_y(array, across, 0, 0, TOK, 1).start()

    def slot_start(array):
        slot_x(array).start()
        slot_out(array, 0)

    def slot_near(array, across):
        if ys == 4:
            slot_came(array, across, -1)
            slot_y(array, across, -1, 0, half, 1).start()
            slot_came(array, across, 1)
            slot_y(array, across, 1, half, half, -1).start()
        elif ys == 2:
            slot_came(array, across, 1)

    def slot_far(array, across):
        if ys == 4:
            slot_came(array, across, 2)
        slot = gathered[array].at[column(across), :, core]
        remote(slot, slot, a_send.at[array, 2], asib_recv.at[array], sibling).start()

    def slot_all(array):
        slot = gathered[array].at[:, :, other]
        remote(slot, slot, a_send.at[array, 2], asib_recv.at[array], sibling).wait_recv()

    kv = (project(xt_all, wkv_all, slice(0, SLOT)) * scale_two).astype(BF16)
    kv_all[lo, y, core] = kv
    slot_start(0)
    slot_out(0, 1)
    slot_near(0, 0)
    weight_crossed(1)
    ring_end(1)
    weight_all(1)
    queries = (project(xt_all, wqo_all, slice(0, WIDE)) * scale_wide).astype(BF16)
    slot_near(0, 1)
    slot_far(0, 0)
    out_dir = project(og_all, wqo_all, slice(WIDE, SLOT)).astype(BF16)
    scaled_queries = (queries.astype(F32) * 0.125).astype(BF16)
    qd_all[lo, y, core] = jnp.concatenate([scaled_queries, out_dir], axis=1)
    slot_start(1)
    slot_far(0, 1)
    low = lax.broadcasted_iota(jnp.int32, (TOK, WIDE), 1) < HDIM

    def stacked(a):
        wide = a.astype(F32)
        parts = [jnp.where(low, wide, 0.0), jnp.where(low, 0.0, wide)]
        return jnp.concatenate(parts, axis=0).astype(BF16)

    query_stack = stacked(scaled_queries)
    dir_stack = stacked(out_dir)

    def slots_of(ref, parity, lanes):
        return ref[:, :, parity, :, lanes].reshape(chips * TOK, lanes.stop - lanes.start)

    def scores_of(parity):
        keys = slots_of(kv_all, parity, slice(0, WIDE))
        scores = dot_nt(keys, query_stack)
        s_ref[:, :, parity] = scores.reshape(los, ys, TOK, SLOT)
        prob_grad = dot_nt(slots_of(kv_all, parity, slice(WIDE, SLOT)), dir_stack)
        dp_ref[:, :, parity] = prob_grad.reshape(los, ys, TOK, SLOT)
        kt_ref[parity] = jnp.transpose(keys)
        return jnp.max(scores.reshape(chips * TOK // 8, 8, SLOT), axis=0)

    most = scores_of(core)
    slot_out(1, 1)
    slot_near(1, 0)
    slot_all(0)
    most = jnp.max(jnp.maximum(most, scores_of(other)), axis=0, keepdims=True)
    slot_near(1, 1)
    slot_far(1, 0)

    def tile_at(i):
        return i // (2 * ys), lax.rem(i // 2, ys), lax.rem(i, 2)

    def folded(a):
        return jnp.sum(a.reshape(TOK // 8, 8, SLOT), axis=0)

    def expo_body(i, sums):
        at = tile_at(i)
        expo = jnp.exp(s_ref[at] - most)
        s_ref[at] = expo
        return sums[0] + folded(expo), sums[1] + folded(expo * dp_ref[at])

    zero = jnp.zeros((8, SLOT), F32)
    totals, delta = lax.fori_loop(0, rows, expo_body, (zero, zero), unroll=2)
    totals = jnp.sum(totals, axis=0, keepdims=True)
    inverse = 1.0 / totals
    delta = jnp.sum(delta, axis=0, keepdims=True) * inverse
    slot_far(1, 1)

    def stat_copy(i):
        to = lax.rem(r + i, rows)
        return remote(st_all.at[r], st_all.at[r], st_send, st_recv, (d, to, c))

    def small_came(ref, count, sem):
        some = ref.at[pl.ds(0, count)]
        remote(some, some, p_send.at[0], sem, sibling).wait_recv()

    st_all[r] = jnp.concatenate([most + jnp.log(totals), delta, jnp.zeros((6, SLOT), F32)], axis=0)

    def score_grad(i):
        at = tile_at(i)
        ds_ref[at] = (s_ref[at] * (dp_ref[at] - delta)).astype(BF16)

    def score_grad_body(i, nothing):
        stat_copy(lax.rem(rows // 2 + i, rows)).start()
        score_grad(i)
        return nothing

    stat_copy(rows // 2).start()
    lax.fori_loop(1, rows // 2, score_grad_body, 0)
    lax.fori_loop(rows // 2 + 1, rows, score_grad_body, 0)
    score_grad(0)
    score_grad(rows // 2)
    query_grad = jnp.zeros((WIDE, SLOT), F32)
    for parity in range(2):
        query_grad = query_grad + dot_nn(kt_ref[parity], slots_of(ds_ref, parity, slice(0, SLOT)))
    query_grad = query_grad * (inverse * 0.125)
    query_grad = jnp.concatenate([query_grad[0:HDIM, 0:TOK], query_grad[HDIM:WIDE, TOK:SLOT]], axis=0)
    query_grad = query_grad.astype(BF16)

    key_stack = stacked(kv[:, 0:WIDE])
    value_stack = stacked(kv[:, WIDE:SLOT])
    wide = pair * TOK
    blocks = [(of_lo, of_y) for of_lo in range(los) for of_y in range(0, ys, pair)]
    parities = (core, other)

    def own_scores(side):
        for n, (of_lo, of_y) in enumerate(blocks):
            block = qd_all[of_lo, of_y : of_y + pair, parities[side]].reshape(wide, SLOT)
            s2_ref[side * len(blocks) + n] = dot_nt(key_stack, block[:, 0:WIDE])
            dp2_ref[side * len(blocks) + n] = dot_nt(value_stack, block[:, WIDE:SLOT])

    own_scores(0)
    slot_all(1)
    own_scores(1)
    small_came(st_all, rows - 1, st_recv)

    for side in range(2):
        for n, (of_lo, of_y) in enumerate(blocks):
            stats = [st_all[(of_lo * ys + of_y + i) * 2 + parities[side]] for i in range(pair)]
            at = side * len(blocks) + n
            lanes = slice(at * wide, (at + 1) * wide)
            for head in range(2):
                part = slice(head * TOK, (head + 1) * TOK)
                total = jnp.concatenate([stat[0:1, part] for stat in stats], axis=1)
                shift = jnp.concatenate([stat[1:2, part] for stat in stats], axis=1)
                probs = jnp.exp(s2_ref[at, part] - total)
                p2_ref[part, lanes] = probs.astype(BF16)
                ds2_ref[part, lanes] = (probs * (dp2_ref[at, part] - shift)).astype(BF16)

    key_grad = jnp.zeros((SLOT, WIDE), F32)
    value_grad = jnp.zeros((SLOT, WIDE), F32)
    for side in range(2):
        lanes = slice(side * chips * TOK, (side + 1) * chips * TOK)
        key_grad = key_grad + dot_nn(ds2_ref[:, lanes], slots_of(qd_all, parities[side], slice(0, WIDE)))
        value_grad = value_grad + dot_nn(p2_ref[:, lanes], slots_of(qd_all, parities[side], slice(WIDE, SLOT)))
    key_grad = jnp.where(low, key_grad[0:TOK], key_grad[TOK:SLOT])
    value_grad = jnp.where(low, value_grad[0:TOK], value_grad[TOK:SLOT])
    kv_grad = jnp.concatenate([key_grad, value_grad], axis=1)
    turned = jnp.concatenate([jnp.transpose(key_grad), jnp.transpose(value_grad)], axis=0).astype(BF16)
    kv_grad = kv_grad.astype(BF16)
    grads_turned = jnp.concatenate([turned, query_grad], axis=0)

    queries_turned = dot_nt(eye(WIDE, WIDE), queries)
    inner = jnp.sum(query_grad.astype(F32) * queries_turned, axis=0, keepdims=True)
    kv_inner = kv_grad.astype(F32) * kv.astype(F32)
    kv_hi = kv_inner.astype(BF16)
    kv_lo = (kv_inner - kv_hi.astype(F32)).astype(BF16)
    ones = jnp.ones((8, SLOT), BF16)
    kv_inner = dot_nt(ones, kv_hi) + dot_nt(ones, kv_lo)
    inner = inner + kv_inner[0:1]

    def partials(places):
        slots = []
        for by in places:
            j = z_at(by)
            at = (j // (2 * ys), lax.rem(j // 2, ys), lax.rem(j, 2))
            slots.append(jnp.concatenate([wkv_all[at], wqo_all[at + (slice(None), slice(0, WIDE))]], axis=1))
        value = dot_nn(jnp.concatenate(slots, axis=0), grads_turned)
        parts = [value[i * PAD : (i + 1) * PAD] for i in range(len(places))]
        return [jnp.where(row_at == FEAT, inner, part) for part in parts]

    some = pl.ds(0, zs - 1)
    for i in range(2):
        sent(streams[i].at[some], z_send.at[i])
        for group, sems, x_slots in ((weights[i], w_send, slice(0, ys)), (gathered[i], a_send, slice(0, 1))):
            if ys > 1:
                columns = slice(0, 1) if group is weights[i] else slice(0, 2)
                sent(group.at[columns, pl.ds(0, ys - 1), 0], sems.at[i, 0])
            sent(group.at[0, x_slots, 0], sems.at[i, 1])
            sent(group.at[:, :, 0], sems.at[i, 2])

    sent(st_all.at[pl.ds(0, rows - 1)], st_send)

    far = 2 * quarter

    def rs_leaf_copy(side, m):
        to = z_device(-1 if side else 1)
        return remote(rs_leaf_tx.at[side, m], rs_leaf.at[side, m], rs_send.at[side], rs_recv.at[side, 1, m], to)

    def rs_hub_copy(side, k):
        to = z_device(-2 if side else 2)
        return remote(rs_hub_tx.at[side, k], rs_hub.at[side, k], rs_send.at[side], rs_recv.at[side, 0, k], to)

    def leaf(side, m, part):
        rs_leaf_tx[side, m] = part.astype(BF16)
        rs_leaf_copy(side, m).start()

    hub_part, right_part, left_part = partials([far, far - 1, 1 - far])
    rs_hub_tx[0, 0] = hub_part.astype(BF16)
    rs_hub_copy(0, 0).start()
    leaf(0, 0, right_part)
    leaf(1, 0, left_part)
    for k in range(1, quarter):
        by = far - 2 * k
        to_right, to_left, right_part, left_part = partials([by, -by, by - 1, 1 - by])
        rs_hub_copy(0, k - 1).wait_recv()
        rs_leaf_copy(0, k - 1).wait_recv()
        total = to_right + rs_hub[0, k - 1].astype(F32) + rs_leaf[0, k - 1].astype(F32)
        rs_hub_tx[0, k] = total.astype(BF16)
        rs_hub_copy(0, k).start()
        rs_leaf_copy(1, k - 1).wait_recv()
        total = to_left + rs_leaf[1, k - 1].astype(F32)
        if k > 1:
            rs_hub_copy(1, k - 2).wait_recv()
            total = total + rs_hub[1, k - 2].astype(F32)
        rs_hub_tx[1, k - 1] = total.astype(BF16)
        rs_hub_copy(1, k - 1).start()
        leaf(0, k, right_part)
        leaf(1, k, left_part)

    own = partials([0])[0]
    for side in range(2):
        last = quarter - 1 - side
        rs_leaf_copy(side, quarter - 1).wait_recv()
        own = own + rs_leaf[side, quarter - 1].astype(F32)
        if last >= 0:
            rs_hub_copy(side, last).wait_recv()
            own = own + rs_hub[side, last].astype(F32)

    inner = own[FEAT : FEAT + 1] * (1.0 / (zs * FEAT))
    scaled = own * gain_own[...]
    normalized = xt_own[...] * scale_row
    raw = og_own[...] + scale_row * (scaled - normalized * inner)
    power = jnp.sum((raw * raw).reshape(PAD // 8, 8, TOK), axis=0)

    def power_stage(stage, landing, me, n, device):
        @pl.loop(0, n - 1)
        def _(m):
            k = (m + 1) // 2
            i = n // 2 + jnp.where(lax.rem(m, 2) == 0, k, -k)
            remote(pw_tx.at[stage], landing.at[me], p_send.at[stage], p_recv.at[stage], device(i)).start()

    def power_column(i):
        at = lax.rem(y * 2 + core + i, 2 * ys)
        return (d, lo * ys * 2 + at, c)

    def power_x(i):
        return plane_device(lax.rem(x + i, xs) * ys + y)

    stages = (
        (pw0, y * 2 + core, 2 * ys, power_column),
        (pw1, x, xs, power_x),
        (pw2, c, zs, lambda i: (d, r, lax.rem(c + i, zs))),
    )
    for stage, (landing, me, n, device) in enumerate(stages):
        pw_tx[stage] = power
        landing[me] = power
        power_stage(stage, landing, me, n, device)
        if stage == 0:
            sent(xt_all.at[pl.ds(0, far)], rs_send.at[0])
            sent(xt_all.at[pl.ds(0, far - 1)], rs_send.at[1])
        small_came(landing, n - 1, p_recv.at[stage])
        sent(landing.at[pl.ds(0, n - 1)], p_send.at[stage])
        power = jnp.sum(landing[...], axis=0)

    power = jnp.sum(power, axis=0, keepdims=True)
    power = jnp.sum(power, axis=1, keepdims=True)
    cells = depths * seq * zs * FEAT
    final = raw * lax.rsqrt(power * (1.0 / cells) + epsilon)
    out_ref[...] = final[0:FEAT].astype(BF16)


def sizes_of(mesh):
    depths, rows, zs = mesh.shape["depth"], mesh.shape["row"], mesh.shape["col"]
    los = 2
    return depths, los, rows // (2 * los), zs


def solution(mesh):
    depths, los, ys, zs = sizes_of(mesh)
    chips, planes = los * ys, depths * los * ys
    rows = chips * 2
    quarter = zs // 4
    dma = pltpu.SemaphoreType.DMA
    scratch = [
        *([pltpu.VMEM((FEAT, TOK), BF16)] * 6),
        pltpu.VMEM((FEAT,), BF16),
        pltpu.VMEM((zs, PAD, TOK), BF16),
        pltpu.VMEM((zs, PAD, TOK), BF16),
        pltpu.VMEM((los, ys, 2, PAD, SLOT), BF16),
        pltpu.VMEM((los, ys, 2, PAD, SLOT), BF16),
        pltpu.VMEM((los, ys, 2, TOK, SLOT), BF16),
        pltpu.VMEM((los, ys, 2, TOK, SLOT), BF16),
        pltpu.VMEM((rows, 8, SLOT), F32),
        pltpu.VMEM((PAD, TOK), F32),
        pltpu.VMEM((PAD, TOK), F32),
        pltpu.VMEM((PAD, TOK), F32),
        pltpu.VMEM((los, ys, 2, TOK, SLOT), F32),
        pltpu.VMEM((los, ys, 2, TOK, SLOT), F32),
        pltpu.VMEM((2, WIDE, chips * TOK), BF16),
        pltpu.VMEM((los, ys, 2, TOK, SLOT), BF16),
        pltpu.VMEM((rows // min(ys, 2), SLOT, min(ys, 2) * TOK), F32),
        pltpu.VMEM((rows // min(ys, 2), SLOT, min(ys, 2) * TOK), F32),
        pltpu.VMEM((SLOT, rows * TOK), BF16),
        pltpu.VMEM((SLOT, rows * TOK), BF16),
        *([pltpu.VMEM((2, quarter, PAD, TOK), BF16)] * 4),
        pltpu.VMEM((3, 8, TOK), F32),
        pltpu.VMEM((2 * ys, 8, TOK), F32),
        pltpu.VMEM((depths * los, 8, TOK), F32),
        pltpu.VMEM((zs, 8, TOK), F32),
        dma((7,)),
        dma((2,)), dma((2, 2, 2 * quarter)),
        dma((2, 3)), dma((2, ys + 1)), dma((2,)),
        dma((2, 3)), dma((2, los, ys)), dma((2,)),
        dma, dma,
        dma((2,)), dma((2, 2, quarter)),
        dma((3,)), dma((3,)),
    ]

    def shards(latents, out_grad, w_query, w_key, w_value, w_out, gain):
        return pl.pallas_call(
            functools.partial(kernel, (depths, los, ys, zs)),
            out_shape=jax.ShapeDtypeStruct((FEAT, TOK), BF16),
            in_specs=[pl.BlockSpec(memory_space=pl.ANY)] * 7,
            out_specs=pl.BlockSpec(memory_space=pltpu.VMEM),
            scratch_shapes=scratch,
            compiler_params=pltpu.CompilerParams(
                collective_id=0, has_side_effects=True, vmem_limit_bytes=56 * 1024 * 1024
            ),
        )(latents.T, out_grad.T, w_query, w_key, w_value, w_out, gain).T

    return jax.shard_map(
        shards,
        mesh=mesh,
        in_specs=(
            P(("depth", "row"), "col"),
            P(("depth", "row"), "col"),
            P("row", "col"),
            P("row", "col"),
            P("row", "col"),
            P("row", "col"),
            P("col"),
        ),
        out_specs=P(("depth", "row"), "col"),
        check_vma=False,
    )
```
